256 devices in a mesh: dp: 4 (over x_hi, core), fsdp: 64 (over y, z, x_lo).
Axes of the slice: x: 4 (x_hi: 2, x_lo: 2; x = x_hi * 2 + x_lo), y: 4, z: 8, core: 2. Of those that a mesh axis runs over, the one named last changes fastest.
Arguments:
- gen_input: bfloat16 [32768, 2560], P(('dp', 'fsdp')), may hold values from -10 to 10
- noise: bfloat16 [32768, 2560], P(('dp', 'fsdp')), may hold values from -6 to 6
- dmd_step: int32 [2], replicated, may hold values from 20 to 980
- scale_group: int32 [3, 2], replicated, may hold values from 0 to 7
- gen_codes: bfloat16 [2560, 2560], P('fsdp', 'dp'), may hold values from -0.125 to 0.125
- teacher_codes: bfloat16 [2560, 2560], P('fsdp', 'dp'), may hold values from -0.125 to 0.125
- critic_codes: bfloat16 [2560, 2560], P('fsdp', 'dp'), may hold values from -0.125 to 0.125
- code_scales: float32 [3, 8, 2560], P(None, None, 'dp'), may hold values from 0.5 to 2
- modulation: float32 [3, 3, 2560], replicated, may hold values from -3 to 3
- time_proj: bfloat16 [2, 256, 7680], replicated, may hold values from -0.375 to 0.375
Outputs:
- sample: bfloat16 [32768, 2560], P(('dp', 'fsdp'))
- dmd_grad: bfloat16 [32768, 2560], P(('dp', 'fsdp'))
- weight_grad: float32 [2560, 2560], P('fsdp', 'dp')
The draws below stay inside these ranges and needn't reach their ends.
All inputs are finite; a program needn't handle non-finite values.
Results may differ from the reference program's by a relative error of at most 0.012.
Values may be sent and summed in bfloat16 or wider, within the bound.
A program may use at most 128 MiB of HBM per device.

```python
import math
import jax
import jax.numpy as jnp
from jax import lax

D = 2560
FREQ = 128
G = 8
CLIPS = 2
TOKENS = 32768
SEQ = 16384


def draw_gen_input(key, part):
    key = jax.random.fold_in(key, 11)
    first_key = jax.random.fold_in(key, 0)
    place = (jnp.arange(TOKENS, dtype=jnp.int32) % SEQ).astype(jnp.float32) / SEQ
    ramp = (0.5 + place)[:, None]
    values = jax.random.normal(first_key, (TOKENS, D), jnp.float32) * ramp
    return jnp.clip(values, -10.0, 10.0).astype(jnp.bfloat16)


def with_ends(entries, own_key, low, largest):
    longest = entries.shape.index(max(entries.shape))
    spots = []
    for shift in (0, 1):
        where = [jax.random.randint(jax.random.fold_in(own_key, axis), (), 0, length) for axis, length in enumerate(entries.shape)]
        where[longest] = (where[longest] + shift) % entries.shape[longest]
        spots.append(tuple(where))
    return entries.at[spots[0]].set(low).at[spots[1]].set(largest)


def block_levels(key, extent, cuts, smallest, high):
    def one(dim, parts):
        heights = jax.random.uniform(jax.random.fold_in(jax.random.fold_in(key, 6), dim), (parts,), jnp.float32, smallest / len(cuts), high / len(cuts))
        return jnp.repeat(jnp.exp(heights), extent[dim] // parts).reshape((-1,) + (1,) * (len(extent) - dim - 1))

    level = one(*cuts[0])
    for cut in cuts[1:]:
        level = level * one(*cut)
    return level


def centred(rng, shape, width, limit, cuts=(), held_as=jnp.bfloat16):
    drawn = width * jax.random.normal(rng, shape, jnp.float32)
    if cuts:
        drawn = drawn * block_levels(rng, shape, cuts, -0.22, 0.18)
    return jnp.clip(drawn, -limit, limit).astype(held_as)


def setup_inputs(seed: int = 0) -> dict:
    key_of = jax.random.split(jax.random.key(seed), 11)
    return {
        "gen_input": draw_gen_input(jax.random.fold_in(key_of[10], 71), 0),
        "noise": centred(key_of[1], (TOKENS, D), 1.0, 6.0, ((0, 256),)),
        "dmd_step": jax.random.randint(key_of[2], (CLIPS,), 20, 981).astype(jnp.int32),
        "scale_group": with_ends(jax.random.randint(key_of[3], (3, CLIPS), 0, G), jax.random.fold_in(key_of[3], 1), 0, G - 1).astype(jnp.int32),
        "gen_codes": centred(key_of[4], (D, D), D ** -0.5, 0.125, ((0, 64), (1, 4))),
        "teacher_codes": centred(key_of[5], (D, D), D ** -0.5, 0.125, ((0, 64), (1, 4))),
        "critic_codes": centred(key_of[6], (D, D), D ** -0.5, 0.125, ((0, 64), (1, 4))),
        "code_scales": jnp.clip(jnp.exp(math.log(2.0) - 1.3862944 * jax.random.uniform(key_of[7], (3, G, D), jnp.float32) ** block_levels(key_of[7], (3, G, D), ((2, 4),), -0.2, 0.2)), 0.5, 2.0),
        "modulation": centred(key_of[8], (3, 3, D), 0.5, 3.0, (), jnp.float32),
        "time_proj": centred(key_of[9], (2, 2 * FREQ, 3 * D), (2 * FREQ) ** -0.5, 0.375),
    }


RMS_EPS = 1e-06
SPREAD_EPS = 1e-05

def normalize(values):
    return values * lax.rsqrt(lax.optimization_barrier(jnp.mean(values * values, axis=-1, keepdims=True)) + RMS_EPS)

def time_features(timesteps, freq_count):
    freq_index = jnp.arange(freq_count, dtype=jnp.float32)
    frequency = jnp.exp(freq_index * (-math.log(10000.0) / freq_count))
    phase_angle = timesteps.astype(jnp.float32)[:, None] * frequency[None, :]
    return jnp.concatenate([jnp.cos(phase_angle), jnp.sin(phase_angle)], axis=1)

def judge_modulations(dmd_step, modulation, time_proj):
    features = time_features(dmd_step, time_proj.shape[1] // 2)
    lifted = jnp.einsum('cf,mfe->mce', features, time_proj.astype(jnp.float32), precision=lax.Precision.HIGHEST)
    return modulation[1:, None] + lifted.reshape(2, dmd_step.shape[0], 3, modulation.shape[2])

def reference(gen_input, noise, dmd_step, scale_group, gen_codes, teacher_codes, critic_codes, code_scales, modulation, time_proj):
    judge_mod = judge_modulations(dmd_step, modulation, time_proj)
    gen_mod = modulation[0]
    noise_levels = dmd_step.astype(jnp.float32) / 1000.0
    scale_pick = jnp.stack([code_scales[model_index][scale_group[model_index]] for model_index in range(3)])
    inputs = gen_input.reshape(CLIPS, SEQ, D)
    noises = noise.reshape(CLIPS, SEQ, D)

    def one_clip(grad_total, clip_index):
        latent = lax.dynamic_index_in_dim(inputs, clip_index, keepdims=False).astype(jnp.float32)
        clip_noise = lax.dynamic_index_in_dim(noises, clip_index, keepdims=False).astype(jnp.float32)
        gen_factor = gen_mod[2] * scale_pick[0, clip_index]
        gen_hat = (normalize(latent) * (1.0 + gen_mod[1]) + gen_mod[0]).astype(jnp.bfloat16)
        gen_branch = (jnp.dot(gen_hat, gen_codes, preferred_element_type=jnp.float32) * gen_factor).astype(jnp.bfloat16)
        clean_est = latent + gen_branch.astype(jnp.float32)
        noise_level = noise_levels[clip_index]
        noisy_latent = (1.0 - noise_level) * clean_est + noise_level * clip_noise
        normed = normalize(noisy_latent).astype(jnp.bfloat16)
        branches = []
        for judge_index, judge_codes in enumerate((teacher_codes, critic_codes)):
            judge_row = judge_mod[judge_index, clip_index]
            judge_hat = (normed.astype(jnp.float32) * (1.0 + judge_row[1]) + judge_row[0]).astype(jnp.bfloat16)
            judge_factor = judge_row[2] * scale_pick[judge_index + 1, clip_index]
            product = jnp.dot(judge_hat, judge_codes, preferred_element_type=jnp.float32)
            branches.append((product * judge_factor).astype(jnp.bfloat16).astype(jnp.float32))
        real_branch, fake_branch = branches
        real_clean = noisy_latent - noise_level * (noisy_latent + real_branch)
        spread = jnp.sum(jnp.abs(clean_est - real_clean)) / (SEQ * D) + SPREAD_EPS
        score_gap = noise_level * (real_branch - fake_branch) / spread
        cotangent = (score_gap * gen_factor).astype(jnp.bfloat16)
        grad_total = grad_total + jnp.dot(gen_hat.T, cotangent, preferred_element_type=jnp.float32)
        return (grad_total, (clean_est.astype(jnp.bfloat16), score_gap.astype(jnp.bfloat16)))
    grad_total, outputs = lax.scan(one_clip, jnp.zeros((D, D), jnp.float32), jnp.arange(CLIPS, dtype=jnp.int32))
    samples, dmd_grads = outputs
    return (samples.reshape(TOKENS, D), dmd_grads.reshape(TOKENS, D), grad_total / TOKENS)
```

```python
import math

import jax
import jax.numpy as jnp
from jax import lax
from jax.experimental import pallas as pl
from jax.experimental.pallas import tpu as pltpu
from jax.sharding import PartitionSpec as P

RMS_EPS = 1e-06
SPREAD_EPS = 1e-05
F32 = jnp.float32
BF16 = jnp.bfloat16
MESH_ID = pl.DeviceIdType.MESH

NY, NZ = 4, 8
D = 2560
COLS = 640
ROWS = 128
GROUP = 4 * ROWS
HALF = 40
PAD = 48
BLK = 80
CA = 256
CB = COLS - CA
CUT = 48
TOKENS = 32768
CLIP_ELEMENTS = 16384 * 2560
TPC = 640
PIECES = 9


def time_features(timesteps, freq_count):
    freq_index = jnp.arange(freq_count, dtype=F32)
    frequency = jnp.exp(freq_index * (-math.log(10000.0) / freq_count))
    phase_angle = timesteps.astype(F32)[:, None] * frequency[None, :]
    return jnp.concatenate([jnp.cos(phase_angle), jnp.sin(phase_angle)], axis=1)


def scratch_table():
    vmem, dma = pltpu.VMEM, pltpu.SemaphoreType.DMA
    return {
        "W": vmem((3, NY, NZ, BLK, COLS), BF16),
        "XO": vmem((3, PAD, COLS), BF16),
        "XS": vmem((3, 2, PAD, COLS), BF16),
        "XG": vmem((4, ROWS, D), BF16),
        "H": vmem((4, GROUP, COLS), BF16),
        "NS": vmem((4, ROWS, COLS), BF16),
        "CL": vmem((GROUP, COLS), F32),
        "NF": vmem((GROUP, COLS), F32),
        "NG": vmem((4, GROUP, COLS), BF16),
        "JH": vmem((2, 4, GROUP, COLS), BF16),
        "ACC": vmem((GROUP, COLS), F32),
        "RP": vmem((GROUP, COLS), BF16),
        "GP": vmem((GROUP, COLS), F32),
        "CT": vmem((GROUP, COLS), BF16),
        "SB": vmem((GROUP, COLS), BF16),
        "DB": vmem((GROUP, COLS), BF16),
        "G": vmem((NY, NZ, BLK, COLS), F32),
        "ZS": vmem((2, 4, NY, BLK, CA), BF16),
        "ZR": vmem((2, 4, NY, BLK, CA), BF16),
        "YS": vmem((2, 2, NZ, BLK, CB), BF16),
        "YR": vmem((2, 2, NZ, BLK, CB), BF16),
        "ys": vmem((2, 2, BLK, CA), BF16),
        "yr": vmem((2, 2, BLK, CA), BF16),
        "zs": vmem((2, 4, BLK, CB), BF16),
        "zr": vmem((2, 4, BLK, CB), BF16),
        "SC": vmem((3, 8, COLS), F32),
        "PK": vmem((8, COLS), F32),
        "TP": vmem((2, 2 * ROWS, TPC), BF16),
        "JM": vmem((2, 2, 4, 1, COLS), F32),
        "SP": vmem((8, 128), F32),
        "SV": vmem((8, 128), F32),
        "SPG": vmem((4, 8, 128), F32),
        "SPZ": vmem((NZ, 8, 128), F32),
        "SPY": vmem((NY, 8, 128), F32),
        "GF": vmem((2, HALF, COLS), F32),
        "OW": vmem((2, HALF, COLS), F32),
        "ag_s": dma((3, 24)),
        "ag_r": dma((3, 24)),
        "x_s": dma((3, 2)),
        "x_r": dma((3, 2)),
        "tk_s": dma((4,)),
        "tk_r": dma((4,)),
        "ns_s": dma((4,)),
        "ns_r": dma((4,)),
        "ng_s": dma((2, 3)),
        "ng_r": dma((2, 3)),
        "sm_s": dma((4,)),
        "sm_r": dma((4,)),
        "dm_s": dma((4,)),
        "dm_r": dma((4,)),
        "sc_s": dma((1,)),
        "sc_r": dma((1,)),
        "tp_m": dma((2,)),
        "sg_s": dma((4,)),
        "sg_r": dma((4,)),
        "sz_s": dma((NZ,)),
        "sz_r": dma((NZ,)),
        "sy_s": dma((NY,)),
        "sy_r": dma((NY,)),
        "rs_s": dma((24,)),
        "rs_r": dma((24,)),
        "ow_s": dma((2,)),
        "ow_r": dma((2,)),
    }


NAMES = tuple(scratch_table())


def kernel(gi, noise, dstep, sgroup, wg, wt, wc, scales, mod, feats, tproj, out_s, out_d, out_w, *rest):
    S = dict(zip(NAMES, rest))
    dp, fs = lax.axis_index("dp"), lax.axis_index("fsdp")
    h, c = dp // 2, dp % 2
    l, plane = fs % 2, fs // 2
    y, z = plane // NZ, plane % NZ
    oh, oc, ol = 1 - h, 1 - c, 1 - l
    q = 2 * l + c
    cb = 2 * ((h + l) % 2) + c

    def dev(h_, c_, y_, z_, l_):
        return (2 * h_ + c_, (y_ * NZ + z_) * 2 + l_)

    def yy(step):
        return (y + step + NY) % NY

    def zz(step):
        return (z + step + NZ) % NZ

    started = []

    def remote(src, dst, ss, rs, target):
        return pltpu.make_async_remote_copy(
            src_ref=src, dst_ref=dst, send_sem=ss, recv_sem=rs, device_id=target, device_id_type=MESH_ID
        )

    def send(src, dst, ss, rs, target):
        copy = remote(src, dst, ss, rs, target)
        copy.start()
        started.append(copy)

    def arrived(dst, ss, rs):
        remote(dst, dst, ss, rs, dev(h, oc, y, z, l)).wait_recv()

    greeted = [dev(h, oc, y, z, l), dev(h, oc, y, z, ol)]
    greeted += [dev(h, c, y, z, ol), dev(oh, c, y, z, l), dev(oh, c, y, z, ol)]
    greeted += [dev(h, c, yy(j), z, l) for j in range(1, NY)]
    greeted += [dev(h, c, y, zz(j), l) for j in range(1, NZ)]
    barrier = pltpu.get_barrier_semaphore()
    for target in greeted:
        pl.semaphore_signal(barrier, inc=1, device_id=target, device_id_type=MESH_ID)
    pl.semaphore_wait(barrier, len(greeted))

    def ag_regions(m, chain, step, way):
        W, s = S["W"], 1 if way == 0 else -1
        if chain == 0:
            lanes = pl.ds(0, CA)
            if step == 0:
                return W.at[m, y, z, :, lanes], W.at[m, yy(-s), z, :, lanes], dev(h, c, yy(s), z, l)
            if step == 1:
                part = pl.ds(way * (CA // 2), CA // 2)
                return W.at[m, yy(-s), z, :, part], W.at[m, yy(2), z, :, part], dev(h, c, yy(s), z, l)
            k = step - 1
            some = pl.ds(0, NY) if k < 4 else pl.ds(way * 2, 2)
            return W.at[m, some, zz(-s * (k - 1)), :, lanes], W.at[m, some, zz(-s * k), :, lanes], dev(h, c, y, zz(s), l)
        lanes = pl.ds(CA, CB)
        if step < 4:
            k = step + 1
            some = pl.ds(0, BLK) if k < 4 else (pl.ds(0, CUT), pl.ds(CUT, BLK - CUT))[way]
            return W.at[m, y, zz(-s * (k - 1)), some, lanes], W.at[m, y, zz(-s * k), some, lanes], dev(h, c, y, zz(s), l)
        if step == 4:
            return W.at[m, y, :, :, lanes], W.at[m, yy(-s), :, :, lanes], dev(h, c, yy(s), z, l)
        some = pl.ds(way * 4, 4)
        return W.at[m, yy(-s), some, :, lanes], W.at[m, yy(2), some, :, lanes], dev(h, c, yy(s), z, l)

    def ag_start(m, chain, step):
        for way in range(2):
            src, _, target = ag_regions(m, chain, step, way)
            i = (chain * 6 + step) * 2 + way
            send(src, src, S["ag_s"].at[m, i], S["ag_r"].at[m, i], target)

    def ag_wait(m, chain, step):
        for way in range(2):
            _, dst, _ = ag_regions(m, chain, step, way)
            i = (chain * 6 + step) * 2 + way
            arrived(dst, S["ag_s"].at[m, i], S["ag_r"].at[m, i])

    XO, XS = S["XO"], S["XS"]

    def x_second(m):
        return remote(XO.at[m], XS.at[m, 1], S["x_s"].at[m, 1], S["x_r"].at[m, 1], dev(h, c, y, z, 0))

    def x_first(m, slot):
        return remote(XO.at[m], XS.at[m, slot], S["x_s"].at[m, 0], S["x_r"].at[m, slot], dev(oh, c, y, z, 1))

    for m, codes in enumerate((wg, wt, wc)):
        own = codes[...].astype(F32)
        own = jnp.concatenate([own, jnp.zeros((PAD - HALF, COLS), F32)], axis=0).astype(BF16)
        XO[m] = own

        @pl.when(l == 0)
        def _():
            XS[m, 0] = own
            x_first(m, 0).start()

        @pl.when(l == 1)
        def _():
            x_second(m).start()
            x_first(m, 1).start()

    def assemble(m):
        @pl.when(l == 1)
        def _():
            arrived(XS.at[m, 0], S["x_s"].at[m, 0], S["x_r"].at[m, 0])

        arrived(XS.at[m, 1], S["x_s"].at[m, 1], S["x_r"].at[m, 1])
        both = [XS[m, i].astype(F32)[:HALF] for i in range(2)]
        S["W"][m, y, z] = jnp.concatenate(both, axis=0).astype(BF16)

    XG, NS, SC = S["XG"], S["NS"], S["SC"]
    send(gi, XG.at[q], S["tk_s"].at[0], S["tk_r"].at[0], dev(h, c, y, z, ol))
    send(gi, XG.at[q], S["tk_s"].at[1], S["tk_r"].at[1], dev(h, oc, y, z, l))
    tok_own = pltpu.make_async_copy(gi, XG.at[q], S["tk_s"].at[3])
    tok_own.start()

    def columns(c_, l_):
        return pl.ds(pl.multiple_of((2 * ((h + l_) % 2) + c_) * COLS, COLS), COLS)

    others = ((oc, l), (c, ol), (oc, ol))
    for i, (c_, l_) in enumerate(others):
        send(noise.at[:, columns(c_, l_)], NS.at[q], S["ns_s"].at[i], S["ns_r"].at[i], dev(h, c_, y, z, l_))
    noise_own = pltpu.make_async_copy(noise.at[:, columns(c, l)], NS.at[q], S["ns_s"].at[3])
    noise_own.start()

    def scale_copy():
        return remote(scales, SC, S["sc_s"].at[0], S["sc_r"].at[0], dev(oh, c, y, z, 1))

    def scale_own():
        return pltpu.make_async_copy(scales, SC, S["sc_r"].at[0])

    @pl.when(l == 0)
    def _():
        scale_copy().start()
        scale_own().start()

    def piece(i):
        m, j = i // PIECES, i % PIECES
        if j < 8:
            offset = j * COLS
        else:
            offset = pl.multiple_of(2 * D + cb * COLS, COLS)
        return pltpu.make_async_copy(tproj.at[m, :, pl.ds(offset, TPC)], S["TP"].at[i % 2], S["tp_m"].at[i % 2])

    piece(0).start()
    piece(1).start()

    def gen_hat(block):
        H = S["H"]

        def rows(r, carry):
            at = pl.ds(pl.multiple_of(r * 16, 16), 16)
            x = XG[block, at, :].astype(F32)
            inv = lax.rsqrt(jnp.sum(x * x, axis=1, keepdims=True) / D + RMS_EPS)
            hat = (x * inv * (1.0 + mod[0, 1:2, :]) + mod[0, 0:1, :]).astype(BF16)
            to = pl.ds(pl.multiple_of(block * ROWS + r * 16, 16), 16)
            for k in range(4):
                H[k, to, :] = hat[:, k * COLS : (k + 1) * COLS]
            return carry

        lax.fori_loop(0, ROWS // 16, rows, 0)

    def judge_mod():
        feature = jnp.where(h == 0, feats[0:1, :], feats[1:2, :])
        hi = feature.astype(BF16)
        rest1 = feature - hi.astype(F32)
        mid = rest1.astype(BF16)
        low = (rest1 - mid.astype(F32)).astype(BF16)
        row = lax.broadcasted_iota(jnp.int32, (16, 2 * ROWS), 0)
        spread_out = [jnp.broadcast_to(v.astype(F32), (16, 2 * ROWS)) for v in (hi, mid, low)]
        parts = jnp.where(row == 0, spread_out[0], jnp.where(row == 1, spread_out[1], jnp.where(row == 2, spread_out[2], 0.0)))
        parts = parts.astype(BF16)
        for i in range(2 * PIECES):
            m, j = i // PIECES, i % PIECES
            piece(i).wait()
            lifted = jnp.dot(parts, S["TP"][i % 2], preferred_element_type=F32)
            lifted = jnp.sum(lifted, axis=0, keepdims=True)
            if j < 8:
                S["JM"][m, j // 4, j % 4] = lifted + mod[m + 1, j // 4 : j // 4 + 1, (j % 4) * COLS : (j % 4 + 1) * COLS]
            else:
                gate = mod[m + 1, 2:3, pl.ds(pl.multiple_of(cb * COLS, COLS), COLS)]
                S["PK"][m + 4 : m + 5, :] = lifted + gate
            if i + 2 < 2 * PIECES:
                piece(i + 2).start()

    def factors():
        arrived(SC, S["sc_s"].at[0], S["sc_r"].at[0])
        row = lax.broadcasted_iota(jnp.int32, (8, COLS), 0)
        for m in range(3):
            picked = jnp.sum(jnp.where(row == sgroup[m, h], SC[m], 0.0), axis=0, keepdims=True)
            if m == 0:
                gate = mod[0, 2:3, pl.ds(pl.multiple_of(cb * COLS, COLS), COLS)]
            else:
                gate = S["PK"][m + 3 : m + 4, :]
            S["PK"][m : m + 1, :] = gate * picked

    def level():
        return jnp.full((1, COLS), dstep[h], jnp.int32).astype(F32) / 1000.0

    def product(lhs, m):
        ACC = S["ACC"]
        for k in range(4):
            part = jnp.dot(lhs[k], S["W"][m, k].reshape(COLS, COLS), preferred_element_type=F32)
            if k == 0:
                ACC[...] = part
            else:
                ACC[...] += part

    TILE = 64

    def clean_rows(half):
        lev = level()
        here = pl.ds(pl.multiple_of(cb * COLS, COLS), COLS)

        def rows(r, carry):
            at = pl.ds(pl.multiple_of(half * (GROUP // 2) + r * TILE, TILE), TILE)
            block = half * 2 + r // 2
            inner = pl.ds(pl.multiple_of((r % 2) * TILE, TILE), TILE)
            branch = (S["ACC"][at, :] * S["PK"][0:1, :]).astype(BF16)
            clean = XG[block, inner, here].astype(F32) + branch.astype(F32)
            noisy = (1.0 - lev) * clean + lev * NS[block, inner, :].astype(F32)
            S["CL"][at, :] = clean
            S["NF"][at, :] = noisy
            S["SB"][at, :] = clean.astype(BF16)
            S["NG"][cb, at, :] = noisy.astype(BF16)
            return carry

        lax.fori_loop(0, GROUP // 2 // TILE, rows, 0)

    def half_rows(half):
        return pl.ds(half * (GROUP // 2), GROUP // 2)

    def noisy_send(half):
        own = S["NG"].at[cb, half_rows(half)]
        send(own, own, S["ng_s"].at[half, 0], S["ng_r"].at[half, 0], dev(h, c, y, z, ol))
        send(own, own, S["ng_s"].at[half, 1], S["ng_r"].at[half, 1], dev(h, oc, y, z, l))

    far = 2 * ((h + ol) % 2) + c

    def noisy_forward(half):
        got = S["NG"].at[far, half_rows(half)]
        arrived(got, S["ng_s"].at[half, 0], S["ng_r"].at[half, 0])
        send(got, got, S["ng_s"].at[half, 2], S["ng_r"].at[half, 2], dev(h, oc, y, z, l))

    def noisy_wait(half):
        near = 2 * ((h + l) % 2) + oc
        last = 2 * ((h + ol) % 2) + oc
        arrived(S["NG"].at[near, half_rows(half)], S["ng_s"].at[half, 1], S["ng_r"].at[half, 1])
        arrived(S["NG"].at[last, half_rows(half)], S["ng_s"].at[half, 2], S["ng_r"].at[half, 2])

    def judge_hats(half):
        NG, JH, JM = S["NG"], S["JH"], S["JM"]

        def rows(r, carry):
            at = pl.ds(pl.multiple_of(half * (GROUP // 2) + r * 16, 16), 16)
            v = [NG[k, at, :].astype(F32) for k in range(4)]
            total = sum(jnp.sum(t * t, axis=1, keepdims=True) for t in v)
            inv = lax.rsqrt(total / D + RMS_EPS)
            for k in range(4):
                normed = (v[k] * inv).astype(BF16).astype(F32)
                for j in range(2):
                    JH[j, k, at, :] = (normed * (1.0 + JM[j, 1, k]) + JM[j, 0, k]).astype(BF16)
            return carry

        lax.fori_loop(0, GROUP // 2 // 16, rows, 0)

    def return_rows(buf, out, ss, rs):
        here = pl.ds(pl.multiple_of(cb * COLS, COLS), COLS)
        for i, (c_, l_) in enumerate(others):
            block = pl.ds(pl.multiple_of((2 * l_ + c_) * ROWS, ROWS), ROWS)
            send(buf.at[block], out.at[:, here], ss.at[i], rs.at[i], dev(h, c_, y, z, l_))
        block = pl.ds(pl.multiple_of(q * ROWS, ROWS), ROWS)
        own = pltpu.make_async_copy(buf.at[block], out.at[:, here], ss.at[3])
        own.start()
        return own

    def return_wait(out, ss, rs):
        for i, (c_, l_) in enumerate(others):
            arrived(out.at[:, columns(c_, l_)], ss.at[i], rs.at[i])

    def real_rows():
        def rows(r, carry):
            at = pl.ds(pl.multiple_of(r * TILE, TILE), TILE)
            S["RP"][at, :] = (S["ACC"][at, :] * S["PK"][1:2, :]).astype(BF16)
            return carry

        lax.fori_loop(0, GROUP // TILE, rows, 0)

    def spread_rows():
        lev = level()

        def rows(r, total):
            at = pl.ds(pl.multiple_of(r * TILE, TILE), TILE)
            noisy = S["NF"][at, :]
            gone = jnp.abs(S["CL"][at, :] - (noisy - lev * (noisy + S["RP"][at, :].astype(F32))))
            return total + jnp.sum(gone.reshape(TILE // 8, 8, COLS), axis=0)

        total = lax.fori_loop(0, GROUP // TILE, rows, jnp.zeros((8, COLS), F32))
        total = jnp.sum(jnp.sum(total, axis=1, keepdims=True), axis=0, keepdims=True)
        S["SP"][...] = jnp.broadcast_to(total, (8, 128))

    def gap_rows():
        lev = level()

        def rows(r, carry):
            at = pl.ds(pl.multiple_of(r * TILE, TILE), TILE)
            fake = (S["ACC"][at, :] * S["PK"][2:3, :]).astype(BF16).astype(F32)
            gap = lev * (S["RP"][at, :].astype(F32) - fake)
            S["GP"][at, :] = gap
            S["CT"][at, :] = (gap * S["PK"][0:1, :]).astype(BF16)
            return carry

        lax.fori_loop(0, GROUP // TILE, rows, 0)

    def spread_group_start():
        S["SPG"][q] = S["SP"][...]
        for i, (c_, l_) in enumerate(others):
            send(S["SP"], S["SPG"].at[q], S["sg_s"].at[i], S["sg_r"].at[i], dev(h, c_, y, z, l_))

    def spread_z_start():
        for i, (c_, l_) in enumerate(others):
            arrived(S["SPG"].at[2 * l_ + c_], S["sg_s"].at[i], S["sg_r"].at[i])
        SPG, SPZ = S["SPG"], S["SPZ"]
        SPZ[z] = (SPG[0] + SPG[1]) + (SPG[2] + SPG[3])
        for j in range(1, NZ):
            send(SPZ.at[z], SPZ.at[z], S["sz_s"].at[j], S["sz_r"].at[j], dev(h, c, y, zz(j), l))

    def spread_y_start():
        SPZ, SPY = S["SPZ"], S["SPY"]
        for j in range(1, NZ):
            arrived(SPZ.at[zz(-j)], S["sz_s"].at[j], S["sz_r"].at[j])
        total = SPZ[0]
        for j in range(1, NZ):
            total = total + SPZ[j]
        SPY[y] = total
        for j in range(1, NY):
            send(SPY.at[y], SPY.at[y], S["sy_s"].at[j], S["sy_r"].at[j], dev(h, c, yy(j), z, l))

    def spread_value():
        SPY = S["SPY"]
        for j in range(1, NY):
            arrived(SPY.at[yy(-j)], S["sy_s"].at[j], S["sy_r"].at[j])
        total = SPY[0]
        for j in range(1, NY):
            total = total + SPY[j]
        S["SV"][...] = total / CLIP_ELEMENTS + SPREAD_EPS

    def dmd_rows():
        def rows(r, carry):
            at = pl.ds(pl.multiple_of(r * TILE, TILE), TILE)
            S["DB"][at, :] = (S["GP"][at, :] / S["SV"][0:1, 0:1]).astype(BF16)
            return carry

        lax.fori_loop(0, GROUP // TILE, rows, 0)

    G = S["G"]

    def grad(k):
        block = lax.dot_general(S["H"][k], S["CT"][...], (((0,), (0,)), ((), ())), preferred_element_type=F32)
        G[k] = block.reshape(NZ, BLK, COLS)

    def rs_send(i, src, dst, target):
        send(src, dst, S["rs_s"].at[i], S["rs_r"].at[i], target)

    def rs_got(i, dst):
        arrived(dst, S["rs_s"].at[i], S["rs_r"].at[i])

    LB = pl.ds(CA, CB)
    LA = pl.ds(0, CA)

    def big_y(step):
        YS, YR = S["YS"], S["YR"]
        for way in range(2):
            s = 1 if way == 0 else -1
            some = pl.ds(way * 4, 4)
            if step == 0:
                for i in range(way * 4, way * 4 + 4):
                    YS[way, 0, i] = G[yy(2), i, :, LB].astype(BF16)
                rs_send(way, YS.at[way, 0, some], YR.at[way, 0, some], dev(h, c, yy(s), z, l))
            else:
                rs_got(way, YR.at[way, 0, some])
                for i in range(NZ):
                    v = G[yy(s), i, :, LB]
                    if way * 4 <= i < way * 4 + 4:
                        v = v + YR[way, 0, i].astype(F32)
                    YS[way, 1, i] = v.astype(BF16)
                rs_send(2 + way, YS.at[way, 1], YR.at[way, 1], dev(h, c, yy(s), z, l))

    def big_y_end():
        YR = S["YR"]
        for way in range(2):
            rs_got(2 + way, YR.at[way, 1])
        for i in range(NZ):
            G[y, i, :, LB] = G[y, i, :, LB] + YR[0, 1, i].astype(F32) + YR[1, 1, i].astype(F32)

    def big_z(k):
        ZS, ZR = S["ZS"], S["ZR"]
        for way in range(2):
            s = 1 if way == 0 else -1
            half = range(way * 2, way * 2 + 2)
            some = pl.ds(way * 2, 2)
            if k > 1:
                got = ZR.at[way, k - 2, some] if k == 2 else ZR.at[way, k - 2]
                rs_got(4 + 2 * (k - 2) + way, got)
            if k < 5:
                for i in half if k == 1 else range(NY):
                    v = G[i, zz(s * (5 - k)), :, LA]
                    if k > 2 or (k == 2 and i in half):
                        v = v + ZR[way, k - 2, i].astype(F32)
                    ZS[way, k - 1, i] = v.astype(BF16)
                src = ZS.at[way, k - 1, some] if k == 1 else ZS.at[way, k - 1]
                dst = ZR.at[way, k - 1, some] if k == 1 else ZR.at[way, k - 1]
                rs_send(4 + 2 * (k - 1) + way, src, dst, dev(h, c, y, zz(s), l))
        if k == 5:
            for i in range(NY):
                G[i, z, :, LA] = G[i, z, :, LA] + ZR[0, 3, i].astype(F32) + ZR[1, 3, i].astype(F32)

    def small_y(step):
        ys, yr = S["ys"], S["yr"]
        for way in range(2):
            s = 1 if way == 0 else -1
            part = pl.ds(way * (CA // 2), CA // 2)
            if step == 0:
                ys[way, 0, :, part] = G[yy(2), z, :, part].astype(BF16)
                rs_send(12 + way, ys.at[way, 0, :, part], yr.at[way, 0, :, part], dev(h, c, yy(s), z, l))
            elif step == 1:
                rs_got(12 + way, yr.at[way, 0, :, part])
                ys[way, 1] = G[yy(s), z, :, LA].astype(BF16)
                ys[way, 1, :, part] = (G[yy(s), z, :, part] + yr[way, 0, :, part].astype(F32)).astype(BF16)
                rs_send(14 + way, ys.at[way, 1], yr.at[way, 1], dev(h, c, yy(s), z, l))
            else:
                rs_got(14 + way, yr.at[way, 1])
        if step == 2:
            G[y, z, :, LA] = G[y, z, :, LA] + yr[0, 1].astype(F32) + yr[1, 1].astype(F32)

    def small_z(k):
        zs, zr = S["zs"], S["zr"]
        for way in range(2):
            s = 1 if way == 0 else -1
            some = (pl.ds(0, CUT), pl.ds(CUT, BLK - CUT))[way]
            if k > 1:
                got = zr.at[way, 0, some] if k == 2 else zr.at[way, k - 2]
                rs_got(16 + 2 * (k - 2) + way, got)
            if k == 1:
                zs[way, 0, some, :] = G[y, zz(4 * s), some, LB].astype(BF16)
                rs_send(16 + way, zs.at[way, 0, some], zr.at[way, 0, some], dev(h, c, y, zz(s), l))
            elif k < 5:
                v = G[y, zz(s * (5 - k)), :, LB]
                if k > 2:
                    zs[way, k - 1] = (v + zr[way, k - 2].astype(F32)).astype(BF16)
                else:
                    zs[way, 1] = v.astype(BF16)
                    zs[way, 1, some, :] = (G[y, zz(3 * s), some, LB] + zr[way, 0, some, :].astype(F32)).astype(BF16)
                rs_send(16 + 2 * (k - 1) + way, zs.at[way, k - 1], zr.at[way, k - 1], dev(h, c, y, zz(s), l))
        if k == 5:
            G[y, z, :, LB] = G[y, z, :, LB] + zr[0, 3].astype(F32) + zr[1, 3].astype(F32)

    for m in range(3):
        assemble(m)
        ag_start(m, 0, 0)
        ag_start(m, 1, 0)
    tok_own.wait()
    gen_hat(q)
    for m in range(3):
        ag_wait(m, 0, 0)
        ag_start(m, 0, 1)
        ag_wait(m, 1, 0)
        ag_start(m, 1, 1)
    q_far = 2 * ol + c
    arrived(XG.at[q_far], S["tk_s"].at[0], S["tk_r"].at[0])
    send(XG.at[q_far], XG.at[q_far], S["tk_s"].at[2], S["tk_r"].at[2], dev(h, oc, y, z, l))
    ag_wait(0, 0, 1)
    ag_start(0, 0, 2)
    ag_wait(0, 1, 1)
    ag_start(0, 1, 2)
    for m in (1, 2):
        ag_wait(m, 0, 1)
        ag_wait(m, 1, 1)
        ag_start(m, 1, 2)
    for m in range(3):
        ag_wait(m, 1, 2)
        ag_start(m, 1, 3)
    q_near = 2 * l + oc
    arrived(XG.at[q_near], S["tk_s"].at[1], S["tk_r"].at[1])
    gen_hat(q_near)
    ag_wait(0, 1, 3)
    ag_start(0, 1, 4)
    ag_wait(0, 0, 2)
    ag_start(0, 0, 3)
    ag_start(1, 0, 2)
    gen_hat(q_far)
    for m in (1, 2):
        ag_wait(m, 1, 3)
    ag_wait(0, 0, 3)
    ag_start(0, 0, 4)
    q_last = 2 * ol + oc
    arrived(XG.at[q_last], S["tk_s"].at[2], S["tk_r"].at[2])
    gen_hat(q_last)
    ag_start(1, 1, 4)
    ag_wait(1, 0, 2)
    ag_start(1, 0, 3)
    ag_wait(0, 0, 4)
    ag_start(0, 0, 5)
    ag_wait(0, 1, 4)
    ag_start(0, 1, 5)
    judge_mod()
    factors()
    ag_wait(1, 0, 3)
    ag_start(1, 0, 4)
    ag_start(2, 0, 2)
    ag_wait(0, 0, 5)
    ag_wait(0, 1, 5)
    ag_start(2, 1, 4)
    product(S["H"], 0)
    noise_own.wait()
    for i, (c_, l_) in enumerate(others):
        arrived(NS.at[2 * l_ + c_], S["ns_s"].at[i], S["ns_r"].at[i])
    for half in range(2):
        clean_rows(half)
        noisy_send(half)
    ag_wait(1, 0, 4)
    ag_start(1, 0, 5)
    ag_wait(2, 0, 2)
    ag_start(2, 0, 3)
    ag_wait(1, 1, 4)
    ag_start(1, 1, 5)
    noisy_forward(0)
    ag_wait(2, 0, 3)
    ag_start(2, 0, 4)
    noisy_forward(1)
    ag_wait(1, 0, 5)
    sample_own = return_rows(S["SB"], out_s, S["sm_s"], S["sm_r"])
    noisy_wait(0)
    judge_hats(0)
    ag_wait(2, 0, 4)
    ag_start(2, 0, 5)
    ag_wait(2, 1, 4)
    ag_start(2, 1, 5)
    noisy_wait(1)
    judge_hats(1)
    ag_wait(1, 1, 5)
    product(S["JH"].at[0], 1)
    real_rows()
    spread_rows()
    spread_group_start()
    ag_wait(2, 0, 5)
    ag_wait(2, 1, 5)
    product(S["JH"].at[1], 2)
    gap_rows()
    spread_z_start()
    grad(yy(2))
    big_y(0)
    grad(yy(1))
    grad(yy(-1))
    big_y(1)
    grad(y)
    spread_y_start()
    big_z(1)
    big_z(2)
    spread_value()
    dmd_rows()
    dmd_own = return_rows(S["DB"], out_d, S["dm_s"], S["dm_r"])
    big_z(3)
    big_z(4)
    big_y_end()
    small_z(1)
    big_z(5)
    small_y(0)
    small_z(2)
    small_y(1)
    small_z(3)
    small_y(2)
    small_z(4)
    small_z(5)
    GF, OW = S["GF"], S["OW"]
    done = G[y, z] / S["SV"][0:1, 0:1] / TOKENS

    def own_row(row, slot, target):
        return remote(GF.at[row], OW.at[slot], S["ow_s"].at[row], S["ow_r"].at[slot], target)

    for row in range(2):
        GF[row] = done[row * HALF : (row + 1) * HALF]

    @pl.when(l == 0)
    def _():
        OW[0] = GF[0]
        own_row(1, 0, dev(h, c, y, z, 1)).start()

    @pl.when(l == 1)
    def _():
        own_row(0, 1, dev(oh, c, y, z, 0)).start()
        own_row(1, 1, dev(oh, c, y, z, 1)).start()
        arrived(OW.at[0], S["ow_s"].at[0], S["ow_r"].at[0])

    arrived(OW.at[1], S["ow_s"].at[1], S["ow_r"].at[1])
    out_w[...] = OW[0] + OW[1]

    return_wait(out_s, S["sm_s"], S["sm_r"])
    return_wait(out_d, S["dm_s"], S["dm_r"])
    sample_own.wait()
    dmd_own.wait()
    for copy in started:
        copy.wait_send()
    for m in range(3):
        x_first(m, 0).wait_send()

    @pl.when(l == 0)
    def _():
        scale_copy().wait_send()
        own_row(1, 0, dev(h, c, y, z, 1)).wait_send()

    @pl.when(l == 1)
    def _():
        for m in range(3):
            x_second(m).wait_send()
        own_row(0, 1, dev(oh, c, y, z, 0)).wait_send()
        own_row(1, 1, dev(oh, c, y, z, 1)).wait_send()


def on_device(gi, noise, dmd_step, scale_group, wg, wt, wc, scales, mod, tproj):
    feats = time_features(dmd_step, tproj.shape[1] // 2)
    vmem = pl.BlockSpec(memory_space=pltpu.VMEM)
    smem = pl.BlockSpec(memory_space=pltpu.SMEM)
    hbm = pl.BlockSpec(memory_space=pl.ANY)
    return pl.pallas_call(
        kernel,
        out_shape=(
            jax.ShapeDtypeStruct((ROWS, D), BF16),
            jax.ShapeDtypeStruct((ROWS, D), BF16),
            jax.ShapeDtypeStruct((HALF, COLS), F32),
        ),
        in_specs=[hbm, hbm, smem, smem, vmem, vmem, vmem, hbm, vmem, vmem, hbm],
        out_specs=(hbm, hbm, vmem),
        scratch_shapes=list(scratch_table().values()),
        compiler_params=pltpu.CompilerParams(
            collective_id=0, has_side_effects=True, vmem_limit_bytes=64 * 1024 * 1024 - 65536
        ),
    )(gi, noise, dmd_step, scale_group, wg, wt, wc, scales, mod, feats, tproj)


def solution(mesh):
    return jax.shard_map(
        on_device,
        mesh=mesh,
        in_specs=(
            P(("dp", "fsdp"), None),
            P(("dp", "fsdp"), None),
            P(),
            P(),
            P("fsdp", "dp"),
            P("fsdp", "dp"),
            P("fsdp", "dp"),
            P(None, None, "dp"),
            P(),
            P(),
        ),
        out_specs=(P(("dp", "fsdp"), None), P(("dp", "fsdp"), None), P("fsdp", "dp")),
        check_vma=False,
    )
```

```python
import functools
import math
import types

import jax
import jax.numpy as jnp
from jax import lax
from jax.experimental import pallas as pl
from jax.experimental.pallas import tpu as pltpu
from jax.sharding import PartitionSpec as P

RMS_EPS = 1e-06
SPREAD_EPS = 1e-05
F32 = jnp.float32
BF16 = jnp.bfloat16
MESH_ID = pl.DeviceIdType.MESH

NY, NZ = 4, 8
D = 2560
COLS = 640
ROWS = 128
GROUP = 4 * ROWS
HALF = 40
PAD = 48
BLK = 80
CA = 256
CB = COLS - CA
CUT = 48
TOKENS = 32768
CLIP_ELEMENTS = 16384 * 2560
TPC = 640
PIECES = 9
SLOTS = 4
AY, AZ, BZ, BY, FY = range(5)


def scratch_table():
    vmem, dma = pltpu.VMEM, pltpu.SemaphoreType.DMA
    return dict(
        W=vmem((3, NY, NZ, BLK, COLS), BF16),
        XO=vmem((3, PAD, COLS), BF16),
        XS=vmem((3, 2, PAD, COLS), BF16),
        XG=vmem((4, ROWS, D), BF16),
        H=vmem((4, GROUP, COLS), BF16),
        NS=vmem((4, ROWS, COLS), BF16),
        CL=vmem((GROUP, COLS), F32),
        NF=vmem((GROUP, COLS), F32),
        NG=vmem((4, GROUP, COLS), BF16),
        JH=vmem((2, 4, GROUP, COLS), BF16),
        ACC=vmem((GROUP, COLS), F32),
        RP=vmem((GROUP, COLS), BF16),
        GP=vmem((GROUP, COLS), F32),
        CT=vmem((GROUP, COLS), BF16),
        SB=vmem((GROUP, COLS), BF16),
        DB=vmem((GROUP, COLS), BF16),
        G=vmem((NY, NZ, BLK, COLS), F32),
        ZS=vmem((8, NY, BLK, CA), BF16),
        ZR=vmem((8, NY, BLK, CA), BF16),
        Y0S=vmem((NZ, BLK, CB), BF16),
        Y0R=vmem((NZ, BLK, CB), BF16),
        Y1S=vmem((NZ, 2, BLK, CB), BF16),
        Y1R=vmem((NZ, 2, BLK, CB), BF16),
        ys=vmem((4, BLK, CA), BF16),
        yr=vmem((4, BLK, CA), BF16),
        zs=vmem((8, BLK, CB), BF16),
        zr=vmem((8, BLK, CB), BF16),
        SC=vmem((3, 8, COLS), F32),
        PK=vmem((8, COLS), F32),
        TP=vmem((SLOTS, 2 * ROWS, TPC), BF16),
        FT=vmem((16, 2 * ROWS), BF16),
        JM=vmem((2, 2, 4, 1, COLS), F32),
        SP=vmem((8, 128), F32),
        SV=vmem((8, 128), F32),
        SPG=vmem((4, 8, 128), F32),
        SPZ=vmem((NZ, 8, 128), F32),
        SPY=vmem((NY, 8, 128), F32),
        GF=vmem((2, HALF, COLS), F32),
        OW=vmem((2, HALF, COLS), F32),
        ag_s=dma((3, 4)),
        ag_r=dma((3, 18)),
        fy_r=dma((16,)),
        x_s=dma((3, 2)),
        x_r=dma((3, 2)),
        tk_s=dma((4,)),
        tk_r=dma((4,)),
        ns_s=dma((4,)),
        ns_r=dma((4,)),
        ng_s=dma((4, 3)),
        ng_r=dma((4, 3)),
        sm_s=dma((4,)),
        sm_r=dma((4,)),
        dm_s=dma((4,)),
        dm_r=dma((4,)),
        sc_s=dma((1,)),
        sc_r=dma((1,)),
        tp_m=dma((SLOTS,)),
        sg_s=dma((4,)),
        sg_r=dma((4,)),
        sz_s=dma((NZ,)),
        sz_r=dma((NZ,)),
        sy_s=dma((NY,)),
        sy_r=dma((NY,)),
        rs_s=dma((5,)),
        b0_r=dma((NZ,)),
        b1_r=dma((NZ,)),
        a_r=dma((4, NY)),
        y_r=dma((2,)),
        z_r=dma((4,)),
        ow_s=dma((2,)),
        ow_r=dma((2,)),
    )


NAMES = tuple(scratch_table())


def kernel(gi, noise, dstep, sgroup, wg, wt, wc, scales, mod, tproj, out_s, out_d, out_w, *rest):
    S = types.SimpleNamespace(**dict(zip(NAMES, rest)))
    dp, fs = lax.axis_index("dp"), lax.axis_index("fsdp")
    h, c = dp // 2, dp % 2
    l, plane = fs % 2, fs // 2
    y, z = plane // NZ, plane % NZ
    oh, oc, ol = 1 - h, 1 - c, 1 - l
    q = 2 * l + c
    cb = 2 * ((h + l) % 2) + c

    def dev(h_, c_, y_, z_, l_):
        return (2 * h_ + c_, (y_ * NZ + z_) * 2 + l_)

    def yy(step):
        return (y + step + NY) % NY

    def zz(step):
        return (z + step + NZ) % NZ

    started = []

    def remote(src, dst, ss, rs, target):
        return pltpu.make_async_remote_copy(
            src_ref=src, dst_ref=dst, send_sem=ss, recv_sem=rs, device_id=target, device_id_type=MESH_ID
        )

    def send(src, dst, ss, rs, target):
        copy = remote(src, dst, ss, rs, target)
        copy.start()
        started.append(copy)

    def drain():
        for copy in started:
            copy.wait_send()
        started.clear()

    def arrived(dst, ss, rs):
        remote(dst, dst, ss, rs, dev(h, oc, y, z, l)).wait_recv()

    greeted = [dev(h, oc, y, z, l), dev(h, oc, y, z, ol)]
    greeted += [dev(h, c, y, z, ol), dev(oh, c, y, z, l), dev(oh, c, y, z, ol)]
    greeted += [dev(h, c, yy(j), z, l) for j in range(1, NY)]
    greeted += [dev(h, c, y, zz(j), l) for j in range(1, NZ)]
    barrier = pltpu.get_barrier_semaphore()
    for target in greeted:
        pl.semaphore_signal(barrier, inc=1, device_id=target, device_id_type=MESH_ID)

    LA, LB = pl.ds(0, CA), pl.ds(CA, CB)
    Z_ORDER = (4, 3, 5, 2, 6, 1, 7, 0)
    Y_ORDER = (2, 1, -1, 0)
    way_of = {r: i % 2 for i, r in enumerate(Z_ORDER)}

    def ag_copies(m, op, k, i):
        W = S.W
        for way in range(2):
            s = 1 - 2 * way
            if op == AY:
                if k == 1:
                    yield W.at[m, y, z, :, LA], W.at[m, yy(-s), z, :, LA], way
                else:
                    part = pl.ds(way * (CA // 2), CA // 2)
                    yield W.at[m, yy(-s), z, :, part], W.at[m, yy(2), z, :, part], way
            elif op == AZ:
                if k < 4 or way == i:
                    some = pl.ds(2 * i, 2)
                    yield W.at[m, some, zz(-s * (k - 1)), :, LA], W.at[m, some, zz(-s * k), :, LA], way
            elif op == BZ:
                some = pl.ds(0, BLK) if k < 4 else (pl.ds(0, CUT), pl.ds(CUT, BLK - CUT))[way]
                yield W.at[m, y, zz(-s * (k - 1)), some, LB], W.at[m, y, zz(-s * k), some, LB], way
            else:
                some = pl.ds(4 * i, 4) if op == BY else zz(i)
                if k == 1:
                    yield W.at[m, y, some, :, LB], W.at[m, yy(-s), some, :, LB], way
                elif way == (i if op == BY else way_of[i]):
                    yield W.at[m, yy(-s), some, :, LB], W.at[m, yy(2), some, :, LB], way

    def ag_sems(m, op, k, i):
        n = {AY: k - 1, AZ: 2 + (k - 1) * 2 + i, BZ: 9 + k, BY: 12 + 2 * k + i, FY: 18 + 8 * (k - 1) + i}[op]
        group = {AY: 0, AZ: 1, BZ: 2, BY: 3, FY: 3}[op]
        return S.ag_s.at[m, group], S.fy_r.at[n - 18] if op == FY else S.ag_r.at[m, n]

    def ag_go(m, op, k, i=0):
        ss, rs = ag_sems(m, op, k, i)
        for src, _, way in ag_copies(m, op, k, i):
            s = 1 - 2 * way
            target = dev(h, c, y, zz(s), l) if op in (AZ, BZ) else dev(h, c, yy(s), z, l)
            remote(src, src, ss, rs, target).start()

    def ag_got(m, op, k, i=0):
        W = S.W
        ss, rs = ag_sems(m, op, k, i)
        if op == AY:
            both = W.at[m, 0:2, z, :, LA] if k == 1 else W.at[m, 0, z, :, LA]
        elif op == AZ:
            both = W.at[m, :, z, :, LA] if k < 4 else W.at[m, 0:2, z, :, LA]
        elif op == BZ:
            both = W.at[m, 0, 0:2, :, LB] if k < 4 else W.at[m, 0, 0, :, LB]
        elif op == BY:
            both = W.at[m, 0, :, :, LB] if k == 1 else W.at[m, 0, 0:4, :, LB]
        else:
            both = W.at[m, 0, 0:2, :, LB] if k == 1 else W.at[m, 0, 0, :, LB]
        arrived(both, ss, rs)

    def ag_sent(m):
        W = S.W
        for group, whole in enumerate(
            (W.at[m, 0:3, 0, :, LA], W.at[m, :, 0:7, :, LA], W.at[m, 0, 0:7, :, LB], W.at[m, 0:3, :, :, LB])
        ):
            remote(whole, whole, S.ag_s.at[m, group], S.ag_r.at[m, 0], dev(h, oc, y, z, l)).wait_send()

    XO, XS = S.XO, S.XS

    def x_second(m):
        return remote(XO.at[m], XS.at[m, 1], S.x_s.at[m, 1], S.x_r.at[m, 1], dev(h, c, y, z, 0))

    def x_first(m, slot):
        return remote(XO.at[m], XS.at[m, slot], S.x_s.at[m, 0], S.x_r.at[m, slot], dev(oh, c, y, z, 1))

    def x_prepare():
        for m, codes in enumerate((wg, wt, wc)):
            own = codes[...].astype(F32)
            own = jnp.concatenate([own, jnp.zeros((PAD - HALF, COLS), F32)], axis=0).astype(BF16)
            XO[m] = own

            @pl.when(l == 0)
            def _():
                XS[m, 0] = own

    def x_start(m):
        @pl.when(l == 0)
        def _():
            x_first(m, 0).start()

        @pl.when(l == 1)
        def _():
            x_second(m).start()
            x_first(m, 1).start()

    def assemble(m):
        @pl.when(l == 1)
        def _():
            arrived(XS.at[m, 0], S.x_s.at[m, 0], S.x_r.at[m, 0])

        arrived(XS.at[m, 1], S.x_s.at[m, 1], S.x_r.at[m, 1])
        both = [XS[m, i].astype(F32)[:HALF] for i in range(2)]
        S.W[m, y, z] = jnp.concatenate(both, axis=0).astype(BF16)

    XG, NS, SC = S.XG, S.NS, S.SC
    tok_own = pltpu.make_async_copy(gi, XG.at[q], S.tk_s.at[3])

    def tok_near():
        send(gi, XG.at[q], S.tk_s.at[1], S.tk_r.at[1], dev(h, oc, y, z, l))

    def tok_far():
        send(gi, XG.at[q], S.tk_s.at[0], S.tk_r.at[0], dev(h, c, y, z, ol))

    def tok_forward():
        arrived(XG.at[q_far], S.tk_s.at[0], S.tk_r.at[0])
        send(XG.at[q_far], XG.at[q_far], S.tk_s.at[2], S.tk_r.at[2], dev(h, oc, y, z, l))

    q_far, q_near, q_last = 2 * ol + c, 2 * l + oc, 2 * ol + oc

    def columns(c_, l_):
        return pl.ds(pl.multiple_of((2 * ((h + l_) % 2) + c_) * COLS, COLS), COLS)

    others = ((oc, l), (c, ol), (oc, ol))

    def noise_send(i):
        c_, l_ = others[i]
        send(noise.at[:, columns(c_, l_)], NS.at[q], S.ns_s.at[i], S.ns_r.at[i], dev(h, c_, y, z, l_))

    def noise_wait():
        noise_own.wait()
        for i, (c_, l_) in enumerate(others):
            arrived(NS.at[2 * l_ + c_], S.ns_s.at[i], S.ns_r.at[i])

    noise_own = pltpu.make_async_copy(noise.at[:, columns(c, l)], NS.at[q], S.ns_s.at[3])

    def scale_copy():
        return remote(scales, SC, S.sc_s.at[0], S.sc_r.at[0], dev(oh, c, y, z, 1))

    def scale_own():
        return pltpu.make_async_copy(scales, SC, S.sc_r.at[0])

    def scale_start():
        @pl.when(l == 0)
        def _():
            scale_copy().start()
            scale_own().start()

    def piece(i):
        m, j = i // PIECES, i % PIECES
        if j < 8:
            offset = j * COLS
        else:
            offset = pl.multiple_of(2 * D + cb * COLS, COLS)
        return pltpu.make_async_copy(tproj.at[m, :, pl.ds(offset, TPC)], S.TP.at[i % SLOTS], S.tp_m.at[i % SLOTS])

    def gen_hat(block, part):
        H = S.H

        def rows(r, carry):
            at = pl.ds(pl.multiple_of(part * 32 + r * 16, 16), 16)
            x = XG[block, at, :].astype(F32)
            inv = lax.rsqrt(jnp.sum(x * x, axis=1, keepdims=True) / D + RMS_EPS)
            hat = (x * inv * (1.0 + mod[0, 1:2, :]) + mod[0, 0:1, :]).astype(BF16)
            to = pl.ds(pl.multiple_of(block * ROWS + part * 32 + r * 16, 16), 16)
            for k in range(4):
                H[k, to, :] = hat[:, k * COLS : (k + 1) * COLS]
            return carry

        lax.fori_loop(0, 2, rows, 0)

    def features():
        index = lax.broadcasted_iota(jnp.int32, (1, ROWS), 1).astype(F32)
        frequency = jnp.exp(index * (-math.log(10000.0) / ROWS))
        phase = jnp.full((1, ROWS), dstep[h], jnp.int32).astype(F32) * frequency
        feature = jnp.concatenate([jnp.cos(phase), jnp.sin(phase)], axis=1)
        hi = feature.astype(BF16).astype(F32)
        mid = (feature - hi).astype(BF16).astype(F32)
        low = (feature - hi - mid).astype(BF16).astype(F32)
        row = lax.broadcasted_iota(jnp.int32, (16, 2 * ROWS), 0)
        a, b, d = [jnp.broadcast_to(v, (16, 2 * ROWS)) for v in (hi, mid, low)]
        S.FT[...] = jnp.where(row == 0, a, jnp.where(row == 1, b, jnp.where(row == 2, d, 0.0))).astype(BF16)

    def judge_piece(i):
        m, j = i // PIECES, i % PIECES
        piece(i).wait()
        lifted = jnp.dot(S.FT[...], S.TP[i % SLOTS], preferred_element_type=F32)
        lifted = jnp.sum(lifted, axis=0, keepdims=True)
        if j < 8:
            S.JM[m, j // 4, j % 4] = lifted + mod[m + 1, j // 4 : j // 4 + 1, (j % 4) * COLS : (j % 4 + 1) * COLS]
        else:
            gate = mod[m + 1, 2:3, pl.ds(pl.multiple_of(cb * COLS, COLS), COLS)]
            S.PK[m + 4 : m + 5, :] = lifted + gate
        if i + SLOTS < 2 * PIECES:
            piece(i + SLOTS).start()

    def factors():
        arrived(SC, S.sc_s.at[0], S.sc_r.at[0])
        row = lax.broadcasted_iota(jnp.int32, (8, COLS), 0)
        for m in range(3):
            group = jnp.where(h == 0, sgroup[0:1, m : m + 1], sgroup[1:2, m : m + 1])
            picked = jnp.sum(jnp.where(row == group, SC[m], 0.0), axis=0, keepdims=True)
            if m == 0:
                gate = mod[0, 2:3, pl.ds(pl.multiple_of(cb * COLS, COLS), COLS)]
            else:
                gate = S.PK[m + 3 : m + 4, :]
            S.PK[m : m + 1, :] = gate * picked

    def level():
        return jnp.full((1, COLS), dstep[h], jnp.int32).astype(F32) / 1000.0

    def product(lhs, m, k, first=False):
        ACC = S.ACC
        part = jnp.dot(lhs[k], S.W[m, k].reshape(COLS, COLS), preferred_element_type=F32)
        if first:
            ACC[...] = part
        else:
            ACC[...] += part

    TILE = 64

    def clean_rows(block):
        lev = level()
        here = pl.ds(pl.multiple_of(cb * COLS, COLS), COLS)

        def rows(r, carry):
            at = pl.ds(pl.multiple_of(block * ROWS + r * TILE, TILE), TILE)
            inner = pl.ds(pl.multiple_of(r * TILE, TILE), TILE)
            branch = (S.ACC[at, :] * S.PK[0:1, :]).astype(BF16)
            clean = XG[block, inner, here].astype(F32) + branch.astype(F32)
            noisy = (1.0 - lev) * clean + lev * NS[block, inner, :].astype(F32)
            S.CL[at, :] = clean
            S.NF[at, :] = noisy
            S.SB[at, :] = clean.astype(BF16)
            S.NG[cb, at, :] = noisy.astype(BF16)
            return carry

        lax.fori_loop(0, ROWS // TILE, rows, 0)

    def block_rows(block):
        return pl.ds(block * ROWS, ROWS)

    def noisy_send(block):
        own = S.NG.at[cb, block_rows(block)]
        send(own, own, S.ng_s.at[block, 0], S.ng_r.at[block, 0], dev(h, c, y, z, ol))
        send(own, own, S.ng_s.at[block, 1], S.ng_r.at[block, 1], dev(h, oc, y, z, l))

    far = 2 * ((h + ol) % 2) + c

    def noisy_forward(block):
        got = S.NG.at[far, block_rows(block)]
        arrived(got, S.ng_s.at[block, 0], S.ng_r.at[block, 0])
        send(got, got, S.ng_s.at[block, 2], S.ng_r.at[block, 2], dev(h, oc, y, z, l))

    def noisy_wait(block):
        near = 2 * ((h + l) % 2) + oc
        last = 2 * ((h + ol) % 2) + oc
        arrived(S.NG.at[near, block_rows(block)], S.ng_s.at[block, 1], S.ng_r.at[block, 1])
        arrived(S.NG.at[last, block_rows(block)], S.ng_s.at[block, 2], S.ng_r.at[block, 2])

    def judge_hats(part):
        NG, JH, JM = S.NG, S.JH, S.JM

        def rows(r, carry):
            at = pl.ds(pl.multiple_of(part * 64 + r * 16, 16), 16)
            v = [NG[k, at, :].astype(F32) for k in range(4)]
            total = sum(jnp.sum(t * t, axis=1, keepdims=True) for t in v)
            inv = lax.rsqrt(total / D + RMS_EPS)
            for k in range(4):
                normed = (v[k] * inv).astype(BF16).astype(F32)
                for j in range(2):
                    JH[j, k, at, :] = (normed * (1.0 + JM[j, 1, k]) + JM[j, 0, k]).astype(BF16)
            return carry

        lax.fori_loop(0, 4, rows, 0)

    def return_rows(buf, out, ss, rs):
        here = pl.ds(pl.multiple_of(cb * COLS, COLS), COLS)
        for i, (c_, l_) in enumerate(others):
            block = pl.ds(pl.multiple_of((2 * l_ + c_) * ROWS, ROWS), ROWS)
            send(buf.at[block], out.at[:, here], ss.at[i], rs.at[i], dev(h, c_, y, z, l_))
        block = pl.ds(pl.multiple_of(q * ROWS, ROWS), ROWS)
        own = pltpu.make_async_copy(buf.at[block], out.at[:, here], ss.at[3])
        own.start()
        return own

    def return_wait(out, ss, rs):
        for i, (c_, l_) in enumerate(others):
            arrived(out.at[:, columns(c_, l_)], ss.at[i], rs.at[i])

    def real_rows():
        def rows(r, carry):
            at = pl.ds(pl.multiple_of(r * TILE, TILE), TILE)
            S.RP[at, :] = (S.ACC[at, :] * S.PK[1:2, :]).astype(BF16)
            return carry

        lax.fori_loop(0, GROUP // TILE, rows, 0)

    def spread_rows():
        lev = level()

        def rows(r, total):
            at = pl.ds(pl.multiple_of(r * TILE, TILE), TILE)
            noisy = S.NF[at, :]
            gone = jnp.abs(S.CL[at, :] - (noisy - lev * (noisy + S.RP[at, :].astype(F32))))
            return total + jnp.sum(gone.reshape(TILE // 8, 8, COLS), axis=0)

        total = lax.fori_loop(0, GROUP // TILE, rows, jnp.zeros((8, COLS), F32))
        total = jnp.sum(jnp.sum(total, axis=1, keepdims=True), axis=0, keepdims=True)
        S.SP[...] = jnp.broadcast_to(total, (8, 128))

    def gap_rows():
        lev = level()

        def rows(r, carry):
            at = pl.ds(pl.multiple_of(r * TILE, TILE), TILE)
            fake = (S.ACC[at, :] * S.PK[2:3, :]).astype(BF16).astype(F32)
            gap = lev * (S.RP[at, :].astype(F32) - fake)
            S.GP[at, :] = gap
            S.CT[at, :] = (gap * S.PK[0:1, :]).astype(BF16)
            return carry

        lax.fori_loop(0, GROUP // TILE, rows, 0)

    def spread_group_start():
        S.SPG[q] = S.SP[...]
        for i, (c_, l_) in enumerate(others):
            send(S.SP, S.SPG.at[q], S.sg_s.at[i], S.sg_r.at[i], dev(h, c_, y, z, l_))

    def spread_z_start():
        for i, (c_, l_) in enumerate(others):
            arrived(S.SPG.at[2 * l_ + c_], S.sg_s.at[i], S.sg_r.at[i])
        SPG, SPZ = S.SPG, S.SPZ
        SPZ[z] = (SPG[0] + SPG[1]) + (SPG[2] + SPG[3])
        for j in range(1, NZ):
            send(SPZ.at[z], SPZ.at[z], S.sz_s.at[j], S.sz_r.at[j], dev(h, c, y, zz(j), l))

    def spread_y_start():
        SPZ, SPY = S.SPZ, S.SPY
        for j in range(1, NZ):
            arrived(SPZ.at[zz(-j)], S.sz_s.at[j], S.sz_r.at[j])
        total = SPZ[0]
        for j in range(1, NZ):
            total = total + SPZ[j]
        SPY[y] = total
        for j in range(1, NY):
            send(SPY.at[y], SPY.at[y], S.sy_s.at[j], S.sy_r.at[j], dev(h, c, yy(j), z, l))

    def spread_value():
        SPY = S.SPY
        for j in range(1, NY):
            arrived(SPY.at[yy(-j)], S.sy_s.at[j], S.sy_r.at[j])
        total = SPY[0]
        for j in range(1, NY):
            total = total + SPY[j]
        S.SV[...] = total / CLIP_ELEMENTS + SPREAD_EPS

    def dmd_rows():
        def rows(r, carry):
            at = pl.ds(pl.multiple_of(r * TILE, TILE), TILE)
            S.DB[at, :] = (S.GP[at, :] / S.SV[0:1, 0:1]).astype(BF16)
            return carry

        lax.fori_loop(0, GROUP // TILE, rows, 0)

    G = S.G

    def grad(k, lanes, width):
        block = lax.dot_general(S.H[k], S.CT[:, lanes], (((0,), (0,)), ((), ())), preferred_element_type=F32)
        G[k, :, :, lanes] = block.reshape(NZ, BLK, width)

    def grad_b(k):
        grad(k, LB, CB)

    def grad_a(k):
        grad(k, LA, CA)

    def big_y0(r):
        S.Y0S[r] = G[yy(2), zz(r), :, LB].astype(BF16)
        target = dev(h, c, yy(1 - 2 * way_of[r]), z, l)
        remote(S.Y0S.at[r], S.Y0R.at[r], S.rs_s.at[0], S.b0_r.at[r], target).start()

    def big_y1(r):
        for way in range(2):
            s = 1 - 2 * way
            v = G[yy(s), zz(r), :, LB]
            if way == way_of[r]:
                arrived(S.Y0R.at[r], S.rs_s.at[0], S.b0_r.at[r])
                v = v + S.Y0R[r].astype(F32)
            S.Y1S[r, way] = v.astype(BF16)
            remote(S.Y1S.at[r, way], S.Y1R.at[r, way], S.rs_s.at[1], S.b1_r.at[r], dev(h, c, yy(s), z, l)).start()

    def big_y2(r):
        Y1R = S.Y1R
        arrived(Y1R.at[r], S.rs_s.at[1], S.b1_r.at[r])
        G[y, zz(r), :, LB] = G[y, zz(r), :, LB] + Y1R[r, 0].astype(F32) + Y1R[r, 1].astype(F32)

    def slot(k, way):
        return 0 if k == 1 else 2 * k - 3 + way

    def pair(k):
        return pl.ds(slot(k, 0), 1 if k == 1 else 2)

    def big_z(k, j):
        ZS, ZR = S.ZS, S.ZR
        at = yy(Y_ORDER[j])
        if k > 1:
            arrived(ZR.at[pair(k - 1), j], S.rs_s.at[2], S.a_r.at[k - 2, j])
        for way in range(2):
            s = 1 - 2 * way
            if k == 5 or (k == 1 and way != j % 2):
                continue
            v = G[at, zz(s * (5 - k)), :, LA]
            if k > 2 or (k == 2 and way == j % 2):
                v = v + ZR[slot(k - 1, way), j].astype(F32)
            n = slot(k, way)
            ZS[n, j] = v.astype(BF16)
            remote(ZS.at[n, j], ZR.at[n, j], S.rs_s.at[2], S.a_r.at[k - 1, j], dev(h, c, y, zz(s), l)).start()
        if k == 5:
            G[at, z, :, LA] = G[at, z, :, LA] + ZR[5, j].astype(F32) + ZR[6, j].astype(F32)

    def small_y(step):
        ys, yr = S.ys, S.yr
        halves = (pl.ds(0, CA // 2), pl.ds(CA // 2, CA // 2))
        if step > 0:
            arrived(yr.at[0] if step == 1 else yr.at[1:3], S.rs_s.at[3], S.y_r.at[step - 1])
        for way in range(2):
            s = 1 - 2 * way
            part = halves[way]
            target = dev(h, c, yy(s), z, l)
            if step == 0:
                ys[0, :, part] = G[yy(2), z, :, part].astype(BF16)
                remote(ys.at[0, :, part], yr.at[0, :, part], S.rs_s.at[3], S.y_r.at[0], target).start()
            elif step == 1:
                other = halves[1 - way]
                ys[1 + way, :, part] = (G[yy(s), z, :, part] + yr[0, :, part].astype(F32)).astype(BF16)
                ys[1 + way, :, other] = G[yy(s), z, :, other].astype(BF16)
                remote(ys.at[1 + way], yr.at[1 + way], S.rs_s.at[3], S.y_r.at[1], target).start()
        if step == 2:
            G[y, z, :, LA] = G[y, z, :, LA] + yr[1].astype(F32) + yr[2].astype(F32)

    def small_z(k):
        zs, zr = S.zs, S.zr
        if k > 1:
            arrived(zr.at[0] if k == 2 else zr.at[pair(k - 1)], S.rs_s.at[4], S.z_r.at[k - 2])
        for way in range(2):
            s = 1 - 2 * way
            some = (pl.ds(0, CUT), pl.ds(CUT, BLK - CUT))[way]
            target = dev(h, c, y, zz(s), l)
            n = slot(k, way)
            if k == 1:
                zs[0, some, :] = G[y, zz(4), some, LB].astype(BF16)
                remote(zs.at[0, some], zr.at[0, some], S.rs_s.at[4], S.z_r.at[0], target).start()
            elif k < 5:
                at = zz(s * (5 - k))
                if k > 2:
                    zs[n] = (G[y, at, :, LB] + zr[slot(k - 1, way)].astype(F32)).astype(BF16)
                else:
                    other = (pl.ds(CUT, BLK - CUT), pl.ds(0, CUT))[way]
                    zs[n, some, :] = (G[y, at, some, LB] + zr[0, some, :].astype(F32)).astype(BF16)
                    zs[n, other, :] = G[y, at, other, LB].astype(BF16)
                remote(zs.at[n], zr.at[n], S.rs_s.at[4], S.z_r.at[k - 1], target).start()
        if k == 5:
            G[y, z, :, LB] = G[y, z, :, LB] + zr[5].astype(F32) + zr[6].astype(F32)

    def rings_sent():
        wholes = (S.Y0S, S.Y1S, S.ZS.at[0:7], S.ys.at[0:3], S.zs.at[0:7])
        for i, whole in enumerate(wholes):
            remote(whole, whole, S.rs_s.at[i], S.b0_r.at[0], dev(h, oc, y, z, l)).wait_send()

    tok_own.start()
    noise_own.start()
    for i in range(SLOTS):
        piece(i).start()
    x_prepare()
    features()
    pl.semaphore_wait(barrier, len(greeted))
    x_start(0)
    x_start(1)
    x_start(2)
    tok_near()
    scale_start()
    tok_own.wait()
    gen_hat(q, 0)
    gen_hat(q, 1)
    gen_hat(q, 2)
    gen_hat(q, 3)
    judge_piece(0)
    judge_piece(1)
    judge_piece(2)
    judge_piece(3)
    judge_piece(4)
    judge_piece(5)
    judge_piece(6)
    judge_piece(7)
    judge_piece(8)
    judge_piece(9)
    judge_piece(10)
    judge_piece(11)
    judge_piece(12)
    assemble(0)
    ag_go(0, AY, 1)
    ag_go(0, BZ, 1)
    ag_go(0, FY, 1, 0)
    judge_piece(13)
    arrived(XG.at[q_near], S.tk_s.at[1], S.tk_r.at[1])
    gen_hat(q_near, 0)
    gen_hat(q_near, 1)
    gen_hat(q_near, 2)
    gen_hat(q_near, 3)
    judge_piece(14)
    judge_piece(15)
    judge_piece(16)
    judge_piece(17)
    assemble(1)
    ag_go(1, AY, 1)
    ag_go(1, BZ, 1)
    ag_got(0, AY, 1)
    ag_go(0, AY, 2)
    ag_got(0, BZ, 1)
    ag_go(0, BZ, 2)
    ag_go(0, FY, 1, 1)
    ag_go(0, FY, 1, 7)
    tok_far()
    ag_got(0, FY, 1, 0)
    ag_go(0, FY, 2, 0)
    assemble(2)
    ag_go(2, BZ, 1)
    factors()
    ag_got(0, AY, 2)
    ag_go(0, AZ, 1, 0)
    ag_got(0, FY, 1, 1)
    ag_go(0, FY, 2, 1)
    ag_got(0, BZ, 2)
    ag_go(0, BZ, 3)
    ag_go(0, FY, 1, 2)
    ag_go(0, FY, 1, 6)
    ag_go(0, AZ, 1, 1)
    ag_got(0, FY, 1, 7)
    ag_go(0, FY, 2, 7)
    ag_got(0, AZ, 1, 0)
    ag_go(0, AZ, 2, 0)
    ag_got(0, FY, 1, 2)
    ag_go(0, FY, 2, 2)
    ag_got(1, AY, 1)
    ag_go(1, AY, 2)
    ag_got(0, BZ, 3)
    ag_go(0, BZ, 4)
    ag_go(0, FY, 1, 3)
    ag_go(0, FY, 1, 5)
    ag_got(1, BZ, 1)
    ag_go(1, BZ, 2)
    ag_got(0, FY, 1, 6)
    ag_go(0, FY, 2, 6)
    ag_got(0, AZ, 1, 1)
    ag_go(0, AZ, 2, 1)
    ag_go(2, AY, 1)
    ag_got(0, FY, 1, 3)
    ag_go(0, FY, 2, 3)
    ag_got(0, AZ, 2, 0)
    ag_go(0, AZ, 3, 0)
    ag_got(0, BZ, 4)
    ag_go(0, FY, 1, 4)
    ag_got(0, FY, 1, 5)
    ag_go(0, FY, 2, 5)
    ag_got(1, BZ, 2)
    ag_go(1, BZ, 3)
    ag_got(2, AY, 1)
    ag_go(2, AY, 2)
    ag_got(0, AZ, 2, 1)
    ag_go(0, AZ, 3, 1)
    ag_got(0, FY, 1, 4)
    ag_go(0, FY, 2, 4)
    ag_got(0, AZ, 3, 0)
    ag_go(0, AZ, 4, 0)
    tok_forward()
    noise_send(0)
    noise_send(1)
    noise_send(2)
    gen_hat(q_far, 0)
    gen_hat(q_far, 1)
    gen_hat(q_far, 2)
    gen_hat(q_far, 3)
    ag_got(1, BZ, 3)
    ag_go(1, BZ, 4)
    ag_got(0, AZ, 3, 1)
    ag_go(0, AZ, 4, 1)
    ag_got(1, AY, 2)
    ag_go(1, AZ, 1, 0)
    arrived(XG.at[q_last], S.tk_s.at[2], S.tk_r.at[2])
    gen_hat(q_last, 0)
    gen_hat(q_last, 1)
    ag_got(1, BZ, 4)
    ag_go(1, BY, 1, 0)
    ag_go(1, AZ, 1, 1)
    gen_hat(q_last, 2)
    gen_hat(q_last, 3)
    ag_got(0, AZ, 4, 0)
    ag_got(0, AZ, 4, 1)
    product(S.H, 0, y, True)
    ag_got(2, BZ, 1)
    ag_go(2, BZ, 2)
    product(S.H, 0, yy(1))
    product(S.H, 0, yy(-1))
    ag_got(1, AZ, 1, 0)
    ag_go(1, AZ, 2, 0)
    ag_got(0, FY, 2, 0)
    ag_got(0, FY, 2, 1)
    ag_got(0, FY, 2, 7)
    ag_got(0, FY, 2, 2)
    ag_got(0, FY, 2, 6)
    ag_got(0, FY, 2, 3)
    ag_got(0, FY, 2, 5)
    ag_got(0, FY, 2, 4)
    product(S.H, 0, yy(2))
    ag_go(1, BY, 1, 1)
    noise_wait()
    clean_rows(0)
    noisy_send(0)
    clean_rows(1)
    noisy_send(1)
    clean_rows(2)
    noisy_send(2)
    ag_got(1, AZ, 1, 1)
    ag_go(1, AZ, 2, 1)
    clean_rows(3)
    noisy_send(3)
    ag_got(2, BZ, 2)
    ag_go(2, BZ, 3)
    ag_got(1, AZ, 2, 0)
    ag_go(1, AZ, 3, 0)
    noisy_forward(0)
    ag_got(1, BY, 1, 0)
    ag_go(1, BY, 2, 0)
    ag_got(1, AZ, 2, 1)
    ag_go(1, AZ, 3, 1)
    ag_got(2, BZ, 3)
    ag_go(2, BZ, 4)
    noisy_wait(0)
    judge_hats(0)
    ag_got(1, BY, 1, 1)
    ag_go(1, BY, 2, 1)
    ag_got(2, AY, 2)
    ag_go(2, AZ, 1, 0)
    judge_hats(1)
    noisy_forward(1)
    ag_got(1, AZ, 3, 0)
    ag_go(1, AZ, 4, 0)
    ag_got(1, AZ, 3, 1)
    ag_go(1, AZ, 4, 1)
    ag_got(2, BZ, 4)
    ag_go(2, BY, 1, 0)
    noisy_wait(1)
    judge_hats(2)
    ag_go(2, AZ, 1, 1)
    judge_hats(3)
    noisy_forward(2)
    ag_got(2, AZ, 1, 0)
    ag_go(2, AZ, 2, 0)
    noisy_wait(2)
    judge_hats(4)
    judge_hats(5)
    noisy_forward(3)
    ag_go(2, BY, 1, 1)
    ag_got(2, AZ, 1, 1)
    ag_go(2, AZ, 2, 1)
    ag_got(2, AZ, 2, 0)
    ag_go(2, AZ, 3, 0)
    noisy_wait(3)
    judge_hats(6)
    judge_hats(7)
    ag_got(1, AZ, 4, 0)
    ag_got(1, AZ, 4, 1)
    product(S.JH.at[0], 1, y, True)
    ag_got(2, AZ, 2, 1)
    ag_go(2, AZ, 3, 1)
    product(S.JH.at[0], 1, yy(1))
    product(S.JH.at[0], 1, yy(-1))
    ag_got(2, BY, 1, 0)
    ag_go(2, BY, 2, 0)
    ag_got(2, AZ, 3, 0)
    ag_go(2, AZ, 4, 0)
    ag_got(1, BY, 2, 0)
    ag_got(1, BY, 2, 1)
    product(S.JH.at[0], 1, yy(2))
    real_rows()
    spread_rows()
    spread_group_start()
    ag_got(2, AZ, 3, 1)
    ag_go(2, AZ, 4, 1)
    ag_got(2, BY, 1, 1)
    ag_go(2, BY, 2, 1)
    sample_own = return_rows(S.SB, out_s, S.sm_s, S.sm_r)
    ag_got(2, AZ, 4, 0)
    ag_got(2, AZ, 4, 1)
    product(S.JH.at[1], 2, y, True)
    product(S.JH.at[1], 2, yy(1))
    product(S.JH.at[1], 2, yy(-1))
    ag_got(2, BY, 2, 0)
    ag_got(2, BY, 2, 1)
    product(S.JH.at[1], 2, yy(2))
    gap_rows()
    spread_z_start()
    grad_b(yy(2))
    big_y0(4)
    big_y0(3)
    grad_a(yy(2))
    big_y0(5)
    big_z(1, 0)
    grad_a(yy(1))
    big_y0(2)
    big_z(1, 1)
    grad_a(yy(-1))
    big_y0(6)
    big_z(1, 2)
    grad_a(yy(0))
    big_y0(1)
    big_z(1, 3)
    grad_b(yy(1))
    big_z(2, 0)
    grad_b(yy(-1))
    big_y0(7)
    big_z(2, 1)
    grad_b(y)
    big_y0(0)
    big_z(2, 2)
    spread_y_start()
    big_y1(4)
    big_z(2, 3)
    ag_sent(0)
    ag_sent(1)
    ag_sent(2)
    big_z(3, 0)
    big_y1(3)
    big_z(3, 1)
    spread_value()
    dmd_rows()
    big_y1(5)
    big_z(3, 2)
    dmd_own = return_rows(S.DB, out_d, S.dm_s, S.dm_r)
    big_z(3, 3)
    big_y2(4)
    small_z(1)
    big_y1(2)
    big_z(4, 0)
    big_y2(3)
    big_y1(6)
    big_z(4, 1)
    big_y2(5)
    big_y1(1)
    big_z(4, 2)
    small_z(2)
    big_y2(2)
    big_y1(7)
    big_z(5, 0)
    small_y(0)
    drain()
    big_z(4, 3)
    big_y2(6)
    big_z(5, 1)
    big_y1(0)
    big_z(5, 2)
    big_y2(1)
    small_z(3)
    big_y2(7)
    small_y(1)
    big_z(5, 3)
    big_y2(0)
    small_z(4)
    small_y(2)
    small_z(5)
    GF, OW = S.GF, S.OW
    done = G[y, z] / S.SV[0:1, 0:1] / TOKENS

    def own_row(row, slot, target):
        return remote(GF.at[row], OW.at[slot], S.ow_s.at[row], S.ow_r.at[slot], target)

    for row in range(2):
        GF[row] = done[row * HALF : (row + 1) * HALF]

    @pl.when(l == 0)
    def _():
        OW[0] = GF[0]
        own_row(1, 0, dev(h, c, y, z, 1)).start()

    @pl.when(l == 1)
    def _():
        own_row(0, 1, dev(oh, c, y, z, 0)).start()
        own_row(1, 1, dev(oh, c, y, z, 1)).start()
        arrived(OW.at[0], S.ow_s.at[0], S.ow_r.at[0])

    arrived(OW.at[1], S.ow_s.at[1], S.ow_r.at[1])
    out_w[...] = OW[0] + OW[1]
    return_wait(out_s, S.sm_s, S.sm_r)
    return_wait(out_d, S.dm_s, S.dm_r)
    sample_own.wait()
    dmd_own.wait()
    rings_sent()
    drain()
    for m in range(3):
        x_first(m, 0).wait_send()

    @pl.when(l == 0)
    def _():
        scale_copy().wait_send()
        own_row(1, 0, dev(h, c, y, z, 1)).wait_send()

    @pl.when(l == 1)
    def _():
        for m in range(3):
            x_second(m).wait_send()
        own_row(0, 1, dev(oh, c, y, z, 0)).wait_send()
        own_row(1, 1, dev(oh, c, y, z, 1)).wait_send()


def copy_results(a_in, b_in, c_in, a_out, b_out, c_out):
    a_out[...] = a_in[...]
    b_out[...] = b_in[...]
    c_out[...] = c_in[...]


def on_device(gi, noise, dmd_step, scale_group, wg, wt, wc, scales, mod, tproj):
    vmem = pl.BlockSpec(memory_space=pltpu.VMEM)
    smem = pl.BlockSpec(memory_space=pltpu.SMEM)
    hbm = pl.BlockSpec(memory_space=pl.ANY)
    out_shape = (
        jax.ShapeDtypeStruct((ROWS, D), BF16),
        jax.ShapeDtypeStruct((ROWS, D), BF16),
        jax.ShapeDtypeStruct((HALF, COLS), F32),
    )
    results = pl.pallas_call(
        kernel,
        out_shape=out_shape,
        in_specs=[hbm, hbm, smem, vmem, vmem, vmem, vmem, hbm, vmem, hbm],
        out_specs=(hbm, hbm, vmem),
        scratch_shapes=list(scratch_table().values()),
        compiler_params=pltpu.CompilerParams(
            collective_id=0, has_side_effects=True, vmem_limit_bytes=64 * 1024 * 1024 - 65536
        ),
    )(gi, noise, dmd_step, scale_group.T, wg, wt, wc, scales, mod, tproj)
    half = pl.BlockSpec((ROWS // 2, D), lambda i: (i, 0))
    whole = pl.BlockSpec((HALF, COLS), lambda i: (0, 0))
    return pl.pallas_call(
        copy_results,
        grid=(2,),
        out_shape=out_shape,
        in_specs=[half, half, whole],
        out_specs=(half, half, whole),
    )(*results)


def solution(mesh):
    return jax.shard_map(
        on_device,
        mesh=mesh,
        in_specs=(
            P(("dp", "fsdp"), None),
            P(("dp", "fsdp"), None),
            P(),
            P(),
            P("fsdp", "dp"),
            P("fsdp", "dp"),
            P("fsdp", "dp"),
            P(None, None, "dp"),
            P(),
            P(),
        ),
        out_specs=(P(("dp", "fsdp"), None), P(("dp", "fsdp"), None), P("fsdp", "dp")),
        check_vma=False,
    )
```

```python
import functools
import math
import types

import jax
import jax.numpy as jnp
from jax import lax
from jax.experimental import pallas as pl
from jax.experimental.pallas import tpu as pltpu
from jax.sharding import PartitionSpec as P

RMS_EPS = 1e-06
SPREAD_EPS = 1e-05
F32 = jnp.float32
BF16 = jnp.bfloat16
MESH_ID = pl.DeviceIdType.MESH

NY, NZ = 4, 8
D = 2560
COLS = 640
ROWS = 128
GROUP = 4 * ROWS
HALF = 40
PAD = 48
BLK = 80
CA = 256
CB = COLS - CA
CUT = 48
TOKENS = 32768
CLIP_ELEMENTS = 16384 * 2560
TPC = 640
PIECES = 9
SLOTS = 4
AY, AZ, BZ, BY, FY, FZ, XY, XZ = range(8)
FINE_Y, FINE_Z = (0, 1, 2), (0, 1, 2)
SHARED = (1, 2)


def ag_table():
    steps = []
    for m in range(3):
        steps += [(m, AY, k, 0) for k in (1, 2)] + [(m, BZ, k, 0) for k in (1, 2, 3, 4)]
        if m in SHARED:
            steps += [(m, FZ, k, i) for k in (1, 2, 3, 4) for i in range(3)] + [(m, XZ, k, 0) for k in (1, 2, 3, 4)]
            steps += [(m, FY, k, i) for k in (1, 2) for i in (0, 1, 7, 4, 8, 9)] + [(m, XY, k, i) for k in (1, 2) for i in (8, 9)]
            continue
        steps += [(m, FZ, k, i) for k in (1, 2, 3, 4) for i in range(4)] if m in FINE_Z else [(m, AZ, k, i) for k in (1, 2, 3, 4) for i in range(2)]
        steps += [(m, FY, k, i) for k in (1, 2) for i in range(8)] if m in FINE_Y else [(m, BY, k, i) for k in (1, 2) for i in range(2)]
    return {step: n for n, step in enumerate(steps)}


AG_SEMS = ag_table()


def scratch_table():
    vmem, dma = pltpu.VMEM, pltpu.SemaphoreType.DMA
    return dict(
        W=vmem((3, NY, NZ, BLK, COLS), BF16),
        XO=vmem((3, PAD, COLS), BF16),
        XS=vmem((3, 2, PAD, COLS), BF16),
        XG=vmem((4, ROWS, D), BF16),
        H=vmem((4, GROUP, COLS), BF16),
        NS=vmem((4, ROWS, COLS), BF16),
        CL=vmem((GROUP, COLS), F32),
        NF=vmem((GROUP, COLS), F32),
        NG=vmem((4, GROUP, COLS), BF16),
        JH=vmem((2, 4, GROUP, COLS), BF16),
        ACC=vmem((GROUP, COLS), F32),
        RP=vmem((GROUP, COLS), BF16),
        GP=vmem((GROUP, COLS), F32),
        CT=vmem((GROUP, COLS), BF16),
        SB=vmem((GROUP, COLS), BF16),
        DB=vmem((GROUP, COLS), BF16),
        G=vmem((NY, NZ, BLK, COLS), F32),
        ZS=vmem((8, NY, BLK, CA), BF16),
        ZR=vmem((8, NY, BLK, CA), BF16),
        Y0S=vmem((NZ, BLK, CB), BF16),
        Y0R=vmem((NZ, BLK, CB), BF16),
        Y1S=vmem((NZ, 2, BLK, CB), BF16),
        Y1R=vmem((NZ, 2, BLK, CB), BF16),
        ys=vmem((4, BLK, CA), BF16),
        yr=vmem((4, BLK, CA), BF16),
        zs=vmem((8, BLK, CB), BF16),
        zr=vmem((8, BLK, CB), BF16),
        SC=vmem((3, 8, COLS), F32),
        PK=vmem((8, COLS), F32),
        TP=vmem((SLOTS, 2 * ROWS, TPC), BF16),
        FT=vmem((16, 2 * ROWS), BF16),
        JM=vmem((2, 2, 4, 1, COLS), F32),
        SP=vmem((8, 128), F32),
        SV=vmem((8, 128), F32),
        SPG=vmem((4, 8, 128), F32),
        SPZ=vmem((NZ, 8, 128), F32),
        SPY=vmem((NY, 8, 128), F32),
        GF=vmem((2, PAD, COLS), BF16),
        OW=vmem((2, PAD, COLS), BF16),
        ag_s=dma((3, 6)),
        ag_r=dma((len(AG_SEMS),)),
        x_s=dma((3, 2)),
        x_r=dma((3, 2)),
        tk_s=dma((2,)),
        tk_r=dma((3,)),
        ns_s=dma((2,)),
        ns_r=dma((1,)),
        ng_s=dma((1,)),
        ng_r=dma((4, 2)),
        sm_s=dma((2,)),
        sm_r=dma((1,)),
        dm_s=dma((2,)),
        dm_r=dma((1,)),
        sc_s=dma((1,)),
        sc_r=dma((1,)),
        tp_m=dma((SLOTS,)),
        sg_s=dma((1,)),
        sg_r=dma((1,)),
        sz_s=dma((1,)),
        sz_r=dma((1,)),
        sy_s=dma((1,)),
        sy_r=dma((1,)),
        rs_s=dma((5,)),
        b0_r=dma((NZ,)),
        b1_r=dma((NZ,)),
        a_r=dma((4, NY)),
        y_r=dma((1,)),
        z_r=dma((4,)),
        ow_s=dma((2,)),
        ow_r=dma((2,)),
    )


NAMES = tuple(scratch_table())


def kernel(gi, noise, dstep, sgroup, wg, wt, wc, scales, mod, tproj, out_s, out_d, out_w, *rest):
    S = types.SimpleNamespace(**dict(zip(NAMES, rest)))
    dp, fs = lax.axis_index("dp"), lax.axis_index("fsdp")
    h, c = dp // 2, dp % 2
    l, plane = fs % 2, fs // 2
    y, z = plane // NZ, plane % NZ
    oh, oc, ol = 1 - h, 1 - c, 1 - l
    q = 2 * l + c
    cb = 2 * ((h + l) % 2) + c

    def dev(h_, c_, y_, z_, l_):
        return (2 * h_ + c_, (y_ * NZ + z_) * 2 + l_)

    def yy(step):
        return (y + step + NY) % NY

    def zz(step):
        return (z + step + NZ) % NZ

    def remote(src, dst, ss, rs, target):
        return pltpu.make_async_remote_copy(
            src_ref=src, dst_ref=dst, send_sem=ss, recv_sem=rs, device_id=target, device_id_type=MESH_ID
        )

    def send(src, dst, ss, rs, target):
        remote(src, dst, ss, rs, target).start()

    def drain():
        wholes = (
            (XG.at[0:3], S.tk_s),
            (NS.at[0:3], S.ns_s),
            (S.NG.at[0:3], S.ng_s),
            (NS.at[0:3], S.sm_s),
            (NS.at[0:3], S.dm_s),
            (S.SPG.at[0:3], S.sg_s),
            (S.SPZ.at[0:7], S.sz_s),
            (S.SPY.at[0:3], S.sy_s),
        )
        for whole, ss in wholes:
            remote(whole, whole, ss.at[0], S.rs_s.at[0], dev(h, oc, y, z, l)).wait_send()

    def arrived(dst, ss, rs):
        remote(dst, dst, ss, rs, dev(h, oc, y, z, l)).wait_recv()

    greeted = [dev(h, oc, y, z, l), dev(h, oc, y, z, ol)]
    greeted += [dev(h, c, y, z, ol), dev(oh, c, y, z, l), dev(oh, c, y, z, ol)]
    greeted += [dev(h, c, yy(j), z, l) for j in range(1, NY)]
    greeted += [dev(h, c, y, zz(j), l) for j in range(1, NZ)]
    barrier = pltpu.get_barrier_semaphore()
    for target in greeted:
        pl.semaphore_signal(barrier, inc=1, device_id=target, device_id_type=MESH_ID)

    LA, LB = pl.ds(0, CA), pl.ds(CA, CB)
    Z_ORDER = (4, 3, 5, 2, 6, 1, 7, 0)
    Y_ORDER = (2, 1, -1, 0)
    Z_FINE = (0, 1, -1, 2)
    way_of = {r: i % 2 for i, r in enumerate(Z_ORDER)}
    way_of.update({8: 1, 9: 0})

    def along_z(i, l_):
        return {8: 2 + 4 * l_, 9: 3 + 2 * l_}.get(i, i)

    def along_y(m, i, l_):
        return 2 - 3 * l_ if i == 2 and m in SHARED else Z_FINE[i]


    def ag_copies(m, op, k, i):
        W = S.W
        for way in range(2):
            s = 1 - 2 * way
            if op == AY:
                if k == 1:
                    yield W.at[m, y, z, :, LA], W.at[m, yy(-s), z, :, LA], s
                else:
                    part = pl.ds(way * (CA // 2), CA // 2)
                    yield W.at[m, yy(-s), z, :, part], W.at[m, yy(2), z, :, part], s
            elif op == AZ:
                if k < 4 or way == i:
                    some = pl.ds(2 * i, 2)
                    yield W.at[m, some, zz(-s * (k - 1)), :, LA], W.at[m, some, zz(-s * k), :, LA], s
            elif op == FZ:
                if k < 4 or way == i % 2:
                    at = yy(along_y(m, i, l))
                    yield W.at[m, at, zz(-s * (k - 1)), :, LA], W.at[m, at, zz(-s * k), :, LA], s
            elif op == XZ:
                if k < 4 or way == 0:
                    mine, theirs = yy(along_y(m, 2, l)), yy(along_y(m, 2, ol))
                    yield W.at[m, mine, zz(-s * k), :, LA], W.at[m, theirs, zz(-s * k), :, LA], s
            elif op == XY:
                if k == 1 or way == 0:
                    at = yy(-s) if k == 1 else yy(2)
                    yield W.at[m, at, zz(along_z(i, l)), :, LB], W.at[m, at, zz(along_z(i, ol)), :, LB], s
            elif op == BZ:
                some = pl.ds(0, BLK) if k < 4 else (pl.ds(0, CUT), pl.ds(CUT, BLK - CUT))[way]
                yield W.at[m, y, zz(-s * (k - 1)), some, LB], W.at[m, y, zz(-s * k), some, LB], s
            else:
                some = pl.ds(4 * i, 4) if op == BY else zz(along_z(i, l))
                if k == 1:
                    yield W.at[m, y, some, :, LB], W.at[m, yy(-s), some, :, LB], s
                elif way == (i if op == BY else way_of[i]):
                    yield W.at[m, yy(-s), some, :, LB], W.at[m, yy(2), some, :, LB], s

    def ag_sems(m, op, k, i):
        group = {AY: 0, AZ: 1, FZ: 1, BZ: 2, BY: 3, FY: 3, XY: 4, XZ: 5}[op]
        return S.ag_s.at[m, group], S.ag_r.at[AG_SEMS[m, op, k, i]]

    def ag_go(m, op, k, i=0):
        ss, rs = ag_sems(m, op, k, i)
        for src, _, s in ag_copies(m, op, k, i):
            if op in (XY, XZ):
                target = dev(oh, c, y, z, ol)
            else:
                target = dev(h, c, y, zz(s), l) if op in (AZ, BZ, FZ) else dev(h, c, yy(s), z, l)
            remote(src, src, ss, rs, target).start()

    def ag_got(m, op, k, i=0):
        W = S.W
        ss, rs = ag_sems(m, op, k, i)
        if op == AY:
            both = W.at[m, 0:2, z, :, LA] if k == 1 else W.at[m, 0, z, :, LA]
        elif op == AZ:
            both = W.at[m, :, z, :, LA] if k < 4 else W.at[m, 0:2, z, :, LA]
        elif op in (FZ, XZ):
            both = W.at[m, 0:2, z, :, LA] if k < 4 else W.at[m, 0, z, :, LA]
        elif op == BZ:
            both = W.at[m, 0, 0:2, :, LB] if k < 4 else W.at[m, 0, 0, :, LB]
        elif op == BY:
            both = W.at[m, 0, :, :, LB] if k == 1 else W.at[m, 0, 0:4, :, LB]
        else:
            both = W.at[m, 0, 0:2, :, LB] if k == 1 else W.at[m, 0, 0, :, LB]
        arrived(both, ss, rs)

    def ag_sent(m):
        W = S.W
        wholes = [W.at[m, 0:3, 0, :, LA], W.at[m, :, 0:7, :, LA], W.at[m, 0, 0:7, :, LB], W.at[m, 0:3, :, :, LB]]
        if m in SHARED:
            wholes[1], wholes[3] = W.at[m, 0:3, 0:7, :, LA], W.at[m, 0:3, 0:6, :, LB]
            wholes += [W.at[m, 0, 0:6, :, LB], W.at[m, 0, 0:7, :, LA]]
        for group, whole in enumerate(wholes):
            remote(whole, whole, S.ag_s.at[m, group], S.ag_r.at[0], dev(h, oc, y, z, l)).wait_send()

    XO, XS = S.XO, S.XS

    def x_second(m):
        return remote(XO.at[m], XS.at[m, 1], S.x_s.at[m, 1], S.x_r.at[m, 1], dev(h, c, y, z, 0))

    def x_first(m, slot):
        return remote(XO.at[m], XS.at[m, slot], S.x_s.at[m, 0], S.x_r.at[m, slot], dev(oh, c, y, z, 1))

    def x_prepare():
        for m, codes in enumerate((wg, wt, wc)):
            own = codes[...].astype(F32)
            own = jnp.concatenate([own, jnp.zeros((PAD - HALF, COLS), F32)], axis=0).astype(BF16)
            XO[m] = own

            @pl.when(l == 0)
            def _():
                XS[m, 0] = own

    def x_start(m):
        @pl.when(l == 0)
        def _():
            x_first(m, 0).start()

        @pl.when(l == 1)
        def _():
            x_second(m).start()
            x_first(m, 1).start()

    def assemble(m):
        @pl.when(l == 1)
        def _():
            arrived(XS.at[m, 0], S.x_s.at[m, 0], S.x_r.at[m, 0])

        arrived(XS.at[m, 1], S.x_s.at[m, 1], S.x_r.at[m, 1])
        both = [XS[m, i].astype(F32)[:HALF] for i in range(2)]
        S.W[m, y, z] = jnp.concatenate(both, axis=0).astype(BF16)

    XG, NS, SC = S.XG, S.NS, S.SC
    tok_own = pltpu.make_async_copy(gi, XG.at[q], S.tk_s.at[1])

    def tok_near():
        send(gi, XG.at[q], S.tk_s.at[0], S.tk_r.at[1], dev(h, oc, y, z, l))

    def tok_far():
        send(gi, XG.at[q], S.tk_s.at[0], S.tk_r.at[0], dev(h, c, y, z, ol))

    def tok_forward():
        arrived(XG.at[q_far], S.tk_s.at[0], S.tk_r.at[0])
        send(XG.at[q_far], XG.at[q_far], S.tk_s.at[0], S.tk_r.at[2], dev(h, oc, y, z, l))

    q_far, q_near, q_last = 2 * ol + c, 2 * l + oc, 2 * ol + oc

    def columns(c_, l_):
        return pl.ds(pl.multiple_of((2 * ((h + l_) % 2) + c_) * COLS, COLS), COLS)

    others = ((oc, l), (c, ol), (oc, ol))

    def noise_send(i):
        c_, l_ = others[i]
        send(noise.at[:, columns(c_, l_)], NS.at[q], S.ns_s.at[0], S.ns_r.at[0], dev(h, c_, y, z, l_))

    def noise_wait():
        noise_own.wait()
        arrived(NS.at[0:3], S.ns_s.at[0], S.ns_r.at[0])

    noise_own = pltpu.make_async_copy(noise.at[:, columns(c, l)], NS.at[q], S.ns_s.at[1])

    def scale_copy():
        return remote(scales, SC, S.sc_s.at[0], S.sc_r.at[0], dev(oh, c, y, z, 1))

    def scale_own():
        return pltpu.make_async_copy(scales, SC, S.sc_r.at[0])

    def scale_start():
        @pl.when(l == 0)
        def _():
            scale_copy().start()
            scale_own().start()

    def piece(i):
        m, j = i // PIECES, i % PIECES
        if j < 8:
            offset = j * COLS
        else:
            offset = pl.multiple_of(2 * D + cb * COLS, COLS)
        return pltpu.make_async_copy(tproj.at[m, :, pl.ds(offset, TPC)], S.TP.at[i % SLOTS], S.tp_m.at[i % SLOTS])

    def gen_hat(block, part):
        H = S.H

        def rows(r, carry):
            at = pl.ds(pl.multiple_of(part * 32 + r * 16, 16), 16)
            x = XG[block, at, :].astype(F32)
            inv = lax.rsqrt(jnp.sum(x * x, axis=1, keepdims=True) / D + RMS_EPS)
            hat = (x * inv * (1.0 + mod[0, 1:2, :]) + mod[0, 0:1, :]).astype(BF16)
            to = pl.ds(pl.multiple_of(block * ROWS + part * 32 + r * 16, 16), 16)
            for k in range(4):
                H[k, to, :] = hat[:, k * COLS : (k + 1) * COLS]
            return carry

        lax.fori_loop(0, 2, rows, 0)

    def features():
        index = lax.broadcasted_iota(jnp.int32, (1, ROWS), 1).astype(F32)
        frequency = jnp.exp(index * (-math.log(10000.0) / ROWS))
        phase = jnp.full((1, ROWS), dstep[h], jnp.int32).astype(F32) * frequency
        feature = jnp.concatenate([jnp.cos(phase), jnp.sin(phase)], axis=1)
        hi = feature.astype(BF16).astype(F32)
        mid = (feature - hi).astype(BF16).astype(F32)
        low = (feature - hi - mid).astype(BF16).astype(F32)
        row = lax.broadcasted_iota(jnp.int32, (16, 2 * ROWS), 0)
        a, b, d = [jnp.broadcast_to(v, (16, 2 * ROWS)) for v in (hi, mid, low)]
        S.FT[...] = jnp.where(row == 0, a, jnp.where(row == 1, b, jnp.where(row == 2, d, 0.0))).astype(BF16)

    def judge_piece(i):
        m, j = i // PIECES, i % PIECES
        piece(i).wait()
        lifted = jnp.dot(S.FT[...], S.TP[i % SLOTS], preferred_element_type=F32)
        lifted = jnp.sum(lifted, axis=0, keepdims=True)
        if j < 8:
            S.JM[m, j // 4, j % 4] = lifted + mod[m + 1, j // 4 : j // 4 + 1, (j % 4) * COLS : (j % 4 + 1) * COLS]
        else:
            gate = mod[m + 1, 2:3, pl.ds(pl.multiple_of(cb * COLS, COLS), COLS)]
            S.PK[m + 4 : m + 5, :] = lifted + gate
        if i + SLOTS < 2 * PIECES:
            piece(i + SLOTS).start()

    def factors():
        arrived(SC, S.sc_s.at[0], S.sc_r.at[0])
        row = lax.broadcasted_iota(jnp.int32, (8, COLS), 0)
        for m in range(3):
            group = jnp.where(h == 0, sgroup[0:1, m : m + 1], sgroup[1:2, m : m + 1])
            picked = jnp.sum(jnp.where(row == group, SC[m], 0.0), axis=0, keepdims=True)
            if m == 0:
                gate = mod[0, 2:3, pl.ds(pl.multiple_of(cb * COLS, COLS), COLS)]
            else:
                gate = S.PK[m + 3 : m + 4, :]
            S.PK[m : m + 1, :] = gate * picked

    def level():
        return jnp.full((1, COLS), dstep[h], jnp.int32).astype(F32) / 1000.0

    def product(lhs, m, k, first=False):
        ACC = S.ACC
        part = jnp.dot(lhs[k], S.W[m, k].reshape(COLS, COLS), preferred_element_type=F32)
        if first:
            ACC[...] = part
        else:
            ACC[...] += part

    TILE = 64

    def clean_rows(block):
        lev = level()
        here = pl.ds(pl.multiple_of(cb * COLS, COLS), COLS)

        def rows(r, carry):
            at = pl.ds(pl.multiple_of(block * ROWS + r * TILE, TILE), TILE)
            inner = pl.ds(pl.multiple_of(r * TILE, TILE), TILE)
            branch = (S.ACC[at, :] * S.PK[0:1, :]).astype(BF16)
            clean = XG[block, inner, here].astype(F32) + branch.astype(F32)
            noisy = (1.0 - lev) * clean + lev * NS[block, inner, :].astype(F32)
            S.CL[at, :] = clean
            S.NF[at, :] = noisy
            S.SB[at, :] = clean.astype(BF16)
            S.NG[cb, at, :] = noisy.astype(BF16)
            return carry

        lax.fori_loop(0, ROWS // TILE, rows, 0)

    def block_rows(block):
        return pl.ds(block * ROWS, ROWS)

    def noisy_send(block):
        own = S.NG.at[cb, block_rows(block)]
        send(own, own, S.ng_s.at[0], S.ng_r.at[block, 0], dev(h, c, y, z, ol))
        send(own, own, S.ng_s.at[0], S.ng_r.at[block, 1], dev(h, oc, y, z, l))

    far = 2 * ((h + ol) % 2) + c

    def noisy_forward(block):
        got = S.NG.at[far, block_rows(block)]
        arrived(got, S.ng_s.at[0], S.ng_r.at[block, 0])
        send(got, got, S.ng_s.at[0], S.ng_r.at[block, 1], dev(h, oc, y, z, l))

    def noisy_wait(block):
        arrived(S.NG.at[0:2, block_rows(block)], S.ng_s.at[0], S.ng_r.at[block, 1])

    def judge_hats(part):
        NG, JH, JM = S.NG, S.JH, S.JM

        def rows(r, carry):
            at = pl.ds(pl.multiple_of(part * 64 + r * 16, 16), 16)
            v = [NG[k, at, :].astype(F32) for k in range(4)]
            total = sum(jnp.sum(t * t, axis=1, keepdims=True) for t in v)
            inv = lax.rsqrt(total / D + RMS_EPS)
            for k in range(4):
                normed = (v[k] * inv).astype(BF16).astype(F32)
                for j in range(2):
                    JH[j, k, at, :] = (normed * (1.0 + JM[j, 1, k]) + JM[j, 0, k]).astype(BF16)
            return carry

        lax.fori_loop(0, 4, rows, 0)

    def return_rows(buf, out, ss, rs):
        here = pl.ds(pl.multiple_of(cb * COLS, COLS), COLS)
        for i, (c_, l_) in enumerate(others):
            block = pl.ds(pl.multiple_of((2 * l_ + c_) * ROWS, ROWS), ROWS)
            send(buf.at[block], out.at[:, here], ss.at[0], rs.at[0], dev(h, c_, y, z, l_))
        block = pl.ds(pl.multiple_of(q * ROWS, ROWS), ROWS)
        own = pltpu.make_async_copy(buf.at[block], out.at[:, here], ss.at[1])
        own.start()
        return own

    def return_wait(out, ss, rs):
        arrived(NS.at[0:3], ss.at[0], rs.at[0])

    def judged(m, half):
        ACC = S.ACC
        at = pl.ds(half * (GROUP // 2), GROUP // 2)
        for k in range(4):
            part = jnp.dot(S.JH[m - 1, k, at, :], S.W[m, k].reshape(COLS, COLS), preferred_element_type=F32)
            if k == 0:
                ACC[at, :] = part
            else:
                ACC[at, :] += part

    def half_tiles(half, body, carry):
        tiles = GROUP // 2 // TILE
        return lax.fori_loop(half * tiles, (half + 1) * tiles, body, carry)

    def real_rows(half):
        lev = level()

        def rows(r, total):
            at = pl.ds(pl.multiple_of(r * TILE, TILE), TILE)
            real = (S.ACC[at, :] * S.PK[1:2, :]).astype(BF16)
            S.RP[at, :] = real
            noisy = S.NF[at, :]
            gone = jnp.abs(S.CL[at, :] - (noisy - lev * (noisy + real.astype(F32))))
            return total + jnp.sum(gone.reshape(TILE // 8, 8, COLS), axis=0)

        total = half_tiles(half, rows, jnp.zeros((8, COLS), F32))
        total = jnp.sum(jnp.sum(total, axis=1, keepdims=True), axis=0, keepdims=True)
        total = jnp.broadcast_to(total, (8, 128))
        S.SP[...] = total if half == 0 else S.SP[...] + total

    def gap_rows(half):
        lev = level()

        def rows(r, carry):
            at = pl.ds(pl.multiple_of(r * TILE, TILE), TILE)
            fake = (S.ACC[at, :] * S.PK[2:3, :]).astype(BF16).astype(F32)
            gap = lev * (S.RP[at, :].astype(F32) - fake)
            S.GP[at, :] = gap
            S.CT[at, :] = (gap * S.PK[0:1, :]).astype(BF16)
            return carry

        half_tiles(half, rows, 0)

    def spread_group_start():
        S.SPG[q] = S.SP[...]
        for c_, l_ in others:
            send(S.SP, S.SPG.at[q], S.sg_s.at[0], S.sg_r.at[0], dev(h, c_, y, z, l_))

    def spread_z_start():
        SPG, SPZ = S.SPG, S.SPZ
        arrived(SPG.at[0:3], S.sg_s.at[0], S.sg_r.at[0])
        SPZ[z] = (SPG[0] + SPG[1]) + (SPG[2] + SPG[3])
        for j in range(1, NZ):
            send(SPZ.at[z], SPZ.at[z], S.sz_s.at[0], S.sz_r.at[0], dev(h, c, y, zz(j), l))

    def spread_y_start():
        SPZ, SPY = S.SPZ, S.SPY
        arrived(SPZ.at[0:7], S.sz_s.at[0], S.sz_r.at[0])
        total = SPZ[0]
        for j in range(1, NZ):
            total = total + SPZ[j]
        SPY[y] = total
        for j in range(1, NY):
            send(SPY.at[y], SPY.at[y], S.sy_s.at[0], S.sy_r.at[0], dev(h, c, yy(j), z, l))

    def spread_value():
        SPY = S.SPY
        arrived(SPY.at[0:3], S.sy_s.at[0], S.sy_r.at[0])
        total = SPY[0]
        for j in range(1, NY):
            total = total + SPY[j]
        S.SV[...] = total / CLIP_ELEMENTS + SPREAD_EPS

    def dmd_rows():
        def rows(r, carry):
            at = pl.ds(pl.multiple_of(r * TILE, TILE), TILE)
            S.DB[at, :] = (S.GP[at, :] / S.SV[0:1, 0:1]).astype(BF16)
            return carry

        lax.fori_loop(0, GROUP // TILE, rows, 0)

    G = S.G

    def grad(k, lanes, width):
        block = lax.dot_general(S.H[k], S.CT[:, lanes], (((0,), (0,)), ((), ())), preferred_element_type=F32)
        G[k, :, :, lanes] = block.reshape(NZ, BLK, width)

    def grad_b(k):
        grad(k, LB, CB)

    def grad_a(k):
        grad(k, LA, CA)

    def big_y0(r):
        S.Y0S[r] = G[yy(2), zz(r), :, LB].astype(BF16)
        target = dev(h, c, yy(1 - 2 * way_of[r]), z, l)
        remote(S.Y0S.at[r], S.Y0R.at[r], S.rs_s.at[0], S.b0_r.at[r], target).start()

    def big_y1(r):
        for way in range(2):
            s = 1 - 2 * way
            v = G[yy(s), zz(r), :, LB]
            if way == way_of[r]:
                arrived(S.Y0R.at[r], S.rs_s.at[0], S.b0_r.at[r])
                v = v + S.Y0R[r].astype(F32)
            S.Y1S[r, way] = v.astype(BF16)
            remote(S.Y1S.at[r, way], S.Y1R.at[r, way], S.rs_s.at[1], S.b1_r.at[r], dev(h, c, yy(s), z, l)).start()

    def big_y2(r):
        Y1R = S.Y1R
        arrived(Y1R.at[r], S.rs_s.at[1], S.b1_r.at[r])
        G[y, zz(r), :, LB] = G[y, zz(r), :, LB] + Y1R[r, 0].astype(F32) + Y1R[r, 1].astype(F32)

    def slot(k, way):
        return 0 if k == 1 else 2 * k - 3 + way

    def pair(k):
        return pl.ds(slot(k, 0), 1 if k == 1 else 2)

    def big_z(k, j):
        ZS, ZR = S.ZS, S.ZR
        at = yy(Y_ORDER[j])
        if k > 1:
            arrived(ZR.at[pair(k - 1), j], S.rs_s.at[2], S.a_r.at[k - 2, j])
        for way in range(2):
            s = 1 - 2 * way
            if k == 5 or (k == 1 and way != j % 2):
                continue
            v = G[at, zz(s * (5 - k)), :, LA]
            if k > 2 or (k == 2 and way == j % 2):
                v = v + ZR[slot(k - 1, way), j].astype(F32)
            n = slot(k, way)
            ZS[n, j] = v.astype(BF16)
            remote(ZS.at[n, j], ZR.at[n, j], S.rs_s.at[2], S.a_r.at[k - 1, j], dev(h, c, y, zz(s), l)).start()
        if k == 5:
            G[at, z, :, LA] = G[at, z, :, LA] + ZR[5, j].astype(F32) + ZR[6, j].astype(F32)

    def small_y(j):
        ys, yr = S.ys, S.yr
        if j < 3:
            at = yy(Y_ORDER[j])
            ys[j] = G[at, z, :, LA].astype(BF16)
            remote(ys.at[j], yr.at[j], S.rs_s.at[3], S.y_r.at[0], dev(h, c, at, z, l)).start()
        else:
            arrived(yr.at[0:3], S.rs_s.at[3], S.y_r.at[0])
            total = yr[0].astype(F32) + yr[1].astype(F32) + yr[2].astype(F32)
            G[y, z, :, LA] = G[y, z, :, LA] + total

    def small_z(k):
        zs, zr = S.zs, S.zr
        if k > 1:
            arrived(zr.at[0] if k == 2 else zr.at[pair(k - 1)], S.rs_s.at[4], S.z_r.at[k - 2])
        for way in range(2):
            s = 1 - 2 * way
            some = (pl.ds(0, CUT), pl.ds(CUT, BLK - CUT))[way]
            target = dev(h, c, y, zz(s), l)
            n = slot(k, way)
            if k == 1:
                zs[0, some, :] = G[y, zz(4), some, LB].astype(BF16)
                remote(zs.at[0, some], zr.at[0, some], S.rs_s.at[4], S.z_r.at[0], target).start()
            elif k < 5:
                at = zz(s * (5 - k))
                if k > 2:
                    zs[n] = (G[y, at, :, LB] + zr[slot(k - 1, way)].astype(F32)).astype(BF16)
                else:
                    other = (pl.ds(CUT, BLK - CUT), pl.ds(0, CUT))[way]
                    zs[n, some, :] = (G[y, at, some, LB] + zr[0, some, :].astype(F32)).astype(BF16)
                    zs[n, other, :] = G[y, at, other, LB].astype(BF16)
                remote(zs.at[n], zr.at[n], S.rs_s.at[4], S.z_r.at[k - 1], target).start()
        if k == 5:
            G[y, z, :, LB] = G[y, z, :, LB] + zr[5].astype(F32) + zr[6].astype(F32)

    def rings_sent():
        wholes = (S.Y0S, S.Y1S, S.ZS.at[0:7], S.ys.at[0:3], S.zs.at[0:7])
        for i, whole in enumerate(wholes):
            remote(whole, whole, S.rs_s.at[i], S.b0_r.at[0], dev(h, oc, y, z, l)).wait_send()

    tok_own.start()
    noise_own.start()
    for i in range(SLOTS):
        piece(i).start()
    x_prepare()
    features()
    pl.semaphore_wait(barrier, len(greeted))
    x_start(0)
    x_start(1)
    x_start(2)
    tok_near()
    scale_start()
    tok_own.wait()
    gen_hat(q, 0)
    gen_hat(q, 1)
    gen_hat(q, 2)
    gen_hat(q, 3)
    judge_piece(0)
    judge_piece(1)
    judge_piece(2)
    judge_piece(3)
    judge_piece(4)
    judge_piece(5)
    judge_piece(6)
    judge_piece(7)
    judge_piece(8)
    judge_piece(9)
    judge_piece(10)
    judge_piece(11)
    judge_piece(12)
    judge_piece(13)
    judge_piece(14)
    assemble(0)
    ag_go(0, AY, 1)
    ag_go(0, BZ, 1)
    ag_go(0, FZ, 1, 0)
    ag_go(0, FY, 1, 0)
    judge_piece(15)
    arrived(XG.at[q_near], S.tk_s.at[0], S.tk_r.at[1])
    gen_hat(q_near, 0)
    gen_hat(q_near, 1)
    gen_hat(q_near, 2)
    gen_hat(q_near, 3)
    judge_piece(16)
    judge_piece(17)
    assemble(1)
    ag_go(1, AY, 1)
    ag_go(1, BZ, 1)
    ag_go(1, FZ, 1, 0)
    ag_go(1, FY, 1, 0)
    ag_got(0, AY, 1)
    ag_go(0, AY, 2)
    ag_go(0, FZ, 1, 1)
    ag_go(0, FZ, 1, 2)
    ag_got(0, BZ, 1)
    ag_go(0, BZ, 2)
    ag_go(0, FY, 1, 1)
    ag_go(0, FY, 1, 7)
    ag_got(0, FY, 1, 0)
    ag_go(0, FY, 2, 0)
    ag_got(0, FZ, 1, 0)
    ag_go(0, FZ, 2, 0)
    tok_far()
    assemble(2)
    factors()
    ag_go(2, AY, 1)
    ag_got(1, BZ, 1)
    ag_go(1, BZ, 2)
    ag_got(0, AY, 2)
    ag_go(0, FZ, 1, 3)
    ag_got(1, AY, 1)
    ag_go(1, AY, 2)
    ag_got(0, FZ, 1, 1)
    ag_go(0, FZ, 2, 1)
    ag_got(0, FY, 1, 1)
    ag_go(0, FY, 2, 1)
    ag_go(1, FY, 1, 1)
    ag_got(0, FZ, 1, 2)
    ag_go(0, FZ, 2, 2)
    ag_got(0, FY, 1, 7)
    ag_go(0, FY, 2, 7)
    ag_got(0, BZ, 2)
    ag_go(0, BZ, 3)
    ag_go(0, FY, 1, 2)
    ag_go(0, FY, 1, 6)
    ag_got(0, FZ, 2, 0)
    ag_go(0, FZ, 3, 0)
    ag_got(0, FZ, 1, 3)
    ag_go(0, FZ, 2, 3)
    ag_got(2, AY, 1)
    ag_go(2, AY, 2)
    ag_got(1, BZ, 2)
    ag_go(1, FY, 1, 8)
    ag_go(1, BZ, 3)
    ag_got(0, FZ, 2, 1)
    ag_go(0, FZ, 3, 1)
    ag_got(0, FZ, 2, 2)
    ag_go(0, FZ, 3, 2)
    ag_got(0, FY, 1, 2)
    ag_go(0, FY, 2, 2)
    ag_go(1, FY, 1, 7)
    ag_got(0, BZ, 3)
    ag_go(0, BZ, 4)
    ag_go(0, FY, 1, 3)
    ag_go(0, FY, 1, 5)
    ag_got(0, FZ, 3, 0)
    ag_go(0, FZ, 4, 0)
    ag_got(0, FY, 1, 6)
    ag_go(0, FY, 2, 6)
    ag_got(0, FZ, 2, 3)
    ag_go(0, FZ, 3, 3)
    ag_got(1, FY, 1, 8)
    ag_go(1, XY, 1, 8)
    ag_got(1, AY, 2)
    ag_go(1, FZ, 1, 2)
    ag_got(0, FZ, 3, 1)
    ag_go(0, FZ, 4, 1)
    tok_forward()
    noise_send(0)
    noise_send(1)
    noise_send(2)
    ag_got(1, BZ, 3)
    ag_go(1, BZ, 4)
    ag_go(1, FY, 1, 9)
    ag_got(0, FZ, 3, 2)
    ag_go(0, FZ, 4, 2)
    gen_hat(q_far, 0)
    gen_hat(q_far, 1)
    ag_go(1, FY, 2, 8)
    ag_got(1, FZ, 1, 0)
    ag_go(1, FZ, 2, 0)
    gen_hat(q_far, 2)
    ag_got(0, BZ, 4)
    ag_go(0, FY, 1, 4)
    gen_hat(q_far, 3)
    ag_got(0, FY, 1, 3)
    ag_go(0, FY, 2, 3)
    ag_got(0, FZ, 3, 3)
    ag_go(0, FZ, 4, 3)
    ag_go(1, FZ, 1, 1)
    ag_got(0, FY, 1, 5)
    ag_go(0, FY, 2, 5)
    ag_got(1, FZ, 1, 2)
    ag_go(1, FZ, 2, 2)
    ag_go(1, XZ, 1)
    ag_got(1, BZ, 4)
    ag_go(1, FY, 1, 4)
    ag_go(2, BZ, 1)
    arrived(XG.at[q_last], S.tk_s.at[0], S.tk_r.at[2])
    gen_hat(q_last, 0)
    ag_got(1, FY, 1, 9)
    ag_go(1, XY, 1, 9)
    gen_hat(q_last, 1)
    ag_got(2, AY, 2)
    ag_go(2, FZ, 1, 2)
    gen_hat(q_last, 2)
    ag_go(1, FY, 2, 9)
    ag_got(1, FY, 2, 8)
    ag_go(1, XY, 2, 8)
    gen_hat(q_last, 3)
    ag_got(0, FZ, 4, 0)
    product(S.H, 0, y, True)
    ag_got(1, FZ, 2, 0)
    ag_go(1, FZ, 3, 0)
    ag_got(1, FY, 1, 0)
    ag_go(1, FY, 2, 0)
    ag_got(0, FY, 1, 4)
    ag_go(0, FY, 2, 4)
    ag_got(0, FZ, 4, 1)
    product(S.H, 0, yy(1))
    ag_got(1, FZ, 1, 1)
    ag_go(1, FZ, 2, 1)
    ag_got(1, FY, 1, 1)
    ag_go(1, FY, 2, 1)
    ag_got(0, FZ, 4, 2)
    product(S.H, 0, yy(-1))
    ag_got(1, FZ, 2, 2)
    ag_go(1, FZ, 3, 2)
    ag_go(1, XZ, 2)
    ag_got(1, FY, 1, 7)
    ag_go(1, FY, 2, 7)
    ag_go(2, FZ, 1, 0)
    ag_go(2, FY, 1, 0)
    ag_got(2, BZ, 1)
    ag_go(2, BZ, 2)
    ag_got(2, FZ, 1, 2)
    ag_go(2, XZ, 1)
    ag_got(1, FY, 2, 9)
    ag_go(1, XY, 2, 9)
    ag_got(1, FY, 1, 4)
    ag_go(1, FY, 2, 4)
    ag_got(1, FZ, 3, 0)
    ag_go(1, FZ, 4, 0)
    ag_go(2, FY, 1, 1)
    ag_go(2, FZ, 2, 2)
    ag_got(0, FZ, 4, 3)
    ag_got(0, FY, 2, 0)
    ag_got(0, FY, 2, 1)
    ag_got(0, FY, 2, 7)
    ag_got(0, FY, 2, 2)
    ag_got(0, FY, 2, 6)
    ag_got(0, FY, 2, 3)
    ag_got(0, FY, 2, 5)
    ag_got(0, FY, 2, 4)
    product(S.H, 0, yy(2))
    ag_got(1, FZ, 2, 1)
    ag_go(1, FZ, 3, 1)
    ag_go(2, FY, 1, 7)
    noise_wait()
    clean_rows(0)
    noisy_send(0)
    clean_rows(1)
    noisy_send(1)
    ag_got(1, FZ, 3, 2)
    ag_go(1, XZ, 3)
    clean_rows(2)
    noisy_send(2)
    clean_rows(3)
    noisy_send(3)
    ag_go(1, FZ, 4, 2)
    ag_got(2, FZ, 1, 0)
    ag_go(2, FZ, 2, 0)
    ag_got(2, FY, 1, 0)
    ag_go(2, FY, 2, 0)
    ag_go(2, FZ, 1, 1)
    ag_got(2, BZ, 2)
    ag_go(2, FY, 1, 8)
    ag_go(2, BZ, 3)
    ag_got(2, FY, 1, 1)
    ag_go(2, FY, 2, 1)
    ag_got(2, FZ, 2, 2)
    ag_go(2, XZ, 2)
    ag_got(1, FZ, 3, 1)
    ag_go(1, FZ, 4, 1)
    ag_go(2, FZ, 3, 2)
    ag_got(2, FY, 1, 7)
    ag_go(2, FY, 2, 7)
    ag_got(1, FZ, 4, 2)
    ag_go(1, XZ, 4)
    noisy_forward(0)
    ag_got(2, FZ, 2, 0)
    ag_go(2, FZ, 3, 0)
    ag_got(2, FZ, 1, 1)
    ag_go(2, FZ, 2, 1)
    ag_got(2, FY, 1, 8)
    ag_go(2, FY, 2, 8)
    ag_go(2, XY, 1, 8)
    noisy_wait(0)
    judge_hats(0)
    ag_got(2, BZ, 3)
    ag_go(2, BZ, 4)
    ag_go(2, FY, 1, 9)
    judge_hats(1)
    noisy_forward(1)
    ag_got(2, FZ, 3, 2)
    ag_go(2, FZ, 4, 2)
    ag_go(2, XZ, 3)
    ag_got(2, FY, 2, 8)
    ag_go(2, XY, 2, 8)
    ag_got(2, FZ, 3, 0)
    ag_go(2, FZ, 4, 0)
    ag_got(2, FZ, 2, 1)
    ag_go(2, FZ, 3, 1)
    noisy_wait(1)
    judge_hats(2)
    ag_got(2, FY, 1, 9)
    ag_go(2, FY, 2, 9)
    ag_got(2, FZ, 4, 2)
    ag_go(2, XZ, 4)
    ag_go(2, XY, 1, 9)
    ag_got(2, BZ, 4)
    ag_go(2, FY, 1, 4)
    judge_hats(3)
    noisy_forward(2)
    ag_got(1, FZ, 4, 0)
    ag_got(1, FZ, 4, 1)
    ag_got(1, XY, 1, 8)
    ag_got(1, XY, 1, 9)
    ag_got(1, XZ, 1)
    ag_got(1, XZ, 2)
    ag_got(1, XZ, 3)
    ag_got(1, XZ, 4)
    ag_got(1, XY, 2, 8)
    ag_got(1, XY, 2, 9)
    ag_got(1, FY, 2, 0)
    ag_got(1, FY, 2, 1)
    ag_got(1, FY, 2, 7)
    ag_got(1, FY, 2, 4)
    judged(1, 0)
    ag_got(2, FZ, 3, 1)
    ag_go(2, FZ, 4, 1)
    real_rows(0)
    ag_got(2, FY, 2, 9)
    ag_go(2, XY, 2, 9)
    noisy_wait(2)
    judge_hats(4)
    noisy_forward(3)
    ag_got(2, FY, 1, 4)
    ag_go(2, FY, 2, 4)
    judge_hats(5)
    noisy_wait(3)
    judge_hats(6)
    judge_hats(7)
    judged(1, 1)
    real_rows(1)
    spread_group_start()
    ag_got(2, FZ, 4, 0)
    ag_got(2, FZ, 4, 1)
    ag_got(2, XY, 1, 8)
    ag_got(2, XY, 1, 9)
    ag_got(2, XZ, 1)
    ag_got(2, XZ, 2)
    ag_got(2, XZ, 3)
    ag_got(2, XZ, 4)
    ag_got(2, XY, 2, 8)
    ag_got(2, XY, 2, 9)
    ag_got(2, FY, 2, 0)
    ag_got(2, FY, 2, 1)
    ag_got(2, FY, 2, 7)
    ag_got(2, FY, 2, 4)
    judged(2, 0)
    gap_rows(0)
    judged(2, 1)
    sample_own = return_rows(S.SB, out_s, S.sm_s, S.sm_r)
    gap_rows(1)
    grad_b(yy(2))
    big_y0(4)
    big_y0(3)
    big_y0(5)
    big_y0(2)
    grad_a(yy(2))
    big_z(1, 0)
    grad_b(yy(1))
    grad_b(yy(-1))
    spread_z_start()
    grad_a(yy(1))
    big_z(1, 1)
    grad_a(yy(-1))
    big_z(1, 2)
    big_y1(4)
    big_z(2, 0)
    big_y1(3)
    big_y0(6)
    big_y0(1)
    grad_a(y)
    big_z(1, 3)
    big_z(2, 1)
    big_y1(5)
    big_z(2, 2)
    big_y1(2)
    big_y0(7)
    big_y0(0)
    grad_b(y)
    spread_y_start()
    big_z(2, 3)
    big_z(3, 0)
    big_y2(4)
    small_z(1)
    big_y1(6)
    big_z(3, 1)
    spread_value()
    dmd_rows()
    dmd_own = return_rows(S.DB, out_d, S.dm_s, S.dm_r)
    big_y2(3)
    big_y2(5)
    big_z(3, 2)
    small_z(2)
    big_z(3, 3)
    big_y1(1)
    big_z(4, 0)
    big_y1(7)
    big_z(4, 1)
    big_y1(0)
    big_y2(2)
    big_y2(6)
    big_z(4, 2)
    small_z(3)
    big_z(4, 3)
    big_z(5, 0)
    small_y(0)
    big_y2(1)
    big_y2(7)
    small_z(4)
    big_z(5, 1)
    small_y(1)
    big_z(5, 2)
    small_y(2)
    ag_sent(0)
    ag_sent(1)
    ag_sent(2)
    sample_own.wait()
    big_z(5, 3)
    big_y2(0)
    small_y(3)
    small_z(5)
    GF, OW = S.GF, S.OW
    done = G[y, z] / S.SV[0:1, 0:1] / TOKENS

    def own_row(row, slot, target):
        return remote(GF.at[row], OW.at[slot], S.ow_s.at[row], S.ow_r.at[slot], target)

    for row in range(2):
        part = jnp.concatenate([done[row * HALF : (row + 1) * HALF], jnp.zeros((PAD - HALF, COLS), F32)], axis=0)
        GF[row] = part.astype(BF16)

    @pl.when(l == 0)
    def _():
        own_row(1, 0, dev(h, c, y, z, 1)).start()
        OW[0] = GF[0]

    @pl.when(l == 1)
    def _():
        own_row(0, 1, dev(oh, c, y, z, 0)).start()
        own_row(1, 1, dev(oh, c, y, z, 1)).start()
        arrived(OW.at[0], S.ow_s.at[0], S.ow_r.at[0])

    arrived(OW.at[1], S.ow_s.at[1], S.ow_r.at[1])
    out_w[...] = (OW[0].astype(F32) + OW[1].astype(F32))[:HALF]
    return_wait(out_s, S.sm_s, S.sm_r)
    return_wait(out_d, S.dm_s, S.dm_r)
    dmd_own.wait()
    rings_sent()
    drain()
    for m in range(3):
        x_first(m, 0).wait_send()

    @pl.when(l == 0)
    def _():
        scale_copy().wait_send()
        own_row(1, 0, dev(h, c, y, z, 1)).wait_send()

    @pl.when(l == 1)
    def _():
        for m in range(3):
            x_second(m).wait_send()
        own_row(0, 1, dev(oh, c, y, z, 0)).wait_send()
        own_row(1, 1, dev(oh, c, y, z, 1)).wait_send()


def copy_results(a_in, b_in, c_in, a_out, b_out, c_out):
    a_out[...] = a_in[...]
    b_out[...] = b_in[...]
    c_out[...] = c_in[...]


def on_device(gi, noise, dmd_step, scale_group, wg, wt, wc, scales, mod, tproj):
    vmem = pl.BlockSpec(memory_space=pltpu.VMEM)
    smem = pl.BlockSpec(memory_space=pltpu.SMEM)
    hbm = pl.BlockSpec(memory_space=pl.ANY)
    out_shape = (
        jax.ShapeDtypeStruct((ROWS, D), BF16),
        jax.ShapeDtypeStruct((ROWS, D), BF16),
        jax.ShapeDtypeStruct((HALF, COLS), F32),
    )
    results = pl.pallas_call(
        kernel,
        out_shape=out_shape,
        in_specs=[hbm, hbm, smem, vmem, vmem, vmem, vmem, hbm, vmem, hbm],
        out_specs=(hbm, hbm, vmem),
        scratch_shapes=list(scratch_table().values()),
        compiler_params=pltpu.CompilerParams(
            collective_id=0, has_side_effects=True, vmem_limit_bytes=64 * 1024 * 1024 - 65536
        ),
    )(gi, noise, dmd_step, scale_group.T, wg, wt, wc, scales, mod, tproj)
    half = pl.BlockSpec((ROWS // 2, D), lambda i: (i, 0))
    whole = pl.BlockSpec((HALF, COLS), lambda i: (0, 0))
    return pl.pallas_call(
        copy_results,
        grid=(2,),
        out_shape=out_shape,
        in_specs=[half, half, whole],
        out_specs=(half, half, whole),
    )(*results)


def solution(mesh):
    return jax.shard_map(
        on_device,
        mesh=mesh,
        in_specs=(
            P(("dp", "fsdp"), None),
            P(("dp", "fsdp"), None),
            P(),
            P(),
            P("fsdp", "dp"),
            P("fsdp", "dp"),
            P("fsdp", "dp"),
            P(None, None, "dp"),
            P(),
            P(),
        ),
        out_specs=(P(("dp", "fsdp"), None), P(("dp", "fsdp"), None), P("fsdp", "dp")),
        check_vma=False,
    )
```

```python
import functools
import math
import types

import jax
import jax.numpy as jnp
from jax import lax
from jax.experimental import pallas as pl
from jax.experimental.pallas import tpu as pltpu
from jax.sharding import PartitionSpec as P

RMS_EPS = 1e-06
SPREAD_EPS = 1e-05
F32 = jnp.float32
BF16 = jnp.bfloat16
MESH_ID = pl.DeviceIdType.MESH

NY, NZ = 4, 8
D = 2560
COLS = 640
ROWS = 128
GROUP = 4 * ROWS
HALF = 40
PAD = 48
BLK = 80
CA = 256
CB = COLS - CA
CUT = 48
TOKENS = 32768
CLIP_ELEMENTS = 16384 * 2560
TPC = 640
PIECES = 9
SLOTS = 4
AY, AZ, BZ, BY, FY, FZ, XY, XZ = range(8)
FINE_Y, FINE_Z = (0, 1, 2), (0, 1, 2)
SHARED = (1, 2)


def ag_table():
    steps = []
    for m in range(3):
        steps += [(m, AY, k, 0) for k in (1, 2)] + [(m, BZ, k, 0) for k in (1, 2, 3, 4)]
        if m in SHARED:
            steps += [(m, FZ, k, i) for k in (1, 2, 3, 4) for i in range(3)] + [(m, XZ, k, 0) for k in (1, 2, 3, 4)]
            steps += [(m, FY, k, i) for k in (1, 2) for i in (0, 1, 7, 4, 8, 9)] + [(m, XY, k, i) for k in (1, 2) for i in (8, 9)]
            continue
        steps += [(m, FZ, k, i) for k in (1, 2, 3, 4) for i in range(4)] if m in FINE_Z else [(m, AZ, k, i) for k in (1, 2, 3, 4) for i in range(2)]
        steps += [(m, FY, k, i) for k in (1, 2) for i in range(8)] if m in FINE_Y else [(m, BY, k, i) for k in (1, 2) for i in range(2)]
    return {step: n for n, step in enumerate(steps)}


AG_SEMS = ag_table()


def scratch_table():
    vmem, dma = pltpu.VMEM, pltpu.SemaphoreType.DMA
    return dict(
        W=vmem((3, NY, NZ, BLK, COLS), BF16),
        XO=vmem((3, PAD, COLS), BF16),
        XS=vmem((3, 2, PAD, COLS), BF16),
        XG=vmem((4, ROWS, D), BF16),
        H=vmem((4, GROUP, COLS), BF16),
        NS=vmem((4, ROWS, COLS), BF16),
        CL=vmem((GROUP, COLS), F32),
        NF=vmem((GROUP, COLS), F32),
        NG=vmem((4, GROUP, COLS), BF16),
        JH=vmem((2, 4, GROUP, COLS), BF16),
        ACC=vmem((GROUP, COLS), F32),
        RP=vmem((GROUP, COLS), BF16),
        GP=vmem((GROUP, COLS), F32),
        CT=vmem((GROUP, COLS), BF16),
        SB=vmem((GROUP, COLS), BF16),
        DB=vmem((GROUP, COLS), BF16),
        G=vmem((NY, NZ, BLK, COLS), F32),
        ZS=vmem((8, NY, BLK, CA), BF16),
        ZR=vmem((8, NY, BLK, CA), BF16),
        Y0S=vmem((NZ, BLK, CB), BF16),
        Y0R=vmem((NZ, BLK, CB), BF16),
        Y1S=vmem((NZ, 2, BLK, CB), BF16),
        Y1R=vmem((NZ, 2, BLK, CB), BF16),
        ys=vmem((4, BLK, CA), BF16),
        yr=vmem((4, BLK, CA), BF16),
        zs=vmem((8, BLK, CB), BF16),
        zr=vmem((8, BLK, CB), BF16),
        SC=vmem((3, 8, COLS), F32),
        PK=vmem((8, COLS), F32),
        TP=vmem((SLOTS, 2 * ROWS, TPC), BF16),
        FT=vmem((16, 2 * ROWS), BF16),
        JM=vmem((2, 2, 4, 1, COLS), F32),
        SP=vmem((8, 128), F32),
        SV=vmem((8, 128), F32),
        SPG=vmem((4, 8, 128), F32),
        SPZ=vmem((NZ, 8, 128), F32),
        SPY=vmem((NY, 8, 128), F32),
        GF=vmem((2, PAD, COLS), BF16),
        OW=vmem((2, PAD, COLS), BF16),
        ag_s=dma((3, 6)),
        ag_r=dma((len(AG_SEMS),)),
        x_s=dma((3, 2)),
        x_r=dma((3, 2)),
        tk_s=dma((2,)),
        tk_r=dma((3,)),
        ns_s=dma((2,)),
        ns_r=dma((1,)),
        ng_s=dma((1,)),
        ng_r=dma((4, 2)),
        sm_s=dma((2,)),
        sm_r=dma((1,)),
        dm_s=dma((2,)),
        dm_r=dma((1,)),
        sc_s=dma((1,)),
        sc_r=dma((1,)),
        tp_m=dma((SLOTS,)),
        sg_s=dma((1,)),
        sg_r=dma((1,)),
        sz_s=dma((1,)),
        sz_r=dma((1,)),
        sy_s=dma((1,)),
        sy_r=dma((1,)),
        rs_s=dma((5,)),
        b0_r=dma((NZ,)),
        b1_r=dma((NZ,)),
        a_r=dma((4, NY)),
        y_r=dma((1,)),
        z_r=dma((4,)),
        ow_s=dma((2,)),
        ow_r=dma((2,)),
    )


NAMES = tuple(scratch_table())


def kernel(gi, noise, dstep, sgroup, wg, wt, wc, scales, mod, tproj, out_s, out_d, out_w, *rest):
    S = types.SimpleNamespace(**dict(zip(NAMES, rest)))
    dp, fs = lax.axis_index("dp"), lax.axis_index("fsdp")
    h, c = dp // 2, dp % 2
    l, plane = fs % 2, fs // 2
    y, z = plane // NZ, plane % NZ
    oh, oc, ol = 1 - h, 1 - c, 1 - l
    q = 2 * l + c
    cb = 2 * ((h + l) % 2) + c

    def dev(h_, c_, y_, z_, l_):
        return (2 * h_ + c_, (y_ * NZ + z_) * 2 + l_)

    def yy(step):
        return (y + step + NY) % NY

    def zz(step):
        return (z + step + NZ) % NZ

    def remote(src, dst, ss, rs, target):
        return pltpu.make_async_remote_copy(
            src_ref=src, dst_ref=dst, send_sem=ss, recv_sem=rs, device_id=target, device_id_type=MESH_ID
        )

    def send(src, dst, ss, rs, target):
        remote(src, dst, ss, rs, target).start()

    def drain():
        wholes = (
            (XG.at[0:3], S.tk_s),
            (NS.at[0:3], S.ns_s),
            (S.NG.at[0:3], S.ng_s),
            (NS.at[0:3], S.sm_s),
            (NS.at[0:3], S.dm_s),
            (S.SPG.at[0:3], S.sg_s),
            (S.SPZ.at[0:7], S.sz_s),
            (S.SPY.at[0:3], S.sy_s),
        )
        for whole, ss in wholes:
            remote(whole, whole, ss.at[0], S.rs_s.at[0], dev(h, oc, y, z, l)).wait_send()

    def arrived(dst, ss, rs):
        remote(dst, dst, ss, rs, dev(h, oc, y, z, l)).wait_recv()

    greeted = [dev(h, oc, y, z, l), dev(h, oc, y, z, ol)]
    greeted += [dev(h, c, y, z, ol), dev(oh, c, y, z, l), dev(oh, c, y, z, ol)]
    greeted += [dev(h, c, yy(j), z, l) for j in range(1, NY)]
    greeted += [dev(h, c, y, zz(j), l) for j in range(1, NZ)]
    barrier = pltpu.get_barrier_semaphore()
    for target in greeted:
        pl.semaphore_signal(barrier, inc=1, device_id=target, device_id_type=MESH_ID)

    LA, LB = pl.ds(0, CA), pl.ds(CA, CB)
    Z_ORDER = (4, 3, 5, 2, 6, 1, 7, 0)
    Y_ORDER = (2, 1, -1, 0)
    Z_FINE = (0, 1, -1, 2)
    way_of = {r: i % 2 for i, r in enumerate(Z_ORDER)}
    way_of.update({8: 1, 9: 0})

    def along_z(i, l_):
        return {8: 2 + 4 * l_, 9: 3 + 2 * l_}.get(i, i)

    def along_y(m, i, l_):
        return 2 - 3 * l_ if i == 2 and m in SHARED else Z_FINE[i]


    def ag_copies(m, op, k, i):
        W = S.W
        for way in range(2):
            s = 1 - 2 * way
            if op == AY:
                if k == 1:
                    yield W.at[m, y, z, :, LA], W.at[m, yy(-s), z, :, LA], s
                else:
                    part = pl.ds(way * (CA // 2), CA // 2)
                    yield W.at[m, yy(-s), z, :, part], W.at[m, yy(2), z, :, part], s
            elif op == AZ:
                if k < 4 or way == i:
                    some = pl.ds(2 * i, 2)
                    yield W.at[m, some, zz(-s * (k - 1)), :, LA], W.at[m, some, zz(-s * k), :, LA], s
            elif op == FZ:
                if k < 4 or way == i % 2:
                    at = yy(along_y(m, i, l))
                    yield W.at[m, at, zz(-s * (k - 1)), :, LA], W.at[m, at, zz(-s * k), :, LA], s
            elif op == XZ:
                if k < 4 or way == 0:
                    mine, theirs = yy(along_y(m, 2, l)), yy(along_y(m, 2, ol))
                    yield W.at[m, mine, zz(-s * k), :, LA], W.at[m, theirs, zz(-s * k), :, LA], s
            elif op == XY:
                if k == 1 or way == 0:
                    at = yy(-s) if k == 1 else yy(2)
                    yield W.at[m, at, zz(along_z(i, l)), :, LB], W.at[m, at, zz(along_z(i, ol)), :, LB], s
            elif op == BZ:
                some = pl.ds(0, BLK) if k < 4 else (pl.ds(0, CUT), pl.ds(CUT, BLK - CUT))[way]
                yield W.at[m, y, zz(-s * (k - 1)), some, LB], W.at[m, y, zz(-s * k), some, LB], s
            else:
                some = pl.ds(4 * i, 4) if op == BY else zz(along_z(i, l))
                if k == 1:
                    yield W.at[m, y, some, :, LB], W.at[m, yy(-s), some, :, LB], s
                elif way == (i if op == BY else way_of[i]):
                    yield W.at[m, yy(-s), some, :, LB], W.at[m, yy(2), some, :, LB], s

    def ag_sems(m, op, k, i):
        group = {AY: 0, AZ: 1, FZ: 1, BZ: 2, BY: 3, FY: 3, XY: 4, XZ: 5}[op]
        return S.ag_s.at[m, group], S.ag_r.at[AG_SEMS[m, op, k, i]]

    def ag_go(m, op, k, i=0):
        ss, rs = ag_sems(m, op, k, i)
        for src, _, s in ag_copies(m, op, k, i):
            if op in (XY, XZ):
                target = dev(oh, c, y, z, ol)
            else:
                target = dev(h, c, y, zz(s), l) if op in (AZ, BZ, FZ) else dev(h, c, yy(s), z, l)
            remote(src, src, ss, rs, target).start()

    def ag_got(m, op, k, i=0):
        W = S.W
        ss, rs = ag_sems(m, op, k, i)
        if op == AY:
            both = W.at[m, 0:2, z, :, LA] if k == 1 else W.at[m, 0, z, :, LA]
        elif op == AZ:
            both = W.at[m, :, z, :, LA] if k < 4 else W.at[m, 0:2, z, :, LA]
        elif op in (FZ, XZ):
            both = W.at[m, 0:2, z, :, LA] if k < 4 else W.at[m, 0, z, :, LA]
        elif op == BZ:
            both = W.at[m, 0, 0:2, :, LB] if k < 4 else W.at[m, 0, 0, :, LB]
        elif op == BY:
            both = W.at[m, 0, :, :, LB] if k == 1 else W.at[m, 0, 0:4, :, LB]
        else:
            both = W.at[m, 0, 0:2, :, LB] if k == 1 else W.at[m, 0, 0, :, LB]
        arrived(both, ss, rs)

    def ag_sent(m):
        W = S.W
        wholes = [W.at[m, 0:3, 0, :, LA], W.at[m, :, 0:7, :, LA], W.at[m, 0, 0:7, :, LB], W.at[m, 0:3, :, :, LB]]
        if m in SHARED:
            wholes[1], wholes[3] = W.at[m, 0:3, 0:7, :, LA], W.at[m, 0:3, 0:6, :, LB]
            wholes += [W.at[m, 0, 0:6, :, LB], W.at[m, 0, 0:7, :, LA]]
        for group, whole in enumerate(wholes):
            remote(whole, whole, S.ag_s.at[m, group], S.ag_r.at[0], dev(h, oc, y, z, l)).wait_send()

    XO, XS = S.XO, S.XS

    def x_second(m):
        return remote(XO.at[m], XS.at[m, 1], S.x_s.at[m, 1], S.x_r.at[m, 1], dev(h, c, y, z, 0))

    def x_first(m, slot):
        return remote(XO.at[m], XS.at[m, slot], S.x_s.at[m, 0], S.x_r.at[m, slot], dev(oh, c, y, z, 1))

    def x_prepare():
        for m, codes in enumerate((wg, wt, wc)):
            own = codes[...].astype(F32)
            own = jnp.concatenate([own, jnp.zeros((PAD - HALF, COLS), F32)], axis=0).astype(BF16)
            XO[m] = own

            @pl.when(l == 0)
            def _():
                XS[m, 0] = own

    def x_start(m):
        @pl.when(l == 0)
        def _():
            x_first(m, 0).start()

        @pl.when(l == 1)
        def _():
            x_second(m).start()
            x_first(m, 1).start()

    def assemble(m):
        @pl.when(l == 1)
        def _():
            arrived(XS.at[m, 0], S.x_s.at[m, 0], S.x_r.at[m, 0])

        arrived(XS.at[m, 1], S.x_s.at[m, 1], S.x_r.at[m, 1])
        both = [XS[m, i].astype(F32)[:HALF] for i in range(2)]
        S.W[m, y, z] = jnp.concatenate(both, axis=0).astype(BF16)

    XG, NS, SC = S.XG, S.NS, S.SC
    tok_own = pltpu.make_async_copy(gi, XG.at[q], S.tk_s.at[1])

    def tok_near():
        send(gi, XG.at[q], S.tk_s.at[0], S.tk_r.at[1], dev(h, oc, y, z, l))

    def tok_far():
        send(gi, XG.at[q], S.tk_s.at[0], S.tk_r.at[0], dev(h, c, y, z, ol))

    def tok_forward():
        arrived(XG.at[q_far], S.tk_s.at[0], S.tk_r.at[0])
        send(XG.at[q_far], XG.at[q_far], S.tk_s.at[0], S.tk_r.at[2], dev(h, oc, y, z, l))

    q_far, q_near, q_last = 2 * ol + c, 2 * l + oc, 2 * ol + oc

    def columns(c_, l_):
        return pl.ds(pl.multiple_of((2 * ((h + l_) % 2) + c_) * COLS, COLS), COLS)

    others = ((oc, l), (c, ol), (oc, ol))

    def noise_send(i):
        c_, l_ = others[i]
        send(noise.at[:, columns(c_, l_)], NS.at[q], S.ns_s.at[0], S.ns_r.at[0], dev(h, c_, y, z, l_))

    def noise_wait():
        noise_own.wait()
        arrived(NS.at[0:3], S.ns_s.at[0], S.ns_r.at[0])

    noise_own = pltpu.make_async_copy(noise.at[:, columns(c, l)], NS.at[q], S.ns_s.at[1])

    def scale_copy():
        return remote(scales, SC, S.sc_s.at[0], S.sc_r.at[0], dev(oh, c, y, z, 1))

    def scale_own():
        return pltpu.make_async_copy(scales, SC, S.sc_r.at[0])

    def scale_start():
        @pl.when(l == 0)
        def _():
            scale_copy().start()
            scale_own().start()

    def piece(i):
        m, j = i // PIECES, i % PIECES
        if j < 8:
            offset = j * COLS
        else:
            offset = pl.multiple_of(2 * D + cb * COLS, COLS)
        return pltpu.make_async_copy(tproj.at[m, :, pl.ds(offset, TPC)], S.TP.at[i % SLOTS], S.tp_m.at[i % SLOTS])

    def gen_hat(block, part):
        H = S.H

        def rows(r, carry):
            at = pl.ds(pl.multiple_of(part * 32 + r * 16, 16), 16)
            x = XG[block, at, :].astype(F32)
            inv = lax.rsqrt(jnp.sum(x * x, axis=1, keepdims=True) / D + RMS_EPS)
            hat = (x * inv * (1.0 + mod[0, 1:2, :]) + mod[0, 0:1, :]).astype(BF16)
            to = pl.ds(pl.multiple_of(block * ROWS + part * 32 + r * 16, 16), 16)
            for k in range(4):
                H[k, to, :] = hat[:, k * COLS : (k + 1) * COLS]
            return carry

        lax.fori_loop(0, 2, rows, 0)

    def features():
        index = lax.broadcasted_iota(jnp.int32, (1, ROWS), 1).astype(F32)
        frequency = jnp.exp(index * (-math.log(10000.0) / ROWS))
        phase = jnp.full((1, ROWS), dstep[h], jnp.int32).astype(F32) * frequency
        feature = jnp.concatenate([jnp.cos(phase), jnp.sin(phase)], axis=1)
        hi = feature.astype(BF16).astype(F32)
        mid = (feature - hi).astype(BF16).astype(F32)
        low = (feature - hi - mid).astype(BF16).astype(F32)
        row = lax.broadcasted_iota(jnp.int32, (16, 2 * ROWS), 0)
        a, b, d = [jnp.broadcast_to(v, (16, 2 * ROWS)) for v in (hi, mid, low)]
        S.FT[...] = jnp.where(row == 0, a, jnp.where(row == 1, b, jnp.where(row == 2, d, 0.0))).astype(BF16)

    def judge_piece(i):
        m, j = i // PIECES, i % PIECES
        piece(i).wait()
        lifted = jnp.dot(S.FT[...], S.TP[i % SLOTS], preferred_element_type=F32)
        lifted = jnp.sum(lifted, axis=0, keepdims=True)
        if j < 8:
            S.JM[m, j // 4, j % 4] = lifted + mod[m + 1, j // 4 : j // 4 + 1, (j % 4) * COLS : (j % 4 + 1) * COLS]
        else:
            gate = mod[m + 1, 2:3, pl.ds(pl.multiple_of(cb * COLS, COLS), COLS)]
            S.PK[m + 4 : m + 5, :] = lifted + gate
        if i + SLOTS < 2 * PIECES:
            piece(i + SLOTS).start()

    def factors():
        arrived(SC, S.sc_s.at[0], S.sc_r.at[0])
        row = lax.broadcasted_iota(jnp.int32, (8, COLS), 0)
        for m in range(3):
            group = jnp.where(h == 0, sgroup[0:1, m : m + 1], sgroup[1:2, m : m + 1])
            picked = jnp.sum(jnp.where(row == group, SC[m], 0.0), axis=0, keepdims=True)
            if m == 0:
                gate = mod[0, 2:3, pl.ds(pl.multiple_of(cb * COLS, COLS), COLS)]
            else:
                gate = S.PK[m + 3 : m + 4, :]
            S.PK[m : m + 1, :] = gate * picked

    def level():
        return jnp.full((1, COLS), dstep[h], jnp.int32).astype(F32) / 1000.0

    def product(lhs, m, k, first=False):
        ACC = S.ACC
        part = jnp.dot(lhs[k], S.W[m, k].reshape(COLS, COLS), preferred_element_type=F32)
        if first:
            ACC[...] = part
        else:
            ACC[...] += part

    TILE = 64

    def clean_rows(block):
        lev = level()
        here = pl.ds(pl.multiple_of(cb * COLS, COLS), COLS)

        def rows(r, carry):
            at = pl.ds(pl.multiple_of(block * ROWS + r * TILE, TILE), TILE)
            inner = pl.ds(pl.multiple_of(r * TILE, TILE), TILE)
            branch = (S.ACC[at, :] * S.PK[0:1, :]).astype(BF16)
            clean = XG[block, inner, here].astype(F32) + branch.astype(F32)
            noisy = (1.0 - lev) * clean + lev * NS[block, inner, :].astype(F32)
            S.CL[at, :] = clean
            S.NF[at, :] = noisy
            S.SB[at, :] = clean.astype(BF16)
            S.NG[cb, at, :] = noisy.astype(BF16)
            return carry

        lax.fori_loop(0, ROWS // TILE, rows, 0)

    def block_rows(block):
        return pl.ds(block * ROWS, ROWS)

    def noisy_send(block):
        own = S.NG.at[cb, block_rows(block)]
        send(own, own, S.ng_s.at[0], S.ng_r.at[block, 0], dev(h, c, y, z, ol))
        send(own, own, S.ng_s.at[0], S.ng_r.at[block, 1], dev(h, oc, y, z, l))

    far = 2 * ((h + ol) % 2) + c

    def noisy_forward(block):
        got = S.NG.at[far, block_rows(block)]
        arrived(got, S.ng_s.at[0], S.ng_r.at[block, 0])
        send(got, got, S.ng_s.at[0], S.ng_r.at[block, 1], dev(h, oc, y, z, l))

    def noisy_wait(block):
        arrived(S.NG.at[0:2, block_rows(block)], S.ng_s.at[0], S.ng_r.at[block, 1])

    def judge_hats(part):
        NG, JH, JM = S.NG, S.JH, S.JM

        def rows(r, carry):
            at = pl.ds(pl.multiple_of(part * 64 + r * 16, 16), 16)
            v = [NG[k, at, :].astype(F32) for k in range(4)]
            total = sum(jnp.sum(t * t, axis=1, keepdims=True) for t in v)
            inv = lax.rsqrt(total / D + RMS_EPS)
            for k in range(4):
                normed = (v[k] * inv).astype(BF16).astype(F32)
                for j in range(2):
                    JH[j, k, at, :] = (normed * (1.0 + JM[j, 1, k]) + JM[j, 0, k]).astype(BF16)
            return carry

        lax.fori_loop(0, 4, rows, 0)

    def return_rows(buf, out, ss, rs):
        here = pl.ds(pl.multiple_of(cb * COLS, COLS), COLS)
        for i, (c_, l_) in enumerate(others):
            block = pl.ds(pl.multiple_of((2 * l_ + c_) * ROWS, ROWS), ROWS)
            send(buf.at[block], out.at[:, here], ss.at[0], rs.at[0], dev(h, c_, y, z, l_))
        block = pl.ds(pl.multiple_of(q * ROWS, ROWS), ROWS)
        own = pltpu.make_async_copy(buf.at[block], out.at[:, here], ss.at[1])
        own.start()
        return own

    def return_wait(out, ss, rs):
        arrived(NS.at[0:3], ss.at[0], rs.at[0])

    def judged(m, half):
        ACC = S.ACC
        at = pl.ds(half * (GROUP // 2), GROUP // 2)
        for k in range(4):
            part = jnp.dot(S.JH[m - 1, k, at, :], S.W[m, k].reshape(COLS, COLS), preferred_element_type=F32)
            if k == 0:
                ACC[at, :] = part
            else:
                ACC[at, :] += part

    def half_tiles(half, body, carry):
        tiles = GROUP // 2 // TILE
        return lax.fori_loop(half * tiles, (half + 1) * tiles, body, carry)

    def real_rows(half):
        lev = level()

        def rows(r, total):
            at = pl.ds(pl.multiple_of(r * TILE, TILE), TILE)
            real = (S.ACC[at, :] * S.PK[1:2, :]).astype(BF16)
            S.RP[at, :] = real
            noisy = S.NF[at, :]
            gone = jnp.abs(S.CL[at, :] - (noisy - lev * (noisy + real.astype(F32))))
            return total + jnp.sum(gone.reshape(TILE // 8, 8, COLS), axis=0)

        total = half_tiles(half, rows, jnp.zeros((8, COLS), F32))
        total = jnp.sum(jnp.sum(total, axis=1, keepdims=True), axis=0, keepdims=True)
        total = jnp.broadcast_to(total, (8, 128))
        S.SP[...] = total if half == 0 else S.SP[...] + total

    def gap_rows(half):
        lev = level()

        def rows(r, carry):
            at = pl.ds(pl.multiple_of(r * TILE, TILE), TILE)
            fake = (S.ACC[at, :] * S.PK[2:3, :]).astype(BF16).astype(F32)
            gap = lev * (S.RP[at, :].astype(F32) - fake)
            S.GP[at, :] = gap
            S.CT[at, :] = (gap * S.PK[0:1, :]).astype(BF16)
            return carry

        half_tiles(half, rows, 0)

    def spread_group_start():
        S.SPG[q] = S.SP[...]
        for c_, l_ in others:
            send(S.SP, S.SPG.at[q], S.sg_s.at[0], S.sg_r.at[0], dev(h, c_, y, z, l_))

    def spread_z_start():
        SPG, SPZ = S.SPG, S.SPZ
        arrived(SPG.at[0:3], S.sg_s.at[0], S.sg_r.at[0])
        SPZ[z] = (SPG[0] + SPG[1]) + (SPG[2] + SPG[3])
        for j in range(1, NZ):
            send(SPZ.at[z], SPZ.at[z], S.sz_s.at[0], S.sz_r.at[0], dev(h, c, y, zz(j), l))

    def spread_y_start():
        SPZ, SPY = S.SPZ, S.SPY
        arrived(SPZ.at[0:7], S.sz_s.at[0], S.sz_r.at[0])
        total = SPZ[0]
        for j in range(1, NZ):
            total = total + SPZ[j]
        SPY[y] = total
        for j in range(1, NY):
            send(SPY.at[y], SPY.at[y], S.sy_s.at[0], S.sy_r.at[0], dev(h, c, yy(j), z, l))

    def spread_value():
        SPY = S.SPY
        arrived(SPY.at[0:3], S.sy_s.at[0], S.sy_r.at[0])
        total = SPY[0]
        for j in range(1, NY):
            total = total + SPY[j]
        S.SV[...] = total / CLIP_ELEMENTS + SPREAD_EPS

    def dmd_rows():
        def rows(r, carry):
            at = pl.ds(pl.multiple_of(r * TILE, TILE), TILE)
            S.DB[at, :] = (S.GP[at, :] / S.SV[0:1, 0:1]).astype(BF16)
            return carry

        lax.fori_loop(0, GROUP // TILE, rows, 0)

    G = S.G

    def grad(k, lanes, width):
        block = lax.dot_general(S.H[k], S.CT[:, lanes], (((0,), (0,)), ((), ())), preferred_element_type=F32)
        G[k, :, :, lanes] = block.reshape(NZ, BLK, width)

    def grad_b(k):
        grad(k, LB, CB)

    def grad_a(k):
        grad(k, LA, CA)

    def big_y0(r):
        S.Y0S[r] = G[yy(2), zz(r), :, LB].astype(BF16)
        target = dev(h, c, yy(1 - 2 * way_of[r]), z, l)
        remote(S.Y0S.at[r], S.Y0R.at[r], S.rs_s.at[0], S.b0_r.at[r], target).start()

    def big_y1(r):
        for way in range(2):
            s = 1 - 2 * way
            v = G[yy(s), zz(r), :, LB]
            if way == way_of[r]:
                arrived(S.Y0R.at[r], S.rs_s.at[0], S.b0_r.at[r])
                v = v + S.Y0R[r].astype(F32)
            S.Y1S[r, way] = v.astype(BF16)
            remote(S.Y1S.at[r, way], S.Y1R.at[r, way], S.rs_s.at[1], S.b1_r.at[r], dev(h, c, yy(s), z, l)).start()

    def big_y2(r):
        Y1R = S.Y1R
        arrived(Y1R.at[r], S.rs_s.at[1], S.b1_r.at[r])
        G[y, zz(r), :, LB] = G[y, zz(r), :, LB] + Y1R[r, 0].astype(F32) + Y1R[r, 1].astype(F32)

    def slot(k, way):
        return 0 if k == 1 else 2 * k - 3 + way

    def pair(k):
        return pl.ds(slot(k, 0), 1 if k == 1 else 2)

    def big_z(k, j):
        ZS, ZR = S.ZS, S.ZR
        at = yy(Y_ORDER[j])
        if k > 1:
            arrived(ZR.at[pair(k - 1), j], S.rs_s.at[2], S.a_r.at[k - 2, j])
        for way in range(2):
            s = 1 - 2 * way
            if k == 5 or (k == 1 and way != j % 2):
                continue
            v = G[at, zz(s * (5 - k)), :, LA]
            if k > 2 or (k == 2 and way == j % 2):
                v = v + ZR[slot(k - 1, way), j].astype(F32)
            n = slot(k, way)
            ZS[n, j] = v.astype(BF16)
            remote(ZS.at[n, j], ZR.at[n, j], S.rs_s.at[2], S.a_r.at[k - 1, j], dev(h, c, y, zz(s), l)).start()
        if k == 5:
            G[at, z, :, LA] = G[at, z, :, LA] + ZR[5, j].astype(F32) + ZR[6, j].astype(F32)

    def small_y(j):
        ys, yr = S.ys, S.yr
        if j < 3:
            at = yy(Y_ORDER[j])
            ys[j] = G[at, z, :, LA].astype(BF16)
            remote(ys.at[j], yr.at[j], S.rs_s.at[3], S.y_r.at[0], dev(h, c, at, z, l)).start()
        else:
            arrived(yr.at[0:3], S.rs_s.at[3], S.y_r.at[0])
            total = yr[0].astype(F32) + yr[1].astype(F32) + yr[2].astype(F32)
            G[y, z, :, LA] = G[y, z, :, LA] + total

    def small_z(k):
        zs, zr = S.zs, S.zr
        if k > 1:
            arrived(zr.at[0] if k == 2 else zr.at[pair(k - 1)], S.rs_s.at[4], S.z_r.at[k - 2])
        for way in range(2):
            s = 1 - 2 * way
            some = (pl.ds(0, CUT), pl.ds(CUT, BLK - CUT))[way]
            target = dev(h, c, y, zz(s), l)
            n = slot(k, way)
            if k == 1:
                zs[0, some, :] = G[y, zz(4), some, LB].astype(BF16)
                remote(zs.at[0, some], zr.at[0, some], S.rs_s.at[4], S.z_r.at[0], target).start()
            elif k < 5:
                at = zz(s * (5 - k))
                if k > 2:
                    zs[n] = (G[y, at, :, LB] + zr[slot(k - 1, way)].astype(F32)).astype(BF16)
                else:
                    other = (pl.ds(CUT, BLK - CUT), pl.ds(0, CUT))[way]
                    zs[n, some, :] = (G[y, at, some, LB] + zr[0, some, :].astype(F32)).astype(BF16)
                    zs[n, other, :] = G[y, at, other, LB].astype(BF16)
                remote(zs.at[n], zr.at[n], S.rs_s.at[4], S.z_r.at[k - 1], target).start()
        if k == 5:
            G[y, z, :, LB] = G[y, z, :, LB] + zr[5].astype(F32) + zr[6].astype(F32)

    def rings_sent():
        wholes = (S.Y0S, S.Y1S, S.ZS.at[0:7], S.ys.at[0:3], S.zs.at[0:7])
        for i, whole in enumerate(wholes):
            remote(whole, whole, S.rs_s.at[i], S.b0_r.at[0], dev(h, oc, y, z, l)).wait_send()

    tok_own.start()
    noise_own.start()
    for i in range(SLOTS):
        piece(i).start()
    x_prepare()
    features()
    pl.semaphore_wait(barrier, len(greeted))
    x_start(0)
    x_start(1)
    x_start(2)
    tok_near()
    scale_start()
    tok_own.wait()
    gen_hat(q, 0)
    gen_hat(q, 1)
    gen_hat(q, 2)
    gen_hat(q, 3)
    judge_piece(0)
    judge_piece(1)
    judge_piece(2)
    judge_piece(3)
    judge_piece(4)
    judge_piece(5)
    judge_piece(6)
    judge_piece(7)
    judge_piece(8)
    judge_piece(9)
    judge_piece(10)
    judge_piece(11)
    judge_piece(12)
    judge_piece(13)
    judge_piece(14)
    assemble(0)
    ag_go(0, AY, 1)
    ag_go(0, BZ, 1)
    ag_go(0, FZ, 1, 0)
    ag_go(0, FY, 1, 0)
    judge_piece(15)
    arrived(XG.at[q_near], S.tk_s.at[0], S.tk_r.at[1])
    gen_hat(q_near, 0)
    gen_hat(q_near, 1)
    gen_hat(q_near, 2)
    gen_hat(q_near, 3)
    judge_piece(16)
    judge_piece(17)
    assemble(1)
    ag_go(1, AY, 1)
    ag_go(1, BZ, 1)
    ag_go(1, FY, 1, 0)
    ag_got(0, AY, 1)
    ag_go(0, AY, 2)
    ag_go(0, FZ, 1, 1)
    ag_go(0, FZ, 1, 2)
    ag_got(0, BZ, 1)
    ag_go(0, BZ, 2)
    ag_go(0, FY, 1, 1)
    ag_go(0, FY, 1, 7)
    tok_far()
    assemble(2)
    ag_got(0, FZ, 1, 0)
    ag_go(0, FZ, 2, 0)
    factors()
    ag_got(0, FY, 1, 0)
    ag_go(0, FY, 2, 0)
    ag_got(1, BZ, 1)
    ag_go(1, BZ, 2)
    ag_go(2, AY, 1)
    ag_got(0, FZ, 1, 1)
    ag_go(0, FZ, 2, 1)
    ag_got(1, AY, 1)
    ag_go(1, AY, 2)
    ag_got(0, FZ, 1, 2)
    ag_go(0, FZ, 2, 2)
    ag_got(0, FY, 1, 1)
    ag_go(0, FY, 2, 1)
    ag_got(0, BZ, 2)
    ag_go(0, BZ, 3)
    ag_go(0, FY, 1, 2)
    ag_go(0, FY, 1, 6)
    ag_got(0, FZ, 2, 0)
    ag_go(0, FZ, 3, 0)
    ag_got(0, AY, 2)
    ag_go(0, FZ, 1, 3)
    ag_got(0, FY, 1, 7)
    ag_go(0, FY, 2, 7)
    ag_got(0, FZ, 2, 1)
    ag_go(0, FZ, 3, 1)
    ag_got(2, AY, 1)
    ag_go(2, AY, 2)
    ag_got(0, FZ, 2, 2)
    ag_go(0, FZ, 3, 2)
    ag_got(0, FY, 1, 2)
    ag_go(0, FY, 2, 2)
    ag_got(1, BZ, 2)
    ag_go(1, FY, 1, 8)
    ag_got(0, BZ, 3)
    ag_go(0, BZ, 4)
    ag_go(0, FY, 1, 3)
    ag_got(0, FZ, 3, 0)
    ag_go(0, FZ, 4, 0)
    ag_go(0, FY, 1, 5)
    ag_go(1, BZ, 3)
    ag_got(0, FZ, 1, 3)
    ag_go(0, FZ, 2, 3)
    ag_got(0, FY, 1, 6)
    ag_go(0, FY, 2, 6)
    ag_got(0, FZ, 3, 1)
    ag_go(0, FZ, 4, 1)
    ag_got(0, FZ, 3, 2)
    ag_go(0, FZ, 4, 2)
    ag_got(1, FY, 1, 8)
    ag_go(1, XY, 1, 8)
    ag_got(0, BZ, 4)
    ag_go(0, FY, 1, 4)
    ag_got(1, AY, 2)
    ag_go(1, FZ, 1, 2)
    ag_got(0, FY, 1, 3)
    ag_go(0, FY, 2, 3)
    ag_got(1, BZ, 3)
    ag_go(1, BZ, 4)
    tok_forward()
    noise_send(0)
    noise_send(1)
    noise_send(2)
    ag_got(0, FY, 1, 5)
    ag_go(0, FY, 2, 5)
    ag_go(1, FZ, 1, 0)
    gen_hat(q_far, 0)
    ag_got(0, FZ, 2, 3)
    ag_go(0, FZ, 3, 3)
    ag_go(1, FY, 1, 9)
    gen_hat(q_far, 1)
    gen_hat(q_far, 2)
    gen_hat(q_far, 3)
    ag_go(1, FY, 2, 8)
    ag_go(1, FZ, 1, 1)
    ag_got(0, FY, 1, 4)
    ag_go(0, FY, 2, 4)
    ag_got(1, FZ, 1, 2)
    ag_go(1, XZ, 1)
    ag_go(1, FZ, 2, 2)
    ag_go(1, FY, 1, 1)
    ag_go(2, BZ, 1)
    ag_go(1, FY, 1, 7)
    ag_got(1, FZ, 1, 0)
    ag_go(1, FZ, 2, 0)
    ag_got(0, FZ, 3, 3)
    ag_go(0, FZ, 4, 3)
    arrived(XG.at[q_last], S.tk_s.at[0], S.tk_r.at[2])
    gen_hat(q_last, 0)
    ag_got(1, FY, 1, 9)
    ag_go(1, XY, 1, 9)
    gen_hat(q_last, 1)
    gen_hat(q_last, 2)
    gen_hat(q_last, 3)
    ag_go(1, FY, 2, 9)
    ag_got(0, FZ, 4, 0)
    product(S.H, 0, y, True)
    ag_got(1, FZ, 2, 2)
    ag_go(1, FZ, 3, 2)
    ag_go(1, XZ, 2)
    ag_got(1, BZ, 4)
    ag_go(1, FY, 1, 4)
    ag_got(0, FZ, 4, 1)
    product(S.H, 0, yy(1))
    ag_got(1, FZ, 1, 1)
    ag_go(1, FZ, 2, 1)
    ag_got(0, FZ, 4, 2)
    product(S.H, 0, yy(-1))
    ag_got(1, FY, 2, 8)
    ag_go(1, XY, 2, 8)
    ag_got(1, FY, 1, 0)
    ag_go(1, FY, 2, 0)
    ag_got(1, FY, 1, 1)
    ag_go(1, FY, 2, 1)
    ag_got(2, BZ, 1)
    ag_go(2, BZ, 2)
    ag_got(1, FZ, 2, 0)
    ag_go(1, FZ, 3, 0)
    ag_got(1, FY, 1, 7)
    ag_go(1, FY, 2, 7)
    ag_got(0, FZ, 4, 3)
    ag_got(0, FY, 2, 0)
    ag_got(0, FY, 2, 1)
    ag_got(0, FY, 2, 7)
    ag_got(0, FY, 2, 2)
    ag_got(0, FY, 2, 6)
    ag_got(0, FY, 2, 3)
    ag_got(0, FY, 2, 5)
    ag_got(0, FY, 2, 4)
    product(S.H, 0, yy(2))
    ag_got(1, FZ, 3, 2)
    ag_go(1, FZ, 4, 2)
    ag_go(1, XZ, 3)
    ag_go(2, FY, 1, 0)
    noise_wait()
    clean_rows(0)
    noisy_send(0)
    clean_rows(1)
    noisy_send(1)
    clean_rows(2)
    noisy_send(2)
    ag_got(2, AY, 2)
    ag_go(2, FZ, 1, 2)
    clean_rows(3)
    noisy_send(3)
    ag_got(1, FY, 2, 9)
    ag_go(1, XY, 2, 9)
    ag_got(1, FY, 1, 4)
    ag_go(1, FY, 2, 4)
    ag_got(1, FZ, 2, 1)
    ag_go(1, FZ, 3, 1)
    ag_go(2, FZ, 1, 0)
    ag_got(2, BZ, 2)
    ag_go(2, FY, 1, 8)
    ag_got(1, FZ, 3, 0)
    ag_go(1, FZ, 4, 0)
    ag_go(2, FY, 1, 1)
    ag_got(1, FZ, 4, 2)
    ag_go(1, XZ, 4)
    ag_go(2, BZ, 3)
    ag_got(2, FZ, 1, 2)
    ag_go(2, XZ, 1)
    ag_go(2, FY, 1, 7)
    ag_go(2, FZ, 2, 2)
    noisy_forward(0)
    ag_got(1, FZ, 3, 1)
    ag_go(1, FZ, 4, 1)
    ag_got(2, FY, 1, 8)
    ag_go(2, FY, 2, 8)
    ag_go(2, XY, 1, 8)
    ag_got(2, FZ, 1, 0)
    ag_go(2, FZ, 2, 0)
    ag_got(2, FY, 1, 0)
    ag_go(2, FY, 2, 0)
    ag_go(2, FZ, 1, 1)
    ag_got(2, FY, 1, 1)
    ag_go(2, FY, 2, 1)
    ag_got(2, BZ, 3)
    ag_go(2, BZ, 4)
    ag_go(2, FY, 1, 9)
    noisy_wait(0)
    judge_hats(0)
    judge_hats(1)
    noisy_forward(1)
    ag_got(2, FZ, 2, 2)
    ag_go(2, FZ, 3, 2)
    ag_go(2, XZ, 2)
    ag_got(2, FY, 1, 7)
    ag_go(2, FY, 2, 7)
    ag_got(2, FY, 2, 8)
    ag_go(2, XY, 2, 8)
    ag_got(2, FZ, 2, 0)
    ag_go(2, FZ, 3, 0)
    ag_got(2, FZ, 1, 1)
    ag_go(2, FZ, 2, 1)
    ag_got(2, BZ, 4)
    ag_go(2, FY, 1, 4)
    noisy_wait(1)
    judge_hats(2)
    ag_got(2, FY, 1, 9)
    ag_go(2, FY, 2, 9)
    ag_go(2, XY, 1, 9)
    judge_hats(3)
    noisy_forward(2)
    ag_got(2, FZ, 3, 2)
    ag_go(2, FZ, 4, 2)
    ag_got(1, FZ, 4, 0)
    ag_got(1, FZ, 4, 1)
    ag_got(1, XY, 1, 8)
    ag_got(1, XY, 1, 9)
    ag_got(1, XZ, 1)
    ag_got(1, XZ, 2)
    ag_got(1, XZ, 3)
    ag_got(1, XZ, 4)
    ag_got(1, XY, 2, 8)
    ag_got(1, XY, 2, 9)
    ag_got(1, FY, 2, 0)
    ag_got(1, FY, 2, 1)
    ag_got(1, FY, 2, 7)
    ag_got(1, FY, 2, 4)
    judged(1, 0)
    ag_go(2, XZ, 3)
    ag_got(2, FZ, 3, 0)
    ag_go(2, FZ, 4, 0)
    ag_got(2, FZ, 2, 1)
    ag_go(2, FZ, 3, 1)
    real_rows(0)
    ag_got(2, FY, 1, 4)
    ag_go(2, FY, 2, 4)
    ag_got(2, FZ, 4, 2)
    ag_go(2, XZ, 4)
    noisy_wait(2)
    judge_hats(4)
    noisy_forward(3)
    judge_hats(5)
    ag_got(2, FY, 2, 9)
    ag_go(2, XY, 2, 9)
    ag_got(2, FZ, 3, 1)
    ag_go(2, FZ, 4, 1)
    noisy_wait(3)
    judge_hats(6)
    judge_hats(7)
    judged(1, 1)
    real_rows(1)
    spread_group_start()
    ag_got(2, FZ, 4, 0)
    ag_got(2, FZ, 4, 1)
    ag_got(2, XY, 1, 8)
    ag_got(2, XY, 1, 9)
    ag_got(2, XZ, 1)
    ag_got(2, XZ, 2)
    ag_got(2, XZ, 3)
    ag_got(2, XZ, 4)
    ag_got(2, XY, 2, 8)
    ag_got(2, XY, 2, 9)
    ag_got(2, FY, 2, 0)
    ag_got(2, FY, 2, 1)
    ag_got(2, FY, 2, 7)
    ag_got(2, FY, 2, 4)
    judged(2, 0)
    gap_rows(0)
    judged(2, 1)
    sample_own = return_rows(S.SB, out_s, S.sm_s, S.sm_r)
    spread_z_start()
    gap_rows(1)
    grad_b(yy(2))
    big_y0(4)
    big_y0(3)
    big_y0(5)
    big_y0(2)
    grad_a(yy(2))
    big_z(1, 0)
    grad_b(yy(1))
    grad_b(yy(-1))
    grad_a(yy(1))
    big_z(1, 1)
    grad_a(yy(-1))
    big_z(1, 2)
    big_y1(4)
    big_z(2, 0)
    big_y1(3)
    big_y0(6)
    big_y0(1)
    grad_a(y)
    big_z(1, 3)
    spread_y_start()
    big_z(2, 1)
    big_y1(5)
    big_z(2, 2)
    big_y1(2)
    big_y0(7)
    big_y0(0)
    grad_b(y)
    big_z(2, 3)
    big_z(3, 0)
    big_y2(4)
    small_z(1)
    big_y1(6)
    big_z(3, 1)
    big_y2(3)
    big_y2(5)
    small_z(2)
    spread_value()
    dmd_rows()
    dmd_own = return_rows(S.DB, out_d, S.dm_s, S.dm_r)
    big_z(3, 2)
    big_z(3, 3)
    big_y1(1)
    big_z(4, 0)
    big_y1(7)
    big_z(4, 1)
    big_y1(0)
    big_y2(2)
    big_y2(6)
    small_z(3)
    big_z(4, 2)
    big_z(4, 3)
    big_z(5, 0)
    small_y(0)
    big_y2(1)
    big_y2(7)
    big_z(5, 1)
    small_y(1)
    big_z(5, 2)
    small_y(2)
    small_z(4)
    ag_sent(0)
    ag_sent(1)
    ag_sent(2)
    sample_own.wait()
    big_z(5, 3)
    big_y2(0)
    small_y(3)
    small_z(5)
    GF, OW = S.GF, S.OW
    done = G[y, z] / S.SV[0:1, 0:1] / TOKENS

    def own_row(row, slot, target):
        return remote(GF.at[row], OW.at[slot], S.ow_s.at[row], S.ow_r.at[slot], target)

    for row in range(2):
        part = jnp.concatenate([done[row * HALF : (row + 1) * HALF], jnp.zeros((PAD - HALF, COLS), F32)], axis=0)
        GF[row] = part.astype(BF16)

    @pl.when(l == 0)
    def _():
        own_row(1, 0, dev(h, c, y, z, 1)).start()
        OW[0] = GF[0]

    @pl.when(l == 1)
    def _():
        own_row(0, 1, dev(oh, c, y, z, 0)).start()
        own_row(1, 1, dev(oh, c, y, z, 1)).start()
        arrived(OW.at[0], S.ow_s.at[0], S.ow_r.at[0])

    arrived(OW.at[1], S.ow_s.at[1], S.ow_r.at[1])
    out_w[...] = (OW[0].astype(F32) + OW[1].astype(F32))[:HALF]
    return_wait(out_s, S.sm_s, S.sm_r)
    return_wait(out_d, S.dm_s, S.dm_r)
    dmd_own.wait()
    rings_sent()
    drain()
    for m in range(3):
        x_first(m, 0).wait_send()

    @pl.when(l == 0)
    def _():
        scale_copy().wait_send()
        own_row(1, 0, dev(h, c, y, z, 1)).wait_send()

    @pl.when(l == 1)
    def _():
        for m in range(3):
            x_second(m).wait_send()
        own_row(0, 1, dev(oh, c, y, z, 0)).wait_send()
        own_row(1, 1, dev(oh, c, y, z, 1)).wait_send()


def copy_results(*refs):
    ins, outs, held, come, gone = refs[:3], refs[3:6], refs[6:9], refs[9], refs[10]
    first, second = [], []
    for source, buffer, target in zip(ins, held, outs):
        rows = min(source.shape[0], ROWS // 4)
        rows = rows if source.shape[0] % rows == 0 else source.shape[0]
        for i in range(source.shape[0] // rows):
            at = pl.ds(i * rows, rows)
            n = len(first)
            first.append(pltpu.make_async_copy(source.at[at], buffer.at[at], come.at[n]))
            second.append(pltpu.make_async_copy(buffer.at[at], target.at[at], gone.at[n]))
    for copy in first:
        copy.start()
    for copy, after in zip(first, second):
        copy.wait()
        after.start()
    for after in second:
        after.wait()


def on_device(gi, noise, dmd_step, scale_group, wg, wt, wc, scales, mod, tproj):
    vmem = pl.BlockSpec(memory_space=pltpu.VMEM)
    smem = pl.BlockSpec(memory_space=pltpu.SMEM)
    hbm = pl.BlockSpec(memory_space=pl.ANY)
    out_shape = (
        jax.ShapeDtypeStruct((ROWS, D), BF16),
        jax.ShapeDtypeStruct((ROWS, D), BF16),
        jax.ShapeDtypeStruct((HALF, COLS), F32),
    )
    results = pl.pallas_call(
        kernel,
        out_shape=out_shape,
        in_specs=[hbm, hbm, smem, vmem, vmem, vmem, vmem, hbm, vmem, hbm],
        out_specs=(hbm, hbm, vmem),
        scratch_shapes=list(scratch_table().values()),
        compiler_params=pltpu.CompilerParams(
            collective_id=0, has_side_effects=True, vmem_limit_bytes=64 * 1024 * 1024 - 65536
        ),
    )(gi, noise, dmd_step, scale_group.T, wg, wt, wc, scales, mod, tproj)
    return pl.pallas_call(
        copy_results,
        out_shape=out_shape,
        in_specs=[hbm] * 3,
        out_specs=(hbm,) * 3,
        scratch_shapes=[pltpu.VMEM(s.shape, s.dtype) for s in out_shape] + [pltpu.SemaphoreType.DMA((9,))] * 2,
    )(*results)


def solution(mesh):
    return jax.shard_map(
        on_device,
        mesh=mesh,
        in_specs=(
            P(("dp", "fsdp"), None),
            P(("dp", "fsdp"), None),
            P(),
            P(),
            P("fsdp", "dp"),
            P("fsdp", "dp"),
            P("fsdp", "dp"),
            P(None, None, "dp"),
            P(),
            P(),
        ),
        out_specs=(P(("dp", "fsdp"), None), P(("dp", "fsdp"), None), P("fsdp", "dp")),
        check_vma=False,
    )
```

```python
import functools
import math
import types

import jax
import jax.numpy as jnp
from jax import lax
from jax.experimental import pallas as pl
from jax.experimental.pallas import tpu as pltpu
from jax.sharding import PartitionSpec as P

RMS_EPS = 1e-06
SPREAD_EPS = 1e-05
F32 = jnp.float32
BF16 = jnp.bfloat16
MESH_ID = pl.DeviceIdType.MESH

NY, NZ = 4, 8
D = 2560
COLS = 640
ROWS = 128
GROUP = 4 * ROWS
HALF = 40
PAD = 48
BLK = 80
CA = 256
CB = COLS - CA
CUT = 48
TOKENS = 32768
CLIP_ELEMENTS = 16384 * 2560
TPC = 640
PIECES = 9
SLOTS = 4
AY, AZ, BZ, BY, FY, FZ, XY, XZ = range(8)
FINE_Y, FINE_Z = (0, 1, 2), (0, 1, 2)
SHARED = (1, 2)


def ag_table():
    steps = []
    for m in range(3):
        steps += [(m, AY, k, 0) for k in (1, 2)] + [(m, BZ, k, 0) for k in (1, 2, 3, 4)]
        if m in SHARED:
            steps += [(m, FZ, k, i) for k in (1, 2, 3, 4) for i in range(3)] + [(m, XZ, k, 0) for k in (1, 2, 3, 4)]
            steps += [(m, FY, k, i) for k in (1, 2) for i in (0, 1, 7, 4, 8, 9)] + [(m, XY, k, i) for k in (1, 2) for i in (8, 9)]
            continue
        steps += [(m, FZ, k, i) for k in (1, 2, 3, 4) for i in range(4)] if m in FINE_Z else [(m, AZ, k, i) for k in (1, 2, 3, 4) for i in range(2)]
        steps += [(m, FY, k, i) for k in (1, 2) for i in range(8)] if m in FINE_Y else [(m, BY, k, i) for k in (1, 2) for i in range(2)]
    return {step: n for n, step in enumerate(steps)}


AG_SEMS = ag_table()


def scratch_table():
    vmem, dma = pltpu.VMEM, pltpu.SemaphoreType.DMA
    return dict(
        W=vmem((3, NY, NZ, BLK, COLS), BF16),
        XO=vmem((3, PAD, COLS), BF16),
        XS=vmem((3, 2, PAD, COLS), BF16),
        XG=vmem((4, ROWS, D), BF16),
        H=vmem((4, GROUP, COLS), BF16),
        NS=vmem((4, ROWS, COLS), BF16),
        CL=vmem((GROUP, COLS), F32),
        NF=vmem((GROUP, COLS), F32),
        NG=vmem((4, GROUP, COLS), BF16),
        JH=vmem((2, 4, GROUP, COLS), BF16),
        ACC=vmem((GROUP, COLS), F32),
        RP=vmem((GROUP, COLS), BF16),
        GP=vmem((GROUP, COLS), F32),
        CT=vmem((GROUP, COLS), BF16),
        SB=vmem((GROUP, COLS), BF16),
        DB=vmem((GROUP, COLS), BF16),
        G=vmem((NY, NZ, BLK, COLS), F32),
        ZS=vmem((8, NY, BLK, CA), BF16),
        ZR=vmem((8, NY, BLK, CA), BF16),
        Y0S=vmem((NZ, BLK, CB), BF16),
        Y0R=vmem((NZ, BLK, CB), BF16),
        Y1S=vmem((NZ, 2, BLK, CB), BF16),
        Y1R=vmem((NZ, 2, BLK, CB), BF16),
        ys=vmem((4, BLK, CA), BF16),
        yr=vmem((4, BLK, CA), BF16),
        zs=vmem((8, BLK, CB), BF16),
        zr=vmem((8, BLK, CB), BF16),
        SC=vmem((3, 8, COLS), F32),
        PK=vmem((8, COLS), F32),
        TP=vmem((SLOTS, 2 * ROWS, TPC), BF16),
        FT=vmem((16, 2 * ROWS), BF16),
        JM=vmem((2, 2, 4, 1, COLS), F32),
        SP=vmem((8, 128), F32),
        SV=vmem((8, 128), F32),
        SPG=vmem((4, 8, 128), F32),
        SPZ=vmem((NZ, 8, 128), F32),
        SPY=vmem((NY, 8, 128), F32),
        GF=vmem((2, PAD, COLS), BF16),
        OW=vmem((2, PAD, COLS), BF16),
        ag_s=dma((3, 6)),
        ag_r=dma((len(AG_SEMS),)),
        x_s=dma((3, 2)),
        x_r=dma((3, 2)),
        tk_s=dma((2,)),
        tk_r=dma((3,)),
        ns_s=dma((2,)),
        ns_r=dma((1,)),
        ng_s=dma((1,)),
        ng_r=dma((4, 2)),
        sm_s=dma((2,)),
        sm_r=dma((1,)),
        dm_s=dma((2,)),
        dm_r=dma((1,)),
        sc_s=dma((1,)),
        sc_r=dma((1,)),
        tp_m=dma((SLOTS,)),
        sg_s=dma((1,)),
        sg_r=dma((1,)),
        sz_s=dma((1,)),
        sz_r=dma((1,)),
        sy_s=dma((1,)),
        sy_r=dma((1,)),
        rs_s=dma((5,)),
        b0_r=dma((NZ,)),
        b1_r=dma((NZ,)),
        a_r=dma((4, NY)),
        y_r=dma((1,)),
        z_r=dma((4,)),
        ow_s=dma((2,)),
        ow_r=dma((2,)),
    )


NAMES = tuple(scratch_table())


def kernel(gi, noise, dstep, sgroup, wg, wt, wc, scales, mod, tproj, out_s, out_d, out_w, *rest):
    S = types.SimpleNamespace(**dict(zip(NAMES, rest)))
    dp, fs = lax.axis_index("dp"), lax.axis_index("fsdp")
    h, c = dp // 2, dp % 2
    l, plane = fs % 2, fs // 2
    y, z = plane // NZ, plane % NZ
    oh, oc, ol = 1 - h, 1 - c, 1 - l
    q = 2 * l + c
    cb = 2 * ((h + l) % 2) + c

    def dev(h_, c_, y_, z_, l_):
        return (2 * h_ + c_, (y_ * NZ + z_) * 2 + l_)

    def yy(step):
        return (y + step + NY) % NY

    def zz(step):
        return (z + step + NZ) % NZ

    def remote(src, dst, ss, rs, target):
        return pltpu.make_async_remote_copy(
            src_ref=src, dst_ref=dst, send_sem=ss, recv_sem=rs, device_id=target, device_id_type=MESH_ID
        )

    def send(src, dst, ss, rs, target):
        remote(src, dst, ss, rs, target).start()

    def drain():
        wholes = (
            (XG.at[0:3], S.tk_s),
            (NS.at[0:3], S.ns_s),
            (S.NG.at[0:3], S.ng_s),
            (NS.at[0:3], S.sm_s),
            (NS.at[0:3], S.dm_s),
            (S.SPG.at[0:3], S.sg_s),
            (S.SPZ.at[0:7], S.sz_s),
            (S.SPY.at[0:3], S.sy_s),
        )
        for whole, ss in wholes:
            remote(whole, whole, ss.at[0], S.rs_s.at[0], dev(h, oc, y, z, l)).wait_send()

    def arrived(dst, ss, rs):
        remote(dst, dst, ss, rs, dev(h, oc, y, z, l)).wait_recv()

    greeted = [dev(h, oc, y, z, l), dev(h, oc, y, z, ol)]
    greeted += [dev(h, c, y, z, ol), dev(oh, c, y, z, l), dev(oh, c, y, z, ol)]
    greeted += [dev(h, c, yy(j), z, l) for j in range(1, NY)]
    greeted += [dev(h, c, y, zz(j), l) for j in range(1, NZ)]
    barrier = pltpu.get_barrier_semaphore()
    for target in greeted:
        pl.semaphore_signal(barrier, inc=1, device_id=target, device_id_type=MESH_ID)

    LA, LB = pl.ds(0, CA), pl.ds(CA, CB)
    Z_ORDER = (4, 3, 5, 2, 6, 1, 7, 0)
    Y_ORDER = (2, 1, -1, 0)
    Z_FINE = (0, 1, -1, 2)
    way_of = {r: i % 2 for i, r in enumerate(Z_ORDER)}
    way_of.update({8: 1, 9: 0})

    def along_z(i, l_):
        return {8: 2 + 4 * l_, 9: 3 + 2 * l_}.get(i, i)

    def along_y(m, i, l_):
        return 2 - 3 * l_ if i == 2 and m in SHARED else Z_FINE[i]


    def ag_copies(m, op, k, i):
        W = S.W
        for way in range(2):
            s = 1 - 2 * way
            if op == AY:
                if k == 1:
                    yield W.at[m, y, z, :, LA], W.at[m, yy(-s), z, :, LA], s
                else:
                    part = pl.ds(way * (CA // 2), CA // 2)
                    yield W.at[m, yy(-s), z, :, part], W.at[m, yy(2), z, :, part], s
            elif op == AZ:
                if k < 4 or way == i:
                    some = pl.ds(2 * i, 2)
                    yield W.at[m, some, zz(-s * (k - 1)), :, LA], W.at[m, some, zz(-s * k), :, LA], s
            elif op == FZ:
                if k < 4 or way == i % 2:
                    at = yy(along_y(m, i, l))
                    yield W.at[m, at, zz(-s * (k - 1)), :, LA], W.at[m, at, zz(-s * k), :, LA], s
            elif op == XZ:
                if k < 4 or way == 0:
                    mine, theirs = yy(along_y(m, 2, l)), yy(along_y(m, 2, ol))
                    yield W.at[m, mine, zz(-s * k), :, LA], W.at[m, theirs, zz(-s * k), :, LA], s
            elif op == XY:
                if k == 1 or way == 0:
                    at = yy(-s) if k == 1 else yy(2)
                    yield W.at[m, at, zz(along_z(i, l)), :, LB], W.at[m, at, zz(along_z(i, ol)), :, LB], s
            elif op == BZ:
                some = pl.ds(0, BLK) if k < 4 else (pl.ds(0, CUT), pl.ds(CUT, BLK - CUT))[way]
                yield W.at[m, y, zz(-s * (k - 1)), some, LB], W.at[m, y, zz(-s * k), some, LB], s
            else:
                some = pl.ds(4 * i, 4) if op == BY else zz(along_z(i, l))
                if k == 1:
                    yield W.at[m, y, some, :, LB], W.at[m, yy(-s), some, :, LB], s
                elif way == (i if op == BY else way_of[i]):
                    yield W.at[m, yy(-s), some, :, LB], W.at[m, yy(2), some, :, LB], s

    def ag_sems(m, op, k, i):
        group = {AY: 0, AZ: 1, FZ: 1, BZ: 2, BY: 3, FY: 3, XY: 4, XZ: 5}[op]
        return S.ag_s.at[m, group], S.ag_r.at[AG_SEMS[m, op, k, i]]

    def ag_go(m, op, k, i=0):
        ss, rs = ag_sems(m, op, k, i)
        for src, _, s in ag_copies(m, op, k, i):
            if op in (XY, XZ):
                target = dev(oh, c, y, z, ol)
            else:
                target = dev(h, c, y, zz(s), l) if op in (AZ, BZ, FZ) else dev(h, c, yy(s), z, l)
            remote(src, src, ss, rs, target).start()

    def ag_got(m, op, k, i=0):
        W = S.W
        ss, rs = ag_sems(m, op, k, i)
        if op == AY:
            both = W.at[m, 0:2, z, :, LA] if k == 1 else W.at[m, 0, z, :, LA]
        elif op == AZ:
            both = W.at[m, :, z, :, LA] if k < 4 else W.at[m, 0:2, z, :, LA]
        elif op in (FZ, XZ):
            both = W.at[m, 0:2, z, :, LA] if k < 4 else W.at[m, 0, z, :, LA]
        elif op == BZ:
            both = W.at[m, 0, 0:2, :, LB] if k < 4 else W.at[m, 0, 0, :, LB]
        elif op == BY:
            both = W.at[m, 0, :, :, LB] if k == 1 else W.at[m, 0, 0:4, :, LB]
        else:
            both = W.at[m, 0, 0:2, :, LB] if k == 1 else W.at[m, 0, 0, :, LB]
        arrived(both, ss, rs)

    def ag_sent(m):
        W = S.W
        wholes = [W.at[m, 0:3, 0, :, LA], W.at[m, :, 0:7, :, LA], W.at[m, 0, 0:7, :, LB], W.at[m, 0:3, :, :, LB]]
        if m in SHARED:
            wholes[1], wholes[3] = W.at[m, 0:3, 0:7, :, LA], W.at[m, 0:3, 0:6, :, LB]
            wholes += [W.at[m, 0, 0:6, :, LB], W.at[m, 0, 0:7, :, LA]]
        for group, whole in enumerate(wholes):
            remote(whole, whole, S.ag_s.at[m, group], S.ag_r.at[0], dev(h, oc, y, z, l)).wait_send()

    XO, XS = S.XO, S.XS

    def x_second(m):
        return remote(XO.at[m], XS.at[m, 1], S.x_s.at[m, 1], S.x_r.at[m, 1], dev(h, c, y, z, 0))

    def x_first(m, slot):
        return remote(XO.at[m], XS.at[m, slot], S.x_s.at[m, 0], S.x_r.at[m, slot], dev(oh, c, y, z, 1))

    def x_prepare():
        for m, codes in enumerate((wg, wt, wc)):
            own = codes[...].astype(F32)
            own = jnp.concatenate([own, jnp.zeros((PAD - HALF, COLS), F32)], axis=0).astype(BF16)
            XO[m] = own

            @pl.when(l == 0)
            def _():
                XS[m, 0] = own

    def x_start(m):
        @pl.when(l == 0)
        def _():
            x_first(m, 0).start()

        @pl.when(l == 1)
        def _():
            x_first(m, 1).start()
            x_second(m).start()

    def assemble(m):
        @pl.when(l == 1)
        def _():
            arrived(XS.at[m, 0], S.x_s.at[m, 0], S.x_r.at[m, 0])

        arrived(XS.at[m, 1], S.x_s.at[m, 1], S.x_r.at[m, 1])
        both = [XS[m, i].astype(F32)[:HALF] for i in range(2)]
        S.W[m, y, z] = jnp.concatenate(both, axis=0).astype(BF16)

    XG, NS, SC = S.XG, S.NS, S.SC
    tok_own = pltpu.make_async_copy(gi, XG.at[q], S.tk_s.at[1])

    def tok_near():
        send(gi, XG.at[q], S.tk_s.at[0], S.tk_r.at[1], dev(h, oc, y, z, l))

    def tok_far():
        send(gi, XG.at[q], S.tk_s.at[0], S.tk_r.at[0], dev(h, c, y, z, ol))

    def tok_forward():
        arrived(XG.at[q_far], S.tk_s.at[0], S.tk_r.at[0])
        send(XG.at[q_far], XG.at[q_far], S.tk_s.at[0], S.tk_r.at[2], dev(h, oc, y, z, l))

    q_far, q_near, q_last = 2 * ol + c, 2 * l + oc, 2 * ol + oc

    def columns(c_, l_):
        return pl.ds(pl.multiple_of((2 * ((h + l_) % 2) + c_) * COLS, COLS), COLS)

    others = ((oc, l), (c, ol), (oc, ol))

    def noise_send(i):
        c_, l_ = others[i]
        send(noise.at[:, columns(c_, l_)], NS.at[q], S.ns_s.at[0], S.ns_r.at[0], dev(h, c_, y, z, l_))

    def noise_wait():
        noise_own.wait()
        arrived(NS.at[0:3], S.ns_s.at[0], S.ns_r.at[0])

    noise_own = pltpu.make_async_copy(noise.at[:, columns(c, l)], NS.at[q], S.ns_s.at[1])

    def scale_copy():
        return remote(scales, SC, S.sc_s.at[0], S.sc_r.at[0], dev(oh, c, y, z, 1))

    def scale_own():
        return pltpu.make_async_copy(scales, SC, S.sc_r.at[0])

    def scale_start():
        @pl.when(l == 0)
        def _():
            scale_copy().start()
            scale_own().start()

    def piece(i):
        m, j = i // PIECES, i % PIECES
        if j < 8:
            offset = j * COLS
        else:
            offset = pl.multiple_of(2 * D + cb * COLS, COLS)
        return pltpu.make_async_copy(tproj.at[m, :, pl.ds(offset, TPC)], S.TP.at[i % SLOTS], S.tp_m.at[i % SLOTS])

    def gen_hat(block, part):
        H = S.H

        def rows(r, carry):
            at = pl.ds(pl.multiple_of(part * 32 + r * 16, 16), 16)
            x = XG[block, at, :].astype(F32)
            inv = lax.rsqrt(jnp.sum(x * x, axis=1, keepdims=True) / D + RMS_EPS)
            hat = (x * inv * (1.0 + mod[0, 1:2, :]) + mod[0, 0:1, :]).astype(BF16)
            to = pl.ds(pl.multiple_of(block * ROWS + part * 32 + r * 16, 16), 16)
            for k in range(4):
                H[k, to, :] = hat[:, k * COLS : (k + 1) * COLS]
            return carry

        lax.fori_loop(0, 2, rows, 0)

    def features():
        index = lax.broadcasted_iota(jnp.int32, (1, ROWS), 1).astype(F32)
        frequency = jnp.exp(index * (-math.log(10000.0) / ROWS))
        phase = jnp.full((1, ROWS), dstep[h], jnp.int32).astype(F32) * frequency
        feature = jnp.concatenate([jnp.cos(phase), jnp.sin(phase)], axis=1)
        hi = feature.astype(BF16).astype(F32)
        mid = (feature - hi).astype(BF16).astype(F32)
        low = (feature - hi - mid).astype(BF16).astype(F32)
        row = lax.broadcasted_iota(jnp.int32, (16, 2 * ROWS), 0)
        a, b, d = [jnp.broadcast_to(v, (16, 2 * ROWS)) for v in (hi, mid, low)]
        S.FT[...] = jnp.where(row == 0, a, jnp.where(row == 1, b, jnp.where(row == 2, d, 0.0))).astype(BF16)

    def judge_piece(i):
        m, j = i // PIECES, i % PIECES
        piece(i).wait()
        lifted = jnp.dot(S.FT[...], S.TP[i % SLOTS], preferred_element_type=F32)
        lifted = jnp.sum(lifted, axis=0, keepdims=True)
        if j < 8:
            S.JM[m, j // 4, j % 4] = lifted + mod[m + 1, j // 4 : j // 4 + 1, (j % 4) * COLS : (j % 4 + 1) * COLS]
        else:
            gate = mod[m + 1, 2:3, pl.ds(pl.multiple_of(cb * COLS, COLS), COLS)]
            S.PK[m + 4 : m + 5, :] = lifted + gate
        if i + SLOTS < 2 * PIECES:
            piece(i + SLOTS).start()

    def factors():
        arrived(SC, S.sc_s.at[0], S.sc_r.at[0])
        row = lax.broadcasted_iota(jnp.int32, (8, COLS), 0)
        for m in range(3):
            group = jnp.where(h == 0, sgroup[0:1, m : m + 1], sgroup[1:2, m : m + 1])
            picked = jnp.sum(jnp.where(row == group, SC[m], 0.0), axis=0, keepdims=True)
            if m == 0:
                gate = mod[0, 2:3, pl.ds(pl.multiple_of(cb * COLS, COLS), COLS)]
            else:
                gate = S.PK[m + 3 : m + 4, :]
            S.PK[m : m + 1, :] = gate * picked

    def level():
        return jnp.full((1, COLS), dstep[h], jnp.int32).astype(F32) / 1000.0

    def product(lhs, m, k, first=False):
        ACC = S.ACC
        part = jnp.dot(lhs[k], S.W[m, k].reshape(COLS, COLS), preferred_element_type=F32)
        if first:
            ACC[...] = part
        else:
            ACC[...] += part

    TILE = 64

    def clean_rows(block):
        lev = level()
        here = pl.ds(pl.multiple_of(cb * COLS, COLS), COLS)

        def rows(r, carry):
            at = pl.ds(pl.multiple_of(block * ROWS + r * TILE, TILE), TILE)
            inner = pl.ds(pl.multiple_of(r * TILE, TILE), TILE)
            branch = (S.ACC[at, :] * S.PK[0:1, :]).astype(BF16)
            clean = XG[block, inner, here].astype(F32) + branch.astype(F32)
            noisy = (1.0 - lev) * clean + lev * NS[block, inner, :].astype(F32)
            S.CL[at, :] = clean
            S.NF[at, :] = noisy
            S.SB[at, :] = clean.astype(BF16)
            S.NG[cb, at, :] = noisy.astype(BF16)
            return carry

        lax.fori_loop(0, ROWS // TILE, rows, 0)

    def block_rows(block):
        return pl.ds(block * ROWS, ROWS)

    def noisy_send(block):
        own = S.NG.at[cb, block_rows(block)]
        send(own, own, S.ng_s.at[0], S.ng_r.at[block, 0], dev(h, c, y, z, ol))
        send(own, own, S.ng_s.at[0], S.ng_r.at[block, 1], dev(h, oc, y, z, l))

    far = 2 * ((h + ol) % 2) + c

    def noisy_forward(block):
        got = S.NG.at[far, block_rows(block)]
        arrived(got, S.ng_s.at[0], S.ng_r.at[block, 0])
        send(got, got, S.ng_s.at[0], S.ng_r.at[block, 1], dev(h, oc, y, z, l))

    def noisy_wait(block):
        arrived(S.NG.at[0:2, block_rows(block)], S.ng_s.at[0], S.ng_r.at[block, 1])

    def judge_hats(part):
        NG, JH, JM = S.NG, S.JH, S.JM

        def rows(r, carry):
            at = pl.ds(pl.multiple_of(part * 64 + r * 16, 16), 16)
            v = [NG[k, at, :].astype(F32) for k in range(4)]
            total = sum(jnp.sum(t * t, axis=1, keepdims=True) for t in v)
            inv = lax.rsqrt(total / D + RMS_EPS)
            for k in range(4):
                normed = (v[k] * inv).astype(BF16).astype(F32)
                for j in range(2):
                    JH[j, k, at, :] = (normed * (1.0 + JM[j, 1, k]) + JM[j, 0, k]).astype(BF16)
            return carry

        lax.fori_loop(0, 4, rows, 0)

    def return_rows(buf, out, ss, rs):
        here = pl.ds(pl.multiple_of(cb * COLS, COLS), COLS)
        for i, (c_, l_) in enumerate(others):
            block = pl.ds(pl.multiple_of((2 * l_ + c_) * ROWS, ROWS), ROWS)
            send(buf.at[block], out.at[:, here], ss.at[0], rs.at[0], dev(h, c_, y, z, l_))
        block = pl.ds(pl.multiple_of(q * ROWS, ROWS), ROWS)
        own = pltpu.make_async_copy(buf.at[block], out.at[:, here], ss.at[1])
        own.start()
        return own

    def return_wait(out, ss, rs):
        arrived(NS.at[0:3], ss.at[0], rs.at[0])

    def judged(m, half):
        ACC = S.ACC
        at = pl.ds(half * (GROUP // 2), GROUP // 2)
        for k in range(4):
            part = jnp.dot(S.JH[m - 1, k, at, :], S.W[m, k].reshape(COLS, COLS), preferred_element_type=F32)
            if k == 0:
                ACC[at, :] = part
            else:
                ACC[at, :] += part

    def half_tiles(half, body, carry):
        tiles = GROUP // 2 // TILE
        return lax.fori_loop(half * tiles, (half + 1) * tiles, body, carry)

    def real_rows(half):
        lev = level()

        def rows(r, total):
            at = pl.ds(pl.multiple_of(r * TILE, TILE), TILE)
            real = (S.ACC[at, :] * S.PK[1:2, :]).astype(BF16)
            S.RP[at, :] = real
            noisy = S.NF[at, :]
            gone = jnp.abs(S.CL[at, :] - (noisy - lev * (noisy + real.astype(F32))))
            return total + jnp.sum(gone.reshape(TILE // 8, 8, COLS), axis=0)

        total = half_tiles(half, rows, jnp.zeros((8, COLS), F32))
        total = jnp.sum(jnp.sum(total, axis=1, keepdims=True), axis=0, keepdims=True)
        total = jnp.broadcast_to(total, (8, 128))
        S.SP[...] = total if half == 0 else S.SP[...] + total

    def gap_rows(half):
        lev = level()

        def rows(r, carry):
            at = pl.ds(pl.multiple_of(r * TILE, TILE), TILE)
            fake = (S.ACC[at, :] * S.PK[2:3, :]).astype(BF16).astype(F32)
            gap = lev * (S.RP[at, :].astype(F32) - fake)
            S.GP[at, :] = gap
            S.CT[at, :] = (gap * S.PK[0:1, :]).astype(BF16)
            return carry

        half_tiles(half, rows, 0)

    def spread_group_start():
        S.SPG[q] = S.SP[...]
        for c_, l_ in others:
            send(S.SP, S.SPG.at[q], S.sg_s.at[0], S.sg_r.at[0], dev(h, c_, y, z, l_))

    def spread_z_start():
        SPG, SPZ = S.SPG, S.SPZ
        arrived(SPG.at[0:3], S.sg_s.at[0], S.sg_r.at[0])
        SPZ[z] = (SPG[0] + SPG[1]) + (SPG[2] + SPG[3])
        for j in range(1, NZ):
            send(SPZ.at[z], SPZ.at[z], S.sz_s.at[0], S.sz_r.at[0], dev(h, c, y, zz(j), l))

    def spread_y_start():
        SPZ, SPY = S.SPZ, S.SPY
        arrived(SPZ.at[0:7], S.sz_s.at[0], S.sz_r.at[0])
        total = SPZ[0]
        for j in range(1, NZ):
            total = total + SPZ[j]
        SPY[y] = total
        for j in range(1, NY):
            send(SPY.at[y], SPY.at[y], S.sy_s.at[0], S.sy_r.at[0], dev(h, c, yy(j), z, l))

    def spread_value():
        SPY = S.SPY
        arrived(SPY.at[0:3], S.sy_s.at[0], S.sy_r.at[0])
        total = SPY[0]
        for j in range(1, NY):
            total = total + SPY[j]
        S.SV[...] = total / CLIP_ELEMENTS + SPREAD_EPS

    def dmd_rows():
        def rows(r, carry):
            at = pl.ds(pl.multiple_of(r * TILE, TILE), TILE)
            S.DB[at, :] = (S.GP[at, :] / S.SV[0:1, 0:1]).astype(BF16)
            return carry

        lax.fori_loop(0, GROUP // TILE, rows, 0)

    G = S.G

    def grad(k, lanes, width):
        block = lax.dot_general(S.H[k], S.CT[:, lanes], (((0,), (0,)), ((), ())), preferred_element_type=F32)
        G[k, :, :, lanes] = block.reshape(NZ, BLK, width)

    def grad_b(k):
        grad(k, LB, CB)

    def grad_a(k):
        grad(k, LA, CA)

    def big_y0(r):
        S.Y0S[r] = G[yy(2), zz(r), :, LB].astype(BF16)
        target = dev(h, c, yy(1 - 2 * way_of[r]), z, l)
        remote(S.Y0S.at[r], S.Y0R.at[r], S.rs_s.at[0], S.b0_r.at[r], target).start()

    def big_y1(r):
        for way in range(2):
            s = 1 - 2 * way
            v = G[yy(s), zz(r), :, LB]
            if way == way_of[r]:
                arrived(S.Y0R.at[r], S.rs_s.at[0], S.b0_r.at[r])
                v = v + S.Y0R[r].astype(F32)
            S.Y1S[r, way] = v.astype(BF16)
            remote(S.Y1S.at[r, way], S.Y1R.at[r, way], S.rs_s.at[1], S.b1_r.at[r], dev(h, c, yy(s), z, l)).start()

    def big_y2(r):
        Y1R = S.Y1R
        arrived(Y1R.at[r], S.rs_s.at[1], S.b1_r.at[r])
        G[y, zz(r), :, LB] = G[y, zz(r), :, LB] + Y1R[r, 0].astype(F32) + Y1R[r, 1].astype(F32)

    def slot(k, way):
        return 0 if k == 1 else 2 * k - 3 + way

    def pair(k):
        return pl.ds(slot(k, 0), 1 if k == 1 else 2)

    def big_z(k, j):
        ZS, ZR = S.ZS, S.ZR
        at = yy(Y_ORDER[j])
        if k > 1:
            arrived(ZR.at[pair(k - 1), j], S.rs_s.at[2], S.a_r.at[k - 2, j])
        for way in range(2):
            s = 1 - 2 * way
            if k == 5 or (k == 1 and way != j % 2):
                continue
            v = G[at, zz(s * (5 - k)), :, LA]
            if k > 2 or (k == 2 and way == j % 2):
                v = v + ZR[slot(k - 1, way), j].astype(F32)
            n = slot(k, way)
            ZS[n, j] = v.astype(BF16)
            remote(ZS.at[n, j], ZR.at[n, j], S.rs_s.at[2], S.a_r.at[k - 1, j], dev(h, c, y, zz(s), l)).start()
        if k == 5:
            G[at, z, :, LA] = G[at, z, :, LA] + ZR[5, j].astype(F32) + ZR[6, j].astype(F32)

    def small_y(j):
        ys, yr = S.ys, S.yr
        if j < 3:
            at = yy(Y_ORDER[j])
            ys[j] = G[at, z, :, LA].astype(BF16)
            remote(ys.at[j], yr.at[j], S.rs_s.at[3], S.y_r.at[0], dev(h, c, at, z, l)).start()
        else:
            arrived(yr.at[0:3], S.rs_s.at[3], S.y_r.at[0])
            total = yr[0].astype(F32) + yr[1].astype(F32) + yr[2].astype(F32)
            G[y, z, :, LA] = G[y, z, :, LA] + total

    def small_z(k):
        zs, zr = S.zs, S.zr
        if k > 1:
            arrived(zr.at[0] if k == 2 else zr.at[pair(k - 1)], S.rs_s.at[4], S.z_r.at[k - 2])
        for way in range(2):
            s = 1 - 2 * way
            some = (pl.ds(0, CUT), pl.ds(CUT, BLK - CUT))[way]
            target = dev(h, c, y, zz(s), l)
            n = slot(k, way)
            if k == 1:
                zs[0, some, :] = G[y, zz(4), some, LB].astype(BF16)
                remote(zs.at[0, some], zr.at[0, some], S.rs_s.at[4], S.z_r.at[0], target).start()
            elif k < 5:
                at = zz(s * (5 - k))
                if k > 2:
                    zs[n] = (G[y, at, :, LB] + zr[slot(k - 1, way)].astype(F32)).astype(BF16)
                else:
                    other = (pl.ds(CUT, BLK - CUT), pl.ds(0, CUT))[way]
                    zs[n, some, :] = (G[y, at, some, LB] + zr[0, some, :].astype(F32)).astype(BF16)
                    zs[n, other, :] = G[y, at, other, LB].astype(BF16)
                remote(zs.at[n], zr.at[n], S.rs_s.at[4], S.z_r.at[k - 1], target).start()
        if k == 5:
            G[y, z, :, LB] = G[y, z, :, LB] + zr[5].astype(F32) + zr[6].astype(F32)

    def rings_sent():
        wholes = (S.Y0S, S.Y1S, S.ZS.at[0:7], S.ys.at[0:3], S.zs.at[0:7])
        for i, whole in enumerate(wholes):
            remote(whole, whole, S.rs_s.at[i], S.b0_r.at[0], dev(h, oc, y, z, l)).wait_send()

    tok_own.start()
    noise_own.start()
    for i in range(SLOTS):
        piece(i).start()
    x_prepare()
    features()
    pl.semaphore_wait(barrier, len(greeted))
    x_start(0)
    x_start(1)
    x_start(2)
    tok_near()
    scale_start()
    tok_own.wait()
    gen_hat(q, 0)
    gen_hat(q, 1)
    gen_hat(q, 2)
    gen_hat(q, 3)
    judge_piece(0)
    judge_piece(1)
    judge_piece(2)
    judge_piece(3)
    judge_piece(4)
    judge_piece(5)
    judge_piece(6)
    judge_piece(7)
    judge_piece(8)
    judge_piece(9)
    judge_piece(10)
    judge_piece(11)
    judge_piece(12)
    judge_piece(13)
    judge_piece(14)
    assemble(0)
    ag_go(0, AY, 1)
    ag_go(0, BZ, 1)
    ag_go(0, FZ, 1, 0)
    ag_go(0, FY, 1, 0)
    judge_piece(15)
    arrived(XG.at[q_near], S.tk_s.at[0], S.tk_r.at[1])
    gen_hat(q_near, 0)
    gen_hat(q_near, 1)
    gen_hat(q_near, 2)
    gen_hat(q_near, 3)
    judge_piece(16)
    judge_piece(17)
    assemble(1)
    ag_go(1, AY, 1)
    ag_go(1, BZ, 1)
    ag_go(1, FY, 1, 0)
    ag_got(0, AY, 1)
    ag_go(0, AY, 2)
    ag_go(0, FZ, 1, 1)
    ag_go(0, FZ, 1, 2)
    ag_got(0, BZ, 1)
    ag_go(0, BZ, 2)
    ag_go(0, FY, 1, 1)
    ag_go(0, FY, 1, 7)
    tok_far()
    assemble(2)
    ag_got(0, FZ, 1, 0)
    ag_go(0, FZ, 2, 0)
    factors()
    ag_got(0, FY, 1, 0)
    ag_go(0, FY, 2, 0)
    ag_got(1, BZ, 1)
    ag_go(1, BZ, 2)
    ag_go(2, AY, 1)
    ag_got(0, FZ, 1, 1)
    ag_go(0, FZ, 2, 1)
    ag_got(1, AY, 1)
    ag_go(1, AY, 2)
    ag_got(0, FZ, 1, 2)
    ag_go(0, FZ, 2, 2)
    ag_got(0, FY, 1, 1)
    ag_go(0, FY, 2, 1)
    ag_got(0, BZ, 2)
    ag_go(0, BZ, 3)
    ag_go(0, FY, 1, 2)
    ag_go(0, FY, 1, 6)
    ag_got(0, FZ, 2, 0)
    ag_go(0, FZ, 3, 0)
    ag_got(0, AY, 2)
    ag_go(0, FZ, 1, 3)
    ag_got(0, FY, 1, 7)
    ag_go(0, FY, 2, 7)
    ag_got(0, FZ, 2, 1)
    ag_go(0, FZ, 3, 1)
    ag_got(2, AY, 1)
    ag_go(2, AY, 2)
    ag_got(0, FZ, 2, 2)
    ag_go(0, FZ, 3, 2)
    ag_got(0, FY, 1, 2)
    ag_go(0, FY, 2, 2)
    ag_got(1, BZ, 2)
    ag_go(1, FY, 1, 8)
    ag_got(0, BZ, 3)
    ag_go(0, BZ, 4)
    ag_go(0, FY, 1, 3)
    ag_got(0, FZ, 3, 0)
    ag_go(0, FZ, 4, 0)
    ag_go(0, FY, 1, 5)
    ag_go(1, BZ, 3)
    ag_got(0, FZ, 1, 3)
    ag_go(0, FZ, 2, 3)
    ag_got(0, FY, 1, 6)
    ag_go(0, FY, 2, 6)
    ag_got(0, FZ, 3, 1)
    ag_go(0, FZ, 4, 1)
    ag_got(0, FZ, 3, 2)
    ag_go(0, FZ, 4, 2)
    ag_got(1, FY, 1, 8)
    ag_go(1, XY, 1, 8)
    ag_got(0, BZ, 4)
    ag_go(0, FY, 1, 4)
    ag_got(1, AY, 2)
    ag_go(1, FZ, 1, 2)
    ag_got(0, FY, 1, 3)
    ag_go(0, FY, 2, 3)
    ag_got(1, BZ, 3)
    ag_go(1, BZ, 4)
    tok_forward()
    noise_send(0)
    noise_send(1)
    noise_send(2)
    ag_got(0, FY, 1, 5)
    ag_go(0, FY, 2, 5)
    ag_go(1, FZ, 1, 0)
    gen_hat(q_far, 0)
    ag_got(0, FZ, 2, 3)
    ag_go(0, FZ, 3, 3)
    ag_go(1, FY, 1, 9)
    gen_hat(q_far, 1)
    gen_hat(q_far, 2)
    gen_hat(q_far, 3)
    ag_go(1, FY, 2, 8)
    ag_go(1, FZ, 1, 1)
    ag_got(0, FY, 1, 4)
    ag_go(0, FY, 2, 4)
    ag_got(1, FZ, 1, 2)
    ag_go(1, XZ, 1)
    ag_go(1, FZ, 2, 2)
    ag_go(1, FY, 1, 1)
    ag_go(2, BZ, 1)
    ag_go(1, FY, 1, 7)
    ag_got(1, FZ, 1, 0)
    ag_go(1, FZ, 2, 0)
    ag_got(0, FZ, 3, 3)
    ag_go(0, FZ, 4, 3)
    arrived(XG.at[q_last], S.tk_s.at[0], S.tk_r.at[2])
    gen_hat(q_last, 0)
    ag_got(1, FY, 1, 9)
    ag_go(1, XY, 1, 9)
    gen_hat(q_last, 1)
    gen_hat(q_last, 2)
    gen_hat(q_last, 3)
    ag_go(1, FY, 2, 9)
    ag_got(0, FZ, 4, 0)
    product(S.H, 0, y, True)
    ag_got(1, FZ, 2, 2)
    ag_go(1, FZ, 3, 2)
    ag_go(1, XZ, 2)
    ag_got(1, BZ, 4)
    ag_go(1, FY, 1, 4)
    ag_got(0, FZ, 4, 1)
    product(S.H, 0, yy(1))
    ag_got(1, FZ, 1, 1)
    ag_go(1, FZ, 2, 1)
    ag_got(0, FZ, 4, 2)
    product(S.H, 0, yy(-1))
    ag_got(1, FY, 2, 8)
    ag_go(1, XY, 2, 8)
    ag_got(1, FY, 1, 0)
    ag_go(1, FY, 2, 0)
    ag_got(1, FY, 1, 1)
    ag_go(1, FY, 2, 1)
    ag_got(2, BZ, 1)
    ag_go(2, BZ, 2)
    ag_got(1, FZ, 2, 0)
    ag_go(1, FZ, 3, 0)
    ag_got(1, FY, 1, 7)
    ag_go(1, FY, 2, 7)
    ag_got(0, FZ, 4, 3)
    ag_got(0, FY, 2, 0)
    ag_got(0, FY, 2, 1)
    ag_got(0, FY, 2, 7)
    ag_got(0, FY, 2, 2)
    ag_got(0, FY, 2, 6)
    ag_got(0, FY, 2, 3)
    ag_got(0, FY, 2, 5)
    ag_got(0, FY, 2, 4)
    product(S.H, 0, yy(2))
    ag_got(1, FZ, 3, 2)
    ag_go(1, FZ, 4, 2)
    ag_go(1, XZ, 3)
    ag_go(2, FY, 1, 0)
    noise_wait()
    clean_rows(0)
    noisy_send(0)
    clean_rows(1)
    noisy_send(1)
    clean_rows(2)
    noisy_send(2)
    ag_got(2, AY, 2)
    ag_go(2, FZ, 1, 2)
    clean_rows(3)
    noisy_send(3)
    ag_got(1, FY, 2, 9)
    ag_go(1, XY, 2, 9)
    ag_got(1, FY, 1, 4)
    ag_go(1, FY, 2, 4)
    ag_got(1, FZ, 2, 1)
    ag_go(1, FZ, 3, 1)
    ag_go(2, FZ, 1, 0)
    ag_got(2, BZ, 2)
    ag_go(2, FY, 1, 8)
    ag_got(1, FZ, 3, 0)
    ag_go(1, FZ, 4, 0)
    ag_go(2, FY, 1, 1)
    ag_got(1, FZ, 4, 2)
    ag_go(1, XZ, 4)
    ag_go(2, BZ, 3)
    ag_got(2, FZ, 1, 2)
    ag_go(2, XZ, 1)
    ag_go(2, FY, 1, 7)
    ag_go(2, FZ, 2, 2)
    noisy_forward(0)
    ag_got(1, FZ, 3, 1)
    ag_go(1, FZ, 4, 1)
    ag_got(2, FY, 1, 8)
    ag_go(2, FY, 2, 8)
    ag_go(2, XY, 1, 8)
    ag_got(2, FZ, 1, 0)
    ag_go(2, FZ, 2, 0)
    ag_got(2, FY, 1, 0)
    ag_go(2, FY, 2, 0)
    ag_go(2, FZ, 1, 1)
    ag_got(2, FY, 1, 1)
    ag_go(2, FY, 2, 1)
    ag_got(2, BZ, 3)
    ag_go(2, BZ, 4)
    ag_go(2, FY, 1, 9)
    noisy_wait(0)
    judge_hats(0)
    judge_hats(1)
    noisy_forward(1)
    ag_got(2, FZ, 2, 2)
    ag_go(2, FZ, 3, 2)
    ag_go(2, XZ, 2)
    ag_got(2, FY, 1, 7)
    ag_go(2, FY, 2, 7)
    ag_got(2, FY, 2, 8)
    ag_go(2, XY, 2, 8)
    ag_got(2, FZ, 2, 0)
    ag_go(2, FZ, 3, 0)
    ag_got(2, FZ, 1, 1)
    ag_go(2, FZ, 2, 1)
    ag_got(2, BZ, 4)
    ag_go(2, FY, 1, 4)
    noisy_wait(1)
    judge_hats(2)
    ag_got(2, FY, 1, 9)
    ag_go(2, FY, 2, 9)
    ag_go(2, XY, 1, 9)
    judge_hats(3)
    noisy_forward(2)
    ag_got(2, FZ, 3, 2)
    ag_go(2, FZ, 4, 2)
    ag_got(1, FZ, 4, 0)
    ag_got(1, FZ, 4, 1)
    ag_got(1, XY, 1, 8)
    ag_got(1, XY, 1, 9)
    ag_got(1, XZ, 1)
    ag_got(1, XZ, 2)
    ag_got(1, XZ, 3)
    ag_got(1, XZ, 4)
    ag_got(1, XY, 2, 8)
    ag_got(1, XY, 2, 9)
    ag_got(1, FY, 2, 0)
    ag_got(1, FY, 2, 1)
    ag_got(1, FY, 2, 7)
    ag_got(1, FY, 2, 4)
    judged(1, 0)
    ag_go(2, XZ, 3)
    ag_got(2, FZ, 3, 0)
    ag_go(2, FZ, 4, 0)
    ag_got(2, FZ, 2, 1)
    ag_go(2, FZ, 3, 1)
    real_rows(0)
    ag_got(2, FY, 1, 4)
    ag_go(2, FY, 2, 4)
    ag_got(2, FZ, 4, 2)
    ag_go(2, XZ, 4)
    noisy_wait(2)
    judge_hats(4)
    noisy_forward(3)
    judge_hats(5)
    ag_got(2, FY, 2, 9)
    ag_go(2, XY, 2, 9)
    ag_got(2, FZ, 3, 1)
    ag_go(2, FZ, 4, 1)
    noisy_wait(3)
    judge_hats(6)
    judge_hats(7)
    judged(1, 1)
    real_rows(1)
    spread_group_start()
    ag_got(2, FZ, 4, 0)
    ag_got(2, FZ, 4, 1)
    ag_got(2, XY, 1, 8)
    ag_got(2, XY, 1, 9)
    ag_got(2, XZ, 1)
    ag_got(2, XZ, 2)
    ag_got(2, XZ, 3)
    ag_got(2, XZ, 4)
    ag_got(2, XY, 2, 8)
    ag_got(2, XY, 2, 9)
    ag_got(2, FY, 2, 0)
    ag_got(2, FY, 2, 1)
    ag_got(2, FY, 2, 7)
    ag_got(2, FY, 2, 4)
    judged(2, 0)
    gap_rows(0)
    judged(2, 1)
    sample_own = return_rows(S.SB, out_s, S.sm_s, S.sm_r)
    spread_z_start()
    gap_rows(1)
    grad_b(yy(2))
    big_y0(4)
    big_y0(3)
    big_y0(5)
    big_y0(2)
    grad_a(yy(2))
    big_z(1, 0)
    grad_b(yy(1))
    grad_b(yy(-1))
    grad_a(yy(1))
    big_z(1, 1)
    grad_a(yy(-1))
    big_z(1, 2)
    big_y1(4)
    big_z(2, 0)
    big_y1(3)
    big_y0(6)
    big_y0(1)
    grad_a(y)
    big_z(1, 3)
    spread_y_start()
    big_z(2, 1)
    big_y1(5)
    big_z(2, 2)
    big_y1(2)
    big_y0(7)
    big_y0(0)
    grad_b(y)
    big_z(2, 3)
    big_z(3, 0)
    big_y2(4)
    small_z(1)
    big_y1(6)
    big_z(3, 1)
    big_y2(3)
    big_y2(5)
    small_z(2)
    spread_value()
    dmd_rows()
    dmd_own = return_rows(S.DB, out_d, S.dm_s, S.dm_r)
    big_z(3, 2)
    big_z(3, 3)
    big_y1(1)
    big_z(4, 0)
    big_y1(7)
    big_z(4, 1)
    big_y1(0)
    big_y2(2)
    big_y2(6)
    small_z(3)
    big_z(4, 2)
    big_z(4, 3)
    big_z(5, 0)
    small_y(0)
    big_y2(1)
    big_y2(7)
    big_z(5, 1)
    small_y(1)
    big_z(5, 2)
    small_y(2)
    small_z(4)
    ag_sent(0)
    ag_sent(1)
    ag_sent(2)
    sample_own.wait()
    big_z(5, 3)
    big_y2(0)
    small_y(3)
    small_z(5)
    GF, OW = S.GF, S.OW
    done = G[y, z] / S.SV[0:1, 0:1] / TOKENS

    def own_row(row, slot, target):
        return remote(GF.at[row], OW.at[slot], S.ow_s.at[row], S.ow_r.at[slot], target)

    for row in range(2):
        part = jnp.concatenate([done[row * HALF : (row + 1) * HALF], jnp.zeros((PAD - HALF, COLS), F32)], axis=0)
        GF[row] = part.astype(BF16)

    @pl.when(l == 0)
    def _():
        own_row(1, 0, dev(h, c, y, z, 1)).start()
        OW[0] = GF[0]

    @pl.when(l == 1)
    def _():
        own_row(0, 1, dev(oh, c, y, z, 0)).start()
        own_row(1, 1, dev(oh, c, y, z, 1)).start()
        arrived(OW.at[0], S.ow_s.at[0], S.ow_r.at[0])

    arrived(OW.at[1], S.ow_s.at[1], S.ow_r.at[1])
    out_w[...] = (OW[0].astype(F32) + OW[1].astype(F32))[:HALF]
    return_wait(out_s, S.sm_s, S.sm_r)
    return_wait(out_d, S.dm_s, S.dm_r)
    dmd_own.wait()
    rings_sent()
    drain()
    for m in range(3):
        x_first(m, 0).wait_send()

    @pl.when(l == 0)
    def _():
        scale_copy().wait_send()
        own_row(1, 0, dev(h, c, y, z, 1)).wait_send()

    @pl.when(l == 1)
    def _():
        for m in range(3):
            x_second(m).wait_send()
        own_row(0, 1, dev(oh, c, y, z, 0)).wait_send()
        own_row(1, 1, dev(oh, c, y, z, 1)).wait_send()


def copy_results(*refs):
    ins, outs, held, come, gone = refs[:3], refs[3:6], refs[6:9], refs[9], refs[10]
    first, second = [], []
    for source, buffer, target in zip(ins, held, outs):
        rows = min(source.shape[0], ROWS // 4)
        rows = rows if source.shape[0] % rows == 0 else source.shape[0]
        for i in range(source.shape[0] // rows):
            at = pl.ds(i * rows, rows)
            n = len(first)
            first.append(pltpu.make_async_copy(source.at[at], buffer.at[at], come.at[n]))
            second.append(pltpu.make_async_copy(buffer.at[at], target.at[at], gone.at[n]))
    for copy in first:
        copy.start()
    for copy, after in zip(first, second):
        copy.wait()
        after.start()
    for after in second:
        after.wait()


def on_device(gi, noise, dmd_step, scale_group, wg, wt, wc, scales, mod, tproj):
    vmem = pl.BlockSpec(memory_space=pltpu.VMEM)
    smem = pl.BlockSpec(memory_space=pltpu.SMEM)
    hbm = pl.BlockSpec(memory_space=pl.ANY)
    out_shape = (
        jax.ShapeDtypeStruct((ROWS, D), BF16),
        jax.ShapeDtypeStruct((ROWS, D), BF16),
        jax.ShapeDtypeStruct((HALF, COLS), F32),
    )
    results = pl.pallas_call(
        kernel,
        out_shape=out_shape,
        in_specs=[hbm, hbm, smem, vmem, vmem, vmem, vmem, hbm, vmem, hbm],
        out_specs=(hbm, hbm, vmem),
        scratch_shapes=list(scratch_table().values()),
        compiler_params=pltpu.CompilerParams(
            collective_id=0, has_side_effects=True, vmem_limit_bytes=64 * 1024 * 1024 - 65536
        ),
    )(gi, noise, dmd_step, scale_group.T, wg, wt, wc, scales, mod, tproj)
    return pl.pallas_call(
        copy_results,
        out_shape=out_shape,
        in_specs=[hbm] * 3,
        out_specs=(hbm,) * 3,
        scratch_shapes=[pltpu.VMEM(s.shape, s.dtype) for s in out_shape] + [pltpu.SemaphoreType.DMA((9,))] * 2,
    )(*results)


def solution(mesh):
    return jax.shard_map(
        on_device,
        mesh=mesh,
        in_specs=(
            P(("dp", "fsdp"), None),
            P(("dp", "fsdp"), None),
            P(),
            P(),
            P("fsdp", "dp"),
            P("fsdp", "dp"),
            P("fsdp", "dp"),
            P(None, None, "dp"),
            P(),
            P(),
        ),
        out_specs=(P(("dp", "fsdp"), None), P(("dp", "fsdp"), None), P("fsdp", "dp")),
        check_vma=False,
    )
```

```python
import functools
import math
import types

import jax
import jax.numpy as jnp
from jax import lax
from jax.experimental import pallas as pl
from jax.experimental.pallas import tpu as pltpu
from jax.sharding import PartitionSpec as P

RMS_EPS = 1e-06
SPREAD_EPS = 1e-05
F32 = jnp.float32
BF16 = jnp.bfloat16
MESH_ID = pl.DeviceIdType.MESH

NY, NZ = 4, 8
D = 2560
COLS = 640
ROWS = 128
GROUP = 4 * ROWS
HALF = 40
PAD = 48
BLK = 80
CA = 256
CB = COLS - CA
CUT = 48
TOKENS = 32768
CLIP_ELEMENTS = 16384 * 2560
TPC = 640
PIECES = 9
SLOTS = 4
AY, AZ, BZ, BY, FY, FZ, XY, XZ = range(8)
FINE_Y, FINE_Z = (0, 1, 2), (0, 1, 2)
SHARED = (1, 2)


def ag_table():
    steps = []
    for m in range(3):
        steps += [(m, AY, k, 0) for k in (1, 2)] + [(m, BZ, k, 0) for k in (1, 2, 3, 4)]
        if m in SHARED:
            steps += [(m, FZ, k, i) for k in (1, 2, 3, 4) for i in range(3)] + [(m, XZ, k, 0) for k in (1, 2, 3, 4)]
            steps += [(m, FY, k, i) for k in (1, 2) for i in (0, 1, 7, 4, 8, 9)] + [(m, XY, k, i) for k in (1, 2) for i in (8, 9)]
            continue
        steps += [(m, FZ, k, i) for k in (1, 2, 3, 4) for i in range(4)] if m in FINE_Z else [(m, AZ, k, i) for k in (1, 2, 3, 4) for i in range(2)]
        steps += [(m, FY, k, i) for k in (1, 2) for i in range(8)] if m in FINE_Y else [(m, BY, k, i) for k in (1, 2) for i in range(2)]
    numbers, table = {}, {}
    for m, op, k, i in steps:
        key = (m, op) if op in (XY, XZ) else (m, op, k) if op == FY and k == 2 and i < 8 else (m, op, k, i)
        table[m, op, k, i] = numbers.setdefault(key, len(numbers))
    return table


AG_SEMS = ag_table()


def scratch_table():
    vmem, dma = pltpu.VMEM, pltpu.SemaphoreType.DMA
    return dict(
        W=vmem((3, NY, NZ, BLK, COLS), BF16),
        XO=vmem((3, PAD, COLS), BF16),
        XS=vmem((3, 2, PAD, COLS), BF16),
        XG=vmem((4, ROWS, D), BF16),
        H=vmem((4, GROUP, COLS), BF16),
        NS=vmem((4, ROWS, COLS), BF16),
        CL=vmem((GROUP, COLS), F32),
        NF=vmem((GROUP, COLS), F32),
        NG=vmem((4, GROUP, COLS), BF16),
        JH=vmem((2, 4, GROUP, COLS), BF16),
        ACC=vmem((GROUP, COLS), F32),
        RP=vmem((GROUP, COLS), BF16),
        GP=vmem((GROUP, COLS), F32),
        CT=vmem((GROUP, COLS), BF16),
        SB=vmem((GROUP, COLS), BF16),
        DB=vmem((GROUP, COLS), BF16),
        G=vmem((NY, NZ, BLK, COLS), F32),
        ZS=vmem((8, NY, BLK, CA), BF16),
        ZR=vmem((8, NY, BLK, CA), BF16),
        Y0S=vmem((NZ, BLK, CB), BF16),
        Y0R=vmem((NZ, BLK, CB), BF16),
        Y1S=vmem((NZ, 2, BLK, CB), BF16),
        Y1R=vmem((NZ, 2, BLK, CB), BF16),
        ys=vmem((4, BLK, CA), BF16),
        yr=vmem((4, BLK, CA), BF16),
        zs=vmem((8, BLK, CB), BF16),
        zr=vmem((8, BLK, CB), BF16),
        SC=vmem((3, 8, COLS), F32),
        PK=vmem((8, COLS), F32),
        TP=vmem((SLOTS, 2 * ROWS, TPC), BF16),
        FT=vmem((16, 2 * ROWS), BF16),
        JM=vmem((2, 2, 4, 1, COLS), F32),
        SP=vmem((8, 128), F32),
        SV=vmem((8, 128), F32),
        SPG=vmem((4, 8, 128), F32),
        SPZ=vmem((NZ, 8, 128), F32),
        SPY=vmem((NY, 8, 128), F32),
        GF=vmem((2, PAD, COLS), BF16),
        OW=vmem((2, PAD, COLS), BF16),
        ag_s=dma((3, 6)),
        ag_r=dma((len(set(AG_SEMS.values())),)),
        x_s=dma((3, 2)),
        x_r=dma((3, 2)),
        tk_s=dma((2,)),
        tk_r=dma((3,)),
        ns_s=dma((2,)),
        ns_r=dma((1,)),
        ng_s=dma((1,)),
        ng_r=dma((4, 2)),
        sm_s=dma((2,)),
        sm_r=dma((1,)),
        dm_s=dma((2,)),
        dm_r=dma((1,)),
        sc_s=dma((1,)),
        sc_r=dma((1,)),
        tp_m=dma((SLOTS,)),
        sg_s=dma((1,)),
        sg_r=dma((1,)),
        sz_s=dma((1,)),
        sz_r=dma((1,)),
        sy_s=dma((1,)),
        sy_r=dma((1,)),
        rs_s=dma((5,)),
        b0_r=dma((NZ,)),
        b1_r=dma((NZ,)),
        a_r=dma((4, NY)),
        y_r=dma((1,)),
        z_r=dma((4,)),
        ow_s=dma((2,)),
        ow_r=dma((2,)),
    )


NAMES = tuple(scratch_table())


def kernel(gi, noise, dstep, sgroup, wg, wt, wc, scales, mod, tproj, out_s, out_d, out_w, *rest):
    S = types.SimpleNamespace(**dict(zip(NAMES, rest)))
    dp, fs = lax.axis_index("dp"), lax.axis_index("fsdp")
    h, c = dp // 2, dp % 2
    l, plane = fs % 2, fs // 2
    y, z = plane // NZ, plane % NZ
    oh, oc, ol = 1 - h, 1 - c, 1 - l
    q = 2 * l + c
    cb = 2 * ((h + l) % 2) + c

    def dev(h_, c_, y_, z_, l_):
        return (2 * h_ + c_, (y_ * NZ + z_) * 2 + l_)

    def yy(step):
        return (y + step + NY) % NY

    def zz(step):
        return (z + step + NZ) % NZ

    def remote(src, dst, ss, rs, target):
        return pltpu.make_async_remote_copy(
            src_ref=src, dst_ref=dst, send_sem=ss, recv_sem=rs, device_id=target, device_id_type=MESH_ID
        )

    def send(src, dst, ss, rs, target):
        remote(src, dst, ss, rs, target).start()

    def drain():
        wholes = (
            (XG.at[0:3], S.tk_s),
            (NS.at[0:3], S.ns_s),
            (S.NG.at[0:3], S.ng_s),
            (NS.at[0:3], S.sm_s),
            (NS.at[0:3], S.dm_s),
            (S.SPG.at[0:3], S.sg_s),
            (S.SPZ.at[0:7], S.sz_s),
            (S.SPY.at[0:3], S.sy_s),
        )
        for whole, ss in wholes:
            remote(whole, whole, ss.at[0], S.rs_s.at[0], dev(h, oc, y, z, l)).wait_send()

    def arrived(dst, ss, rs):
        remote(dst, dst, ss, rs, dev(h, oc, y, z, l)).wait_recv()

    greeted = [dev(h, oc, y, z, l), dev(h, oc, y, z, ol)]
    greeted += [dev(h, c, y, z, ol), dev(oh, c, y, z, l), dev(oh, c, y, z, ol)]
    greeted += [dev(h, c, yy(j), z, l) for j in range(1, NY)]
    greeted += [dev(h, c, y, zz(j), l) for j in range(1, NZ)]
    barrier = pltpu.get_barrier_semaphore()
    for target in greeted:
        pl.semaphore_signal(barrier, inc=1, device_id=target, device_id_type=MESH_ID)

    LA, LB = pl.ds(0, CA), pl.ds(CA, CB)
    Z_ORDER = (4, 3, 5, 2, 6, 1, 7, 0)
    Y_ORDER = (2, 1, -1, 0)
    Z_FINE = (0, 1, -1, 2)
    way_of = {r: i % 2 for i, r in enumerate(Z_ORDER)}
    way_of.update({8: 1, 9: 0})

    def along_z(i, l_):
        return {8: 2 + 4 * l_, 9: 3 + 2 * l_}.get(i, i)

    def along_y(m, i, l_):
        return 2 - 3 * l_ if i == 2 and m in SHARED else Z_FINE[i]


    def ag_copies(m, op, k, i):
        W = S.W
        for way in range(2):
            s = 1 - 2 * way
            if op == AY:
                if k == 1:
                    yield W.at[m, y, z, :, LA], W.at[m, yy(-s), z, :, LA], s
                else:
                    part = pl.ds(way * (CA // 2), CA // 2)
                    yield W.at[m, yy(-s), z, :, part], W.at[m, yy(2), z, :, part], s
            elif op == AZ:
                if k < 4 or way == i:
                    some = pl.ds(2 * i, 2)
                    yield W.at[m, some, zz(-s * (k - 1)), :, LA], W.at[m, some, zz(-s * k), :, LA], s
            elif op == FZ:
                if k < 4 or way == i % 2:
                    at = yy(along_y(m, i, l))
                    yield W.at[m, at, zz(-s * (k - 1)), :, LA], W.at[m, at, zz(-s * k), :, LA], s
            elif op == XZ:
                if k < 4 or way == 0:
                    mine, theirs = yy(along_y(m, 2, l)), yy(along_y(m, 2, ol))
                    yield W.at[m, mine, zz(-s * k), :, LA], W.at[m, theirs, zz(-s * k), :, LA], s
            elif op == XY:
                if k == 1 or way == 0:
                    at = yy(-s) if k == 1 else yy(2)
                    yield W.at[m, at, zz(along_z(i, l)), :, LB], W.at[m, at, zz(along_z(i, ol)), :, LB], s
            elif op == BZ:
                some = pl.ds(0, BLK) if k < 4 else (pl.ds(0, CUT), pl.ds(CUT, BLK - CUT))[way]
                yield W.at[m, y, zz(-s * (k - 1)), some, LB], W.at[m, y, zz(-s * k), some, LB], s
            else:
                some = pl.ds(4 * i, 4) if op == BY else zz(along_z(i, l))
                if k == 1:
                    yield W.at[m, y, some, :, LB], W.at[m, yy(-s), some, :, LB], s
                elif way == (i if op == BY else way_of[i]):
                    yield W.at[m, yy(-s), some, :, LB], W.at[m, yy(2), some, :, LB], s

    def ag_sems(m, op, k, i):
        group = {AY: 0, AZ: 1, FZ: 1, BZ: 2, BY: 3, FY: 3, XY: 4, XZ: 5}[op]
        return S.ag_s.at[m, group], S.ag_r.at[AG_SEMS[m, op, k, i]]

    def ag_go(m, op, k, i=0):
        ss, rs = ag_sems(m, op, k, i)
        for src, _, s in ag_copies(m, op, k, i):
            if op in (XY, XZ):
                target = dev(oh, c, y, z, ol)
            else:
                target = dev(h, c, y, zz(s), l) if op in (AZ, BZ, FZ) else dev(h, c, yy(s), z, l)
            remote(src, src, ss, rs, target).start()

    def ag_got(m, op, k, i=0):
        W = S.W
        ss, rs = ag_sems(m, op, k, i)
        if op == XZ or op == XY or (op == FY and k == 2 and i < 8):
            if op == XZ and k == 4:
                arrived(W.at[m, 0, 0:7, :, LA], ss, rs)
            elif op == XY and k == 2 and i == 9:
                arrived(W.at[m, 0, 0:6, :, LB], ss, rs)
            elif op == FY and i == 4:
                arrived(W.at[m, 0, 0:4, :, LB] if m in SHARED else W.at[m, 0, :, :, LB], ss, rs)
            return
        if op == AY:
            both = W.at[m, 0:2, z, :, LA] if k == 1 else W.at[m, 0, z, :, LA]
        elif op == AZ:
            both = W.at[m, :, z, :, LA] if k < 4 else W.at[m, 0:2, z, :, LA]
        elif op in (FZ, XZ):
            both = W.at[m, 0:2, z, :, LA] if k < 4 else W.at[m, 0, z, :, LA]
        elif op == BZ:
            both = W.at[m, 0, 0:2, :, LB] if k < 4 else W.at[m, 0, 0, :, LB]
        elif op == BY:
            both = W.at[m, 0, :, :, LB] if k == 1 else W.at[m, 0, 0:4, :, LB]
        else:
            both = W.at[m, 0, 0:2, :, LB] if k == 1 else W.at[m, 0, 0, :, LB]
        arrived(both, ss, rs)

    def ag_sent(m):
        W = S.W
        wholes = [W.at[m, 0:3, 0, :, LA], W.at[m, :, 0:7, :, LA], W.at[m, 0, 0:7, :, LB], W.at[m, 0:3, :, :, LB]]
        if m in SHARED:
            wholes[1], wholes[3] = W.at[m, 0:3, 0:7, :, LA], W.at[m, 0:3, 0:6, :, LB]
            wholes += [W.at[m, 0, 0:6, :, LB], W.at[m, 0, 0:7, :, LA]]
        for group, whole in enumerate(wholes):
            remote(whole, whole, S.ag_s.at[m, group], S.ag_r.at[0], dev(h, oc, y, z, l)).wait_send()

    XO, XS = S.XO, S.XS

    def x_second(m):
        return remote(XO.at[m], XS.at[m, 1], S.x_s.at[m, 1], S.x_r.at[m, 1], dev(h, c, y, z, 0))

    def x_first(m, slot):
        return remote(XO.at[m], XS.at[m, slot], S.x_s.at[m, 0], S.x_r.at[m, slot], dev(oh, c, y, z, 1))

    def x_prepare():
        for m, codes in enumerate((wg, wt, wc)):
            own = codes[...].astype(F32)
            own = jnp.concatenate([own, jnp.zeros((PAD - HALF, COLS), F32)], axis=0).astype(BF16)
            XO[m] = own

            @pl.when(l == 0)
            def _():
                XS[m, 0] = own

    def x_start(m):
        @pl.when(l == 0)
        def _():
            x_first(m, 0).start()

        @pl.when(l == 1)
        def _():
            x_first(m, 1).start()
            x_second(m).start()

    def assemble(m):
        @pl.when(l == 1)
        def _():
            arrived(XS.at[m, 0], S.x_s.at[m, 0], S.x_r.at[m, 0])

        arrived(XS.at[m, 1], S.x_s.at[m, 1], S.x_r.at[m, 1])
        both = [XS[m, i].astype(F32)[:HALF] for i in range(2)]
        S.W[m, y, z] = jnp.concatenate(both, axis=0).astype(BF16)

    XG, NS, SC = S.XG, S.NS, S.SC
    tok_own = pltpu.make_async_copy(gi, XG.at[q], S.tk_s.at[1])

    def tok_near():
        send(gi, XG.at[q], S.tk_s.at[0], S.tk_r.at[1], dev(h, oc, y, z, l))

    def tok_far():
        send(gi, XG.at[q], S.tk_s.at[0], S.tk_r.at[0], dev(h, c, y, z, ol))

    def tok_forward():
        arrived(XG.at[q_far], S.tk_s.at[0], S.tk_r.at[0])
        send(XG.at[q_far], XG.at[q_far], S.tk_s.at[0], S.tk_r.at[2], dev(h, oc, y, z, l))

    q_far, q_near, q_last = 2 * ol + c, 2 * l + oc, 2 * ol + oc

    def columns(c_, l_):
        return pl.ds(pl.multiple_of((2 * ((h + l_) % 2) + c_) * COLS, COLS), COLS)

    others = ((oc, l), (c, ol), (oc, ol))

    def noise_send(i):
        c_, l_ = others[i]
        send(noise.at[:, columns(c_, l_)], NS.at[q], S.ns_s.at[0], S.ns_r.at[0], dev(h, c_, y, z, l_))

    def noise_wait():
        noise_own.wait()
        arrived(NS.at[0:3], S.ns_s.at[0], S.ns_r.at[0])

    noise_own = pltpu.make_async_copy(noise.at[:, columns(c, l)], NS.at[q], S.ns_s.at[1])

    def scale_copy():
        return remote(scales, SC, S.sc_s.at[0], S.sc_r.at[0], dev(oh, c, y, z, 1))

    def scale_own():
        return pltpu.make_async_copy(scales, SC, S.sc_r.at[0])

    def scale_start():
        @pl.when(l == 0)
        def _():
            scale_copy().start()
            scale_own().start()

    def piece(i):
        m, j = i // PIECES, i % PIECES
        if j < 8:
            offset = j * COLS
        else:
            offset = pl.multiple_of(2 * D + cb * COLS, COLS)
        return pltpu.make_async_copy(tproj.at[m, :, pl.ds(offset, TPC)], S.TP.at[i % SLOTS], S.tp_m.at[i % SLOTS])

    def gen_hat(block, part):
        H = S.H

        def rows(r, carry):
            at = pl.ds(pl.multiple_of(part * 32 + r * 16, 16), 16)
            x = XG[block, at, :].astype(F32)
            inv = lax.rsqrt(jnp.sum(x * x, axis=1, keepdims=True) / D + RMS_EPS)
            hat = (x * inv * (1.0 + mod[0, 1:2, :]) + mod[0, 0:1, :]).astype(BF16)
            to = pl.ds(pl.multiple_of(block * ROWS + part * 32 + r * 16, 16), 16)
            for k in range(4):
                H[k, to, :] = hat[:, k * COLS : (k + 1) * COLS]
            return carry

        lax.fori_loop(0, 2, rows, 0)

    def features():
        index = lax.broadcasted_iota(jnp.int32, (1, ROWS), 1).astype(F32)
        frequency = jnp.exp(index * (-math.log(10000.0) / ROWS))
        phase = jnp.full((1, ROWS), dstep[h], jnp.int32).astype(F32) * frequency
        feature = jnp.concatenate([jnp.cos(phase), jnp.sin(phase)], axis=1)
        hi = feature.astype(BF16).astype(F32)
        mid = (feature - hi).astype(BF16).astype(F32)
        low = (feature - hi - mid).astype(BF16).astype(F32)
        row = lax.broadcasted_iota(jnp.int32, (16, 2 * ROWS), 0)
        a, b, d = [jnp.broadcast_to(v, (16, 2 * ROWS)) for v in (hi, mid, low)]
        S.FT[...] = jnp.where(row == 0, a, jnp.where(row == 1, b, jnp.where(row == 2, d, 0.0))).astype(BF16)

    def judge_piece(i):
        m, j = i // PIECES, i % PIECES
        piece(i).wait()
        lifted = jnp.dot(S.FT[...], S.TP[i % SLOTS], preferred_element_type=F32)
        lifted = jnp.sum(lifted, axis=0, keepdims=True)
        if j < 8:
            S.JM[m, j // 4, j % 4] = lifted + mod[m + 1, j // 4 : j // 4 + 1, (j % 4) * COLS : (j % 4 + 1) * COLS]
        else:
            gate = mod[m + 1, 2:3, pl.ds(pl.multiple_of(cb * COLS, COLS), COLS)]
            S.PK[m + 4 : m + 5, :] = lifted + gate
        if i + SLOTS < 2 * PIECES:
            piece(i + SLOTS).start()

    def factors():
        arrived(SC, S.sc_s.at[0], S.sc_r.at[0])
        row = lax.broadcasted_iota(jnp.int32, (8, COLS), 0)
        for m in range(3):
            group = jnp.where(h == 0, sgroup[0:1, m : m + 1], sgroup[1:2, m : m + 1])
            picked = jnp.sum(jnp.where(row == group, SC[m], 0.0), axis=0, keepdims=True)
            if m == 0:
                gate = mod[0, 2:3, pl.ds(pl.multiple_of(cb * COLS, COLS), COLS)]
            else:
                gate = S.PK[m + 3 : m + 4, :]
            S.PK[m : m + 1, :] = gate * picked

    def level():
        return jnp.full((1, COLS), dstep[h], jnp.int32).astype(F32) / 1000.0

    def product(lhs, m, k, first=False):
        ACC = S.ACC
        part = jnp.dot(lhs[k], S.W[m, k].reshape(COLS, COLS), preferred_element_type=F32)
        if first:
            ACC[...] = part
        else:
            ACC[...] += part

    TILE = 64

    def clean_rows(block):
        lev = level()
        here = pl.ds(pl.multiple_of(cb * COLS, COLS), COLS)

        def rows(r, carry):
            at = pl.ds(pl.multiple_of(block * ROWS + r * TILE, TILE), TILE)
            inner = pl.ds(pl.multiple_of(r * TILE, TILE), TILE)
            branch = (S.ACC[at, :] * S.PK[0:1, :]).astype(BF16)
            clean = XG[block, inner, here].astype(F32) + branch.astype(F32)
            noisy = (1.0 - lev) * clean + lev * NS[block, inner, :].astype(F32)
            S.CL[at, :] = clean
            S.NF[at, :] = noisy
            S.SB[at, :] = clean.astype(BF16)
            S.NG[cb, at, :] = noisy.astype(BF16)
            return carry

        lax.fori_loop(0, ROWS // TILE, rows, 0)

    def block_rows(block):
        return pl.ds(block * ROWS, ROWS)

    def noisy_send(block):
        own = S.NG.at[cb, block_rows(block)]
        send(own, own, S.ng_s.at[0], S.ng_r.at[block, 0], dev(h, c, y, z, ol))
        send(own, own, S.ng_s.at[0], S.ng_r.at[block, 1], dev(h, oc, y, z, l))

    far = 2 * ((h + ol) % 2) + c

    def noisy_forward(block):
        got = S.NG.at[far, block_rows(block)]
        arrived(got, S.ng_s.at[0], S.ng_r.at[block, 0])
        send(got, got, S.ng_s.at[0], S.ng_r.at[block, 1], dev(h, oc, y, z, l))

    def noisy_wait(block):
        arrived(S.NG.at[0:2, block_rows(block)], S.ng_s.at[0], S.ng_r.at[block, 1])

    def judge_hats(part):
        NG, JH, JM = S.NG, S.JH, S.JM

        def rows(r, carry):
            at = pl.ds(pl.multiple_of(part * 64 + r * 16, 16), 16)
            v = [NG[k, at, :].astype(F32) for k in range(4)]
            total = sum(jnp.sum(t * t, axis=1, keepdims=True) for t in v)
            inv = lax.rsqrt(total / D + RMS_EPS)
            for k in range(4):
                normed = (v[k] * inv).astype(BF16).astype(F32)
                for j in range(2):
                    JH[j, k, at, :] = (normed * (1.0 + JM[j, 1, k]) + JM[j, 0, k]).astype(BF16)
            return carry

        lax.fori_loop(0, 4, rows, 0)

    def return_rows(buf, out, ss, rs):
        here = pl.ds(pl.multiple_of(cb * COLS, COLS), COLS)
        for i, (c_, l_) in enumerate(others):
            block = pl.ds(pl.multiple_of((2 * l_ + c_) * ROWS, ROWS), ROWS)
            send(buf.at[block], out.at[:, here], ss.at[0], rs.at[0], dev(h, c_, y, z, l_))
        block = pl.ds(pl.multiple_of(q * ROWS, ROWS), ROWS)
        own = pltpu.make_async_copy(buf.at[block], out.at[:, here], ss.at[1])
        own.start()
        return own

    def return_wait(out, ss, rs):
        arrived(NS.at[0:3], ss.at[0], rs.at[0])

    def judged(m, half):
        ACC = S.ACC
        at = pl.ds(half * (GROUP // 2), GROUP // 2)
        for k in range(4):
            part = jnp.dot(S.JH[m - 1, k, at, :], S.W[m, k].reshape(COLS, COLS), preferred_element_type=F32)
            if k == 0:
                ACC[at, :] = part
            else:
                ACC[at, :] += part

    def half_tiles(half, body, carry):
        tiles = GROUP // 2 // TILE
        return lax.fori_loop(half * tiles, (half + 1) * tiles, body, carry)

    def real_rows(half):
        lev = level()

        def rows(r, total):
            at = pl.ds(pl.multiple_of(r * TILE, TILE), TILE)
            real = (S.ACC[at, :] * S.PK[1:2, :]).astype(BF16)
            S.RP[at, :] = real
            noisy = S.NF[at, :]
            gone = jnp.abs(S.CL[at, :] - (noisy - lev * (noisy + real.astype(F32))))
            return total + jnp.sum(gone.reshape(TILE // 8, 8, COLS), axis=0)

        total = half_tiles(half, rows, jnp.zeros((8, COLS), F32))
        total = jnp.sum(jnp.sum(total, axis=1, keepdims=True), axis=0, keepdims=True)
        total = jnp.broadcast_to(total, (8, 128))
        S.SP[...] = total if half == 0 else S.SP[...] + total

    def gap_rows(half):
        lev = level()

        def rows(r, carry):
            at = pl.ds(pl.multiple_of(r * TILE, TILE), TILE)
            fake = (S.ACC[at, :] * S.PK[2:3, :]).astype(BF16).astype(F32)
            gap = lev * (S.RP[at, :].astype(F32) - fake)
            S.GP[at, :] = gap
            S.CT[at, :] = (gap * S.PK[0:1, :]).astype(BF16)
            return carry

        half_tiles(half, rows, 0)

    def spread_group_start():
        S.SPG[q] = S.SP[...]
        for c_, l_ in others:
            send(S.SP, S.SPG.at[q], S.sg_s.at[0], S.sg_r.at[0], dev(h, c_, y, z, l_))

    def spread_z_start():
        SPG, SPZ = S.SPG, S.SPZ
        arrived(SPG.at[0:3], S.sg_s.at[0], S.sg_r.at[0])
        SPZ[z] = (SPG[0] + SPG[1]) + (SPG[2] + SPG[3])
        for j in range(1, NZ):
            send(SPZ.at[z], SPZ.at[z], S.sz_s.at[0], S.sz_r.at[0], dev(h, c, y, zz(j), l))

    def spread_y_start():
        SPZ, SPY = S.SPZ, S.SPY
        arrived(SPZ.at[0:7], S.sz_s.at[0], S.sz_r.at[0])
        total = SPZ[0]
        for j in range(1, NZ):
            total = total + SPZ[j]
        SPY[y] = total
        for j in range(1, NY):
            send(SPY.at[y], SPY.at[y], S.sy_s.at[0], S.sy_r.at[0], dev(h, c, yy(j), z, l))

    def spread_value():
        SPY = S.SPY
        arrived(SPY.at[0:3], S.sy_s.at[0], S.sy_r.at[0])
        total = SPY[0]
        for j in range(1, NY):
            total = total + SPY[j]
        S.SV[...] = total / CLIP_ELEMENTS + SPREAD_EPS

    def dmd_rows():
        def rows(r, carry):
            at = pl.ds(pl.multiple_of(r * TILE, TILE), TILE)
            S.DB[at, :] = (S.GP[at, :] / S.SV[0:1, 0:1]).astype(BF16)
            return carry

        lax.fori_loop(0, GROUP // TILE, rows, 0)

    G = S.G

    def grad(k, lanes, width):
        block = lax.dot_general(S.H[k], S.CT[:, lanes], (((0,), (0,)), ((), ())), preferred_element_type=F32)
        G[k, :, :, lanes] = block.reshape(NZ, BLK, width)

    def grad_b(k):
        grad(k, LB, CB)

    def grad_a(k):
        grad(k, LA, CA)

    def big_y0(r):
        S.Y0S[r] = G[yy(2), zz(r), :, LB].astype(BF16)
        target = dev(h, c, yy(1 - 2 * way_of[r]), z, l)
        remote(S.Y0S.at[r], S.Y0R.at[r], S.rs_s.at[0], S.b0_r.at[r], target).start()

    def big_y1(r):
        for way in range(2):
            s = 1 - 2 * way
            v = G[yy(s), zz(r), :, LB]
            if way == way_of[r]:
                arrived(S.Y0R.at[r], S.rs_s.at[0], S.b0_r.at[r])
                v = v + S.Y0R[r].astype(F32)
            S.Y1S[r, way] = v.astype(BF16)
            remote(S.Y1S.at[r, way], S.Y1R.at[r, way], S.rs_s.at[1], S.b1_r.at[r], dev(h, c, yy(s), z, l)).start()

    def big_y2(r):
        Y1R = S.Y1R
        arrived(Y1R.at[r], S.rs_s.at[1], S.b1_r.at[r])
        G[y, zz(r), :, LB] = G[y, zz(r), :, LB] + Y1R[r, 0].astype(F32) + Y1R[r, 1].astype(F32)

    def slot(k, way):
        return 0 if k == 1 else 2 * k - 3 + way

    def pair(k):
        return pl.ds(slot(k, 0), 1 if k == 1 else 2)

    def big_z(k, j):
        ZS, ZR = S.ZS, S.ZR
        at = yy(Y_ORDER[j])
        if k > 1:
            arrived(ZR.at[pair(k - 1), j], S.rs_s.at[2], S.a_r.at[k - 2, j])
        for way in range(2):
            s = 1 - 2 * way
            if k == 5 or (k == 1 and way != j % 2):
                continue
            v = G[at, zz(s * (5 - k)), :, LA]
            if k > 2 or (k == 2 and way == j % 2):
                v = v + ZR[slot(k - 1, way), j].astype(F32)
            n = slot(k, way)
            ZS[n, j] = v.astype(BF16)
            remote(ZS.at[n, j], ZR.at[n, j], S.rs_s.at[2], S.a_r.at[k - 1, j], dev(h, c, y, zz(s), l)).start()
        if k == 5:
            G[at, z, :, LA] = G[at, z, :, LA] + ZR[5, j].astype(F32) + ZR[6, j].astype(F32)

    def small_y(j):
        ys, yr = S.ys, S.yr
        if j < 3:
            at = yy(Y_ORDER[j])
            ys[j] = G[at, z, :, LA].astype(BF16)
            remote(ys.at[j], yr.at[j], S.rs_s.at[3], S.y_r.at[0], dev(h, c, at, z, l)).start()
        else:
            arrived(yr.at[0:3], S.rs_s.at[3], S.y_r.at[0])
            total = yr[0].astype(F32) + yr[1].astype(F32) + yr[2].astype(F32)
            G[y, z, :, LA] = G[y, z, :, LA] + total

    def small_z(k):
        zs, zr = S.zs, S.zr
        if k > 1:
            arrived(zr.at[0] if k == 2 else zr.at[pair(k - 1)], S.rs_s.at[4], S.z_r.at[k - 2])
        for way in range(2):
            s = 1 - 2 * way
            some = (pl.ds(0, CUT), pl.ds(CUT, BLK - CUT))[way]
            target = dev(h, c, y, zz(s), l)
            n = slot(k, way)
            if k == 1:
                zs[0, some, :] = G[y, zz(4), some, LB].astype(BF16)
                remote(zs.at[0, some], zr.at[0, some], S.rs_s.at[4], S.z_r.at[0], target).start()
            elif k < 5:
                at = zz(s * (5 - k))
                if k > 2:
                    zs[n] = (G[y, at, :, LB] + zr[slot(k - 1, way)].astype(F32)).astype(BF16)
                else:
                    other = (pl.ds(CUT, BLK - CUT), pl.ds(0, CUT))[way]
                    zs[n, some, :] = (G[y, at, some, LB] + zr[0, some, :].astype(F32)).astype(BF16)
                    zs[n, other, :] = G[y, at, other, LB].astype(BF16)
                remote(zs.at[n], zr.at[n], S.rs_s.at[4], S.z_r.at[k - 1], target).start()
        if k == 5:
            G[y, z, :, LB] = G[y, z, :, LB] + zr[5].astype(F32) + zr[6].astype(F32)

    def rings_sent():
        wholes = (S.Y0S, S.Y1S, S.ZS.at[0:7], S.ys.at[0:3], S.zs.at[0:7])
        for i, whole in enumerate(wholes):
            remote(whole, whole, S.rs_s.at[i], S.b0_r.at[0], dev(h, oc, y, z, l)).wait_send()

    tok_own.start()
    noise_own.start()
    for i in range(SLOTS):
        piece(i).start()
    x_prepare()
    features()
    pl.semaphore_wait(barrier, len(greeted))
    x_start(0)
    x_start(1)
    x_start(2)
    tok_near()
    scale_start()
    tok_own.wait()
    gen_hat(q, 0)
    gen_hat(q, 1)
    gen_hat(q, 2)
    gen_hat(q, 3)
    judge_piece(0)
    judge_piece(1)
    judge_piece(2)
    judge_piece(3)
    judge_piece(4)
    judge_piece(5)
    judge_piece(6)
    judge_piece(7)
    judge_piece(8)
    judge_piece(9)
    judge_piece(10)
    judge_piece(11)
    judge_piece(12)
    judge_piece(13)
    judge_piece(14)
    assemble(0)
    ag_go(0, AY, 1)
    ag_go(0, BZ, 1)
    ag_go(0, FZ, 1, 0)
    ag_go(0, FY, 1, 0)
    judge_piece(15)
    arrived(XG.at[q_near], S.tk_s.at[0], S.tk_r.at[1])
    gen_hat(q_near, 0)
    gen_hat(q_near, 1)
    gen_hat(q_near, 2)
    gen_hat(q_near, 3)
    judge_piece(16)
    judge_piece(17)
    assemble(1)
    ag_go(1, AY, 1)
    ag_go(1, BZ, 1)
    ag_go(1, FY, 1, 0)
    ag_got(0, AY, 1)
    ag_go(0, AY, 2)
    ag_go(0, FZ, 1, 1)
    ag_go(0, FZ, 1, 2)
    ag_got(0, BZ, 1)
    ag_go(0, BZ, 2)
    ag_go(0, FY, 1, 1)
    ag_go(0, FY, 1, 7)
    tok_far()
    assemble(2)
    ag_got(0, FZ, 1, 0)
    ag_go(0, FZ, 2, 0)
    factors()
    ag_got(0, FY, 1, 0)
    ag_go(0, FY, 2, 0)
    ag_got(1, BZ, 1)
    ag_go(1, BZ, 2)
    ag_go(2, AY, 1)
    ag_got(0, FZ, 1, 1)
    ag_go(0, FZ, 2, 1)
    ag_got(1, AY, 1)
    ag_go(1, AY, 2)
    ag_got(0, FZ, 1, 2)
    ag_go(0, FZ, 2, 2)
    ag_got(0, FY, 1, 1)
    ag_go(0, FY, 2, 1)
    ag_got(0, BZ, 2)
    ag_go(0, BZ, 3)
    ag_go(0, FY, 1, 2)
    ag_go(0, FY, 1, 6)
    ag_got(0, FZ, 2, 0)
    ag_go(0, FZ, 3, 0)
    ag_got(0, AY, 2)
    ag_go(0, FZ, 1, 3)
    ag_got(0, FY, 1, 7)
    ag_go(0, FY, 2, 7)
    ag_got(0, FZ, 2, 1)
    ag_go(0, FZ, 3, 1)
    ag_got(2, AY, 1)
    ag_go(2, AY, 2)
    ag_got(0, FZ, 2, 2)
    ag_go(0, FZ, 3, 2)
    ag_got(0, FY, 1, 2)
    ag_go(0, FY, 2, 2)
    ag_got(1, BZ, 2)
    ag_go(1, FY, 1, 8)
    ag_got(0, BZ, 3)
    ag_go(0, BZ, 4)
    ag_go(0, FY, 1, 3)
    ag_got(0, FZ, 3, 0)
    ag_go(0, FZ, 4, 0)
    ag_go(0, FY, 1, 5)
    ag_go(1, BZ, 3)
    ag_got(0, FZ, 1, 3)
    ag_go(0, FZ, 2, 3)
    ag_got(0, FY, 1, 6)
    ag_go(0, FY, 2, 6)
    ag_got(0, FZ, 3, 1)
    ag_go(0, FZ, 4, 1)
    ag_got(0, FZ, 3, 2)
    ag_go(0, FZ, 4, 2)
    ag_got(1, FY, 1, 8)
    ag_go(1, XY, 1, 8)
    ag_got(0, BZ, 4)
    ag_go(0, FY, 1, 4)
    ag_got(1, AY, 2)
    ag_go(1, FZ, 1, 2)
    ag_got(0, FY, 1, 3)
    ag_go(0, FY, 2, 3)
    ag_got(1, BZ, 3)
    ag_go(1, BZ, 4)
    tok_forward()
    noise_send(0)
    noise_send(1)
    noise_send(2)
    ag_got(0, FY, 1, 5)
    ag_go(0, FY, 2, 5)
    ag_go(1, FZ, 1, 0)
    gen_hat(q_far, 0)
    ag_got(0, FZ, 2, 3)
    ag_go(0, FZ, 3, 3)
    ag_go(1, FY, 1, 9)
    gen_hat(q_far, 1)
    gen_hat(q_far, 2)
    gen_hat(q_far, 3)
    ag_go(1, FY, 2, 8)
    ag_go(1, FZ, 1, 1)
    ag_got(0, FY, 1, 4)
    ag_go(0, FY, 2, 4)
    ag_got(1, FZ, 1, 2)
    ag_go(1, XZ, 1)
    ag_go(1, FZ, 2, 2)
    ag_go(1, FY, 1, 1)
    ag_go(2, BZ, 1)
    ag_go(1, FY, 1, 7)
    ag_got(1, FZ, 1, 0)
    ag_go(1, FZ, 2, 0)
    ag_got(0, FZ, 3, 3)
    ag_go(0, FZ, 4, 3)
    arrived(XG.at[q_last], S.tk_s.at[0], S.tk_r.at[2])
    gen_hat(q_last, 0)
    ag_got(1, FY, 1, 9)
    ag_go(1, XY, 1, 9)
    gen_hat(q_last, 1)
    gen_hat(q_last, 2)
    gen_hat(q_last, 3)
    ag_go(1, FY, 2, 9)
    ag_got(0, FZ, 4, 0)
    product(S.H, 0, y, True)
    ag_got(1, FZ, 2, 2)
    ag_go(1, FZ, 3, 2)
    ag_go(1, XZ, 2)
    ag_got(1, BZ, 4)
    ag_go(1, FY, 1, 4)
    ag_got(0, FZ, 4, 1)
    product(S.H, 0, yy(1))
    ag_got(1, FZ, 1, 1)
    ag_go(1, FZ, 2, 1)
    ag_got(0, FZ, 4, 2)
    product(S.H, 0, yy(-1))
    ag_got(1, FY, 2, 8)
    ag_go(1, XY, 2, 8)
    ag_got(1, FY, 1, 0)
    ag_go(1, FY, 2, 0)
    ag_got(1, FY, 1, 1)
    ag_go(1, FY, 2, 1)
    ag_got(2, BZ, 1)
    ag_go(2, BZ, 2)
    ag_got(1, FZ, 2, 0)
    ag_go(1, FZ, 3, 0)
    ag_got(1, FY, 1, 7)
    ag_go(1, FY, 2, 7)
    ag_got(0, FZ, 4, 3)
    ag_got(0, FY, 2, 0)
    ag_got(0, FY, 2, 1)
    ag_got(0, FY, 2, 7)
    ag_got(0, FY, 2, 2)
    ag_got(0, FY, 2, 6)
    ag_got(0, FY, 2, 3)
    ag_got(0, FY, 2, 5)
    ag_got(0, FY, 2, 4)
    product(S.H, 0, yy(2))
    ag_got(1, FZ, 3, 2)
    ag_go(1, FZ, 4, 2)
    ag_go(1, XZ, 3)
    ag_go(2, FY, 1, 0)
    noise_wait()
    clean_rows(0)
    noisy_send(0)
    clean_rows(1)
    noisy_send(1)
    clean_rows(2)
    noisy_send(2)
    ag_got(2, AY, 2)
    ag_go(2, FZ, 1, 2)
    clean_rows(3)
    noisy_send(3)
    ag_got(1, FY, 2, 9)
    ag_go(1, XY, 2, 9)
    ag_got(1, FY, 1, 4)
    ag_go(1, FY, 2, 4)
    ag_got(1, FZ, 2, 1)
    ag_go(1, FZ, 3, 1)
    ag_go(2, FZ, 1, 0)
    ag_got(2, BZ, 2)
    ag_go(2, FY, 1, 8)
    ag_got(1, FZ, 3, 0)
    ag_go(1, FZ, 4, 0)
    ag_go(2, FY, 1, 1)
    ag_got(1, FZ, 4, 2)
    ag_go(1, XZ, 4)
    ag_go(2, BZ, 3)
    ag_got(2, FZ, 1, 2)
    ag_go(2, XZ, 1)
    ag_go(2, FY, 1, 7)
    ag_go(2, FZ, 2, 2)
    noisy_forward(0)
    ag_got(1, FZ, 3, 1)
    ag_go(1, FZ, 4, 1)
    ag_got(2, FY, 1, 8)
    ag_go(2, FY, 2, 8)
    ag_go(2, XY, 1, 8)
    ag_got(2, FZ, 1, 0)
    ag_go(2, FZ, 2, 0)
    ag_got(2, FY, 1, 0)
    ag_go(2, FY, 2, 0)
    ag_go(2, FZ, 1, 1)
    ag_got(2, FY, 1, 1)
    ag_go(2, FY, 2, 1)
    ag_got(2, BZ, 3)
    ag_go(2, BZ, 4)
    ag_go(2, FY, 1, 9)
    noisy_wait(0)
    judge_hats(0)
    judge_hats(1)
    noisy_forward(1)
    ag_got(2, FZ, 2, 2)
    ag_go(2, FZ, 3, 2)
    ag_go(2, XZ, 2)
    ag_got(2, FY, 1, 7)
    ag_go(2, FY, 2, 7)
    ag_got(2, FY, 2, 8)
    ag_go(2, XY, 2, 8)
    ag_got(2, FZ, 2, 0)
    ag_go(2, FZ, 3, 0)
    ag_got(2, FZ, 1, 1)
    ag_go(2, FZ, 2, 1)
    ag_got(2, BZ, 4)
    ag_go(2, FY, 1, 4)
    noisy_wait(1)
    judge_hats(2)
    ag_got(2, FY, 1, 9)
    ag_go(2, FY, 2, 9)
    ag_go(2, XY, 1, 9)
    judge_hats(3)
    noisy_forward(2)
    ag_got(2, FZ, 3, 2)
    ag_go(2, FZ, 4, 2)
    ag_got(1, FZ, 4, 0)
    ag_got(1, FZ, 4, 1)
    ag_got(1, XY, 1, 8)
    ag_got(1, XY, 1, 9)
    ag_got(1, XZ, 1)
    ag_got(1, XZ, 2)
    ag_got(1, XZ, 3)
    ag_got(1, XZ, 4)
    ag_got(1, XY, 2, 8)
    ag_got(1, XY, 2, 9)
    ag_got(1, FY, 2, 0)
    ag_got(1, FY, 2, 1)
    ag_got(1, FY, 2, 7)
    ag_got(1, FY, 2, 4)
    judged(1, 0)
    ag_go(2, XZ, 3)
    ag_got(2, FZ, 3, 0)
    ag_go(2, FZ, 4, 0)
    ag_got(2, FZ, 2, 1)
    ag_go(2, FZ, 3, 1)
    real_rows(0)
    ag_got(2, FY, 1, 4)
    ag_go(2, FY, 2, 4)
    ag_got(2, FZ, 4, 2)
    ag_go(2, XZ, 4)
    noisy_wait(2)
    judge_hats(4)
    noisy_forward(3)
    judge_hats(5)
    ag_got(2, FY, 2, 9)
    ag_go(2, XY, 2, 9)
    ag_got(2, FZ, 3, 1)
    ag_go(2, FZ, 4, 1)
    noisy_wait(3)
    judge_hats(6)
    judge_hats(7)
    judged(1, 1)
    real_rows(1)
    spread_group_start()
    ag_got(2, FZ, 4, 0)
    ag_got(2, FZ, 4, 1)
    ag_got(2, XY, 1, 8)
    ag_got(2, XY, 1, 9)
    ag_got(2, XZ, 1)
    ag_got(2, XZ, 2)
    ag_got(2, XZ, 3)
    ag_got(2, XZ, 4)
    ag_got(2, XY, 2, 8)
    ag_got(2, XY, 2, 9)
    ag_got(2, FY, 2, 0)
    ag_got(2, FY, 2, 1)
    ag_got(2, FY, 2, 7)
    ag_got(2, FY, 2, 4)
    judged(2, 0)
    gap_rows(0)
    judged(2, 1)
    sample_own = return_rows(S.SB, out_s, S.sm_s, S.sm_r)
    spread_z_start()
    gap_rows(1)
    grad_b(yy(2))
    big_y0(4)
    big_y0(3)
    big_y0(5)
    big_y0(2)
    grad_a(yy(2))
    big_z(1, 0)
    grad_b(yy(1))
    grad_b(yy(-1))
    grad_a(yy(1))
    big_z(1, 1)
    grad_a(yy(-1))
    big_z(1, 2)
    big_y1(4)
    big_z(2, 0)
    big_y1(3)
    big_y0(6)
    big_y0(1)
    grad_a(y)
    big_z(1, 3)
    spread_y_start()
    big_z(2, 1)
    big_y1(5)
    big_z(2, 2)
    big_y1(2)
    big_y0(7)
    big_y0(0)
    grad_b(y)
    big_z(2, 3)
    big_z(3, 0)
    big_y2(4)
    small_z(1)
    big_y1(6)
    big_z(3, 1)
    big_y2(3)
    big_y2(5)
    small_z(2)
    spread_value()
    dmd_rows()
    dmd_own = return_rows(S.DB, out_d, S.dm_s, S.dm_r)
    big_z(3, 2)
    big_z(3, 3)
    big_y1(1)
    big_z(4, 0)
    big_y1(7)
    big_z(4, 1)
    big_y1(0)
    big_y2(2)
    big_y2(6)
    small_z(3)
    big_z(4, 2)
    big_z(4, 3)
    big_z(5, 0)
    small_y(0)
    big_y2(1)
    big_y2(7)
    big_z(5, 1)
    small_y(1)
    big_z(5, 2)
    small_y(2)
    small_z(4)
    ag_sent(0)
    ag_sent(1)
    ag_sent(2)
    sample_own.wait()
    big_z(5, 3)
    big_y2(0)
    small_y(3)
    small_z(5)
    GF, OW = S.GF, S.OW
    done = G[y, z] / S.SV[0:1, 0:1] / TOKENS

    def own_row(row, slot, target):
        return remote(GF.at[row], OW.at[slot], S.ow_s.at[row], S.ow_r.at[slot], target)

    for row in range(2):
        part = jnp.concatenate([done[row * HALF : (row + 1) * HALF], jnp.zeros((PAD - HALF, COLS), F32)], axis=0)
        GF[row] = part.astype(BF16)

    @pl.when(l == 0)
    def _():
        own_row(1, 0, dev(h, c, y, z, 1)).start()
        OW[0] = GF[0]

    @pl.when(l == 1)
    def _():
        own_row(0, 1, dev(oh, c, y, z, 0)).start()
        own_row(1, 1, dev(oh, c, y, z, 1)).start()
        arrived(OW.at[0], S.ow_s.at[0], S.ow_r.at[0])

    arrived(OW.at[1], S.ow_s.at[1], S.ow_r.at[1])
    out_w[...] = (OW[0].astype(F32) + OW[1].astype(F32))[:HALF]
    return_wait(out_s, S.sm_s, S.sm_r)
    return_wait(out_d, S.dm_s, S.dm_r)
    dmd_own.wait()
    rings_sent()
    drain()
    for m in range(3):
        x_first(m, 0).wait_send()

    @pl.when(l == 0)
    def _():
        scale_copy().wait_send()
        own_row(1, 0, dev(h, c, y, z, 1)).wait_send()

    @pl.when(l == 1)
    def _():
        for m in range(3):
            x_second(m).wait_send()
        own_row(0, 1, dev(oh, c, y, z, 0)).wait_send()
        own_row(1, 1, dev(oh, c, y, z, 1)).wait_send()


def copy_results(*refs):
    ins, outs, held, come, gone = refs[:3], refs[3:6], refs[6:9], refs[9], refs[10]
    first, second = [], []
    for source, buffer, target in zip(ins, held, outs):
        rows = min(source.shape[0], ROWS // 4)
        rows = rows if source.shape[0] % rows == 0 else source.shape[0]
        for i in range(source.shape[0] // rows):
            at = pl.ds(i * rows, rows)
            n = len(first)
            first.append(pltpu.make_async_copy(source.at[at], buffer.at[at], come.at[n]))
            second.append(pltpu.make_async_copy(buffer.at[at], target.at[at], gone.at[n]))
    for copy in first:
        copy.start()
    for copy, after in zip(first, second):
        copy.wait()
        after.start()
    for after in second:
        after.wait()


def on_device(gi, noise, dmd_step, scale_group, wg, wt, wc, scales, mod, tproj):
    vmem = pl.BlockSpec(memory_space=pltpu.VMEM)
    smem = pl.BlockSpec(memory_space=pltpu.SMEM)
    hbm = pl.BlockSpec(memory_space=pl.ANY)
    out_shape = (
        jax.ShapeDtypeStruct((ROWS, D), BF16),
        jax.ShapeDtypeStruct((ROWS, D), BF16),
        jax.ShapeDtypeStruct((HALF, COLS), F32),
    )
    results = pl.pallas_call(
        kernel,
        out_shape=out_shape,
        in_specs=[hbm, hbm, smem, vmem, vmem, vmem, vmem, hbm, vmem, hbm],
        out_specs=(hbm, hbm, vmem),
        scratch_shapes=list(scratch_table().values()),
        compiler_params=pltpu.CompilerParams(
            collective_id=0, has_side_effects=True, vmem_limit_bytes=64 * 1024 * 1024 - 65536
        ),
    )(gi, noise, dmd_step, scale_group.T, wg, wt, wc, scales, mod, tproj)
    return pl.pallas_call(
        copy_results,
        out_shape=out_shape,
        in_specs=[hbm] * 3,
        out_specs=(hbm,) * 3,
        scratch_shapes=[pltpu.VMEM(s.shape, s.dtype) for s in out_shape] + [pltpu.SemaphoreType.DMA((9,))] * 2,
    )(*results)


def solution(mesh):
    return jax.shard_map(
        on_device,
        mesh=mesh,
        in_specs=(
            P(("dp", "fsdp"), None),
            P(("dp", "fsdp"), None),
            P(),
            P(),
            P("fsdp", "dp"),
            P("fsdp", "dp"),
            P("fsdp", "dp"),
            P(None, None, "dp"),
            P(),
            P(),
        ),
        out_specs=(P(("dp", "fsdp"), None), P(("dp", "fsdp"), None), P("fsdp", "dp")),
        check_vma=False,
    )
```
